32 devices in a mesh: blk: 4 (over y, x), grp: 8 (over z, core).
Axes of the slice: x: 2, y: 2, z: 4, core: 2. Of those that a mesh axis runs over, the one named last changes fastest.
Arguments:
- tokens: bfloat16 [16, 512, 1024], P('grp', 'blk'), may hold values from -6 to 6
- gain_one: bfloat16 [1024], replicated, may hold values from 0.5 to 1.5
- bias_one: bfloat16 [1024], replicated, may hold values from -1.75 to 1.75
- w_qkv: bfloat16 [1024, 3072], replicated, may hold values from -0.1875 to 0.1875
- w_out: bfloat16 [1024, 1024], replicated, may hold values from -3 to 3
- gain_two: bfloat16 [1024], replicated, may hold values from 0.5 to 1.5
- bias_two: bfloat16 [1024], replicated, may hold values from -1.75 to 1.75
- w_in: bfloat16 [1024, 4096], replicated, may hold values from -0.1875 to 0.1875
- w_down: bfloat16 [4096, 1024], replicated, may hold values from -0.09375 to 0.09375
- mem_keys: bfloat16 [16, 512, 1024], P('grp', 'blk'), may hold values from -6 to 6
- mem_values: bfloat16 [16, 512, 1024], P('grp', 'blk'), may hold values from -6 to 6
- continues: int32 [16], replicated, may hold values from 0 to 15, each once
- block_place: int32 [4], replicated, may hold values from 0 to 3, each once
- cotangent: bfloat16 [16, 512, 1024], P('grp', 'blk'), may hold values from -6 to 6
Outputs:
- mixed: bfloat16 [16, 512, 1024], P('grp', 'blk')
- grad_tokens: float32 [16, 512, 1024], P('grp', 'blk')
- grad_gain_one: float32 [1024], P('blk')
- grad_bias_one: float32 [1024], P('blk')
- grad_qkv: float32 [1024, 3072], P('blk')
- grad_out: float32 [1024, 1024], P('blk')
- grad_gain_two: float32 [1024], P('blk')
- grad_bias_two: float32 [1024], P('blk')
- grad_in: float32 [1024, 4096], P('blk')
- grad_down: float32 [4096, 1024], P('blk')
The draws below stay inside these ranges and needn't reach their ends.
Inputs may be any that keep to these rules, and one draw needn't show every extreme that they name: Segment s reads cached bank continues[s]; every bank is read by exactly one segment. Blk index b holds positions block_place[b] * 128 to block_place[b] * 128 + 127 of each of its segments; every block is held once.
All inputs are finite; a program needn't handle non-finite values.
Results may differ from the reference program's by a relative error of at most 0.025.
Values may be sent and summed in bfloat16 or wider, within the bound.
No kernel may reach another device: no remote copies, remote signals or barrier semaphores. Data moves between devices by JAX's collectives and lax.ppermute only.
A program may use at most 256 MiB of HBM per device.

```python
import math
from functools import partial
import jax
import jax.numpy as jnp
from jax import lax

D = 1024
HEADS = 16
FF = 4096
TOK_DEV = 128
BLOCKS = 4
SEG_LEN = 512
SEGMENTS = 16
MEM = 512
N_BLK = 4


def levels(rng, dims, pieces, least, largest):
    def one(dim, blocks):
        steps = jax.random.uniform(jax.random.fold_in(jax.random.fold_in(rng, 6), dim), (blocks,), jnp.float32, least / len(pieces), largest / len(pieces))
        return jnp.repeat(jnp.exp(steps), dims[dim] // blocks).reshape((-1,) + (1,) * (len(dims) - dim - 1))

    loudness = one(*pieces[0])
    for cut in pieces[1:]:
        loudness = loudness * one(*cut)
    return loudness


def noise(own_key, dims, deviation, reach, cuts=(), kind=jnp.bfloat16):
    values = jax.random.normal(own_key, dims, jnp.float32) * deviation
    if len(cuts) > 0:
        values = levels(own_key, dims, cuts, -0.22, 0.18) * values
    return jnp.clip(values, min=-reach, max=reach).astype(kind)


def setup_inputs(seed: int = 0) -> dict:
    arg_keys = jax.random.split(jax.random.key(seed), 15)
    tokens = noise(arg_keys[0], (SEGMENTS, SEG_LEN, D), 1.0, 6.0, ((0, 8), (1, 4)))
    gain_one = jnp.clip(1.0 + 0.1 * jax.random.normal(arg_keys[1], (D,), jnp.float32), 0.5, 1.5).astype(jnp.bfloat16)
    bias_one = noise(arg_keys[2], (D,), 0.3, 1.75)
    w_qkv = noise(arg_keys[3], (D, 3 * D), D ** -0.5, 0.1875)
    w_out = noise(arg_keys[4], (D, D), (max(D // 256, 1)) ** -0.5, 3.0)
    gain_two = jnp.clip(1.0 + 0.1 * jax.random.normal(arg_keys[5], (D,), jnp.float32), 0.5, 1.5).astype(jnp.bfloat16)
    bias_two = noise(arg_keys[6], (D,), 0.3, 1.75)
    w_in = noise(arg_keys[7], (D, FF), D ** -0.5, 0.1875)
    w_down = noise(arg_keys[8], (FF, D), FF ** -0.5, 0.09375)
    mem_keys = noise(arg_keys[9], (SEGMENTS, MEM, D), 1.0, 6.0, ((0, 8), (1, 4)))
    mem_values = noise(arg_keys[10], (SEGMENTS, MEM, D), 1.0, 6.0, ((0, 8), (1, 4)))
    continues = jax.random.permutation(arg_keys[11], SEGMENTS).astype(jnp.int32)
    block_place = jax.random.permutation(arg_keys[12], BLOCKS).astype(jnp.int32)
    cotangent = noise(arg_keys[13], (SEGMENTS, SEG_LEN, D), 1.0, 6.0, ((0, 8), (1, 4)))
    return dict(tokens=tokens, gain_one=gain_one, bias_one=bias_one, w_qkv=w_qkv, w_out=w_out, gain_two=gain_two, bias_two=bias_two, w_in=w_in, w_down=w_down, mem_keys=mem_keys, mem_values=mem_values, continues=continues, block_place=block_place, cotangent=cotangent)


@jax.custom_vjp
def low(v):
    return lax.optimization_barrier(v.astype(jnp.bfloat16)).astype(jnp.float32)

@jax.custom_vjp
def low_back(v):
    return v

def low_keep(v):
    return (low(v), None)

def low_pass(kept, grad):
    return (grad,)

def back_keep(v):
    return (v, None)

def back_low(kept, grad):
    return (low(grad),)
low.defvjp(low_keep, low_pass)
low_back.defvjp(back_keep, back_low)
highest = lax.Precision.HIGHEST

def both_round(values):
    return low_back(low(values))

def layer_norm(values, gain, bias):
    average = lax.optimization_barrier(jnp.mean(values, -1, keepdims=True))
    centred = values - average
    spread = lax.optimization_barrier(jnp.mean(centred * centred, -1, keepdims=True))
    return centred * lax.rsqrt(spread + 1e-05) * gain + bias

def attend_block(inputs, keys_all, values_all, key_positions):
    queries, own_keys, query_positions = inputs
    score_scale = queries.shape[-1] ** (-0.5)
    scores = low_back(jnp.einsum('qhd,khd->hqk', queries, keys_all, precision=highest) * score_scale)
    self_score = jnp.transpose(lax.optimization_barrier(jnp.sum(queries * own_keys, -1))) * score_scale
    allowed = key_positions[None, None, :] <= query_positions[None, :, None]
    weights = jnp.exp(jnp.where(allowed, scores - self_score[:, :, None], -1e+30))
    totals = lax.optimization_barrier(jnp.sum(weights, -1))
    summed = low_back(jnp.einsum('hqk,khd->qhd', low(weights), values_all, precision=highest))
    return summed / jnp.transpose(totals)[:, :, None]

def layer_forward(hidden, params, memory_keys, memory_values, positions):
    gain_one, bias_one, w_qkv, w_out, gain_two, bias_two, w_in, w_down = params
    seg_rows, model_width = hidden.shape
    head_dim = model_width // HEADS
    normed_one = low(layer_norm(hidden, gain_one, bias_one))
    projected = jnp.dot(normed_one, w_qkv, precision=highest)
    queries = both_round(projected[:, :model_width])
    key_rows = both_round(projected[:, model_width:2 * model_width])
    value_rows = both_round(projected[:, 2 * model_width:])
    keys_all = jnp.concatenate([key_rows, memory_keys], 0).reshape(-1, HEADS, head_dim)
    values_all = jnp.concatenate([value_rows, memory_values], 0).reshape(-1, HEADS, head_dim)
    key_positions = jnp.concatenate([positions, jnp.full((memory_keys.shape[0],), -1, jnp.int32)])
    block_rows = math.gcd(seg_rows, 512)
    block_count = seg_rows // block_rows
    attend = jax.checkpoint(partial(attend_block, keys_all=keys_all, values_all=values_all, key_positions=key_positions))
    attended = lax.map(attend, (queries.reshape(block_count, block_rows, HEADS, head_dim), key_rows.reshape(block_count, block_rows, HEADS, head_dim), positions.reshape(block_count, block_rows)))
    attended = both_round(attended.reshape(seg_rows, model_width))
    branch = low_back(jnp.dot(attended, w_out, precision=highest))
    residual = hidden + branch
    normed_two = low(layer_norm(residual, gain_two, bias_two))
    inner_pre = low_back(jnp.dot(normed_two, w_in, precision=highest))
    activated = low(jax.nn.gelu(inner_pre))
    return residual + jnp.dot(activated, w_down, precision=highest)

def reference(tokens, gain_one, bias_one, w_qkv, w_out, gain_two, bias_two, w_in, w_down, mem_keys, mem_values, continues, block_place, cotangent):
    seg_rows = TOK_DEV * N_BLK
    row_index = jnp.arange(seg_rows, dtype=jnp.int32)
    positions = (block_place[row_index // TOK_DEV] * TOK_DEV + row_index % TOK_DEV).astype(jnp.int32)
    params = tuple((item.astype(jnp.float32) for item in (gain_one, bias_one, w_qkv, w_out, gain_two, bias_two, w_in, w_down)))

    def segment_step(carried, inputs):
        segment_tokens, segment_cot, bank = inputs
        memory_keys = mem_keys[bank].astype(jnp.float32)
        memory_values = mem_values[bank].astype(jnp.float32)

        def forward(hidden, weights):
            return layer_forward(hidden, weights, memory_keys, memory_values, positions)
        output, pullback = jax.vjp(forward, segment_tokens.astype(jnp.float32), params)
        grad_hidden, grad_params = pullback(segment_cot.astype(jnp.float32))
        updated = tuple((left + right for left, right in zip(carried, grad_params)))
        return (updated, (output.astype(jnp.bfloat16), grad_hidden))
    zeros_init = tuple((jnp.zeros(item.shape, jnp.float32) for item in params))
    sums, outputs = lax.scan(segment_step, zeros_init, (tokens, cotangent, continues))
    mixed, grad_tokens = outputs
    return (mixed, grad_tokens, sums[0], sums[1], sums[2], sums[3], sums[4], sums[5], sums[6], sums[7])
```

```python
import jax
import jax.numpy as jnp
from jax import lax
from jax.sharding import PartitionSpec as P

HEADS = 16
F32 = jnp.float32
BF16 = jnp.bfloat16


def layer_norm(values, gain, bias):
    average = jnp.mean(values, -1, keepdims=True)
    centred = values - average
    spread = jnp.mean(centred * centred, -1, keepdims=True)
    return centred * lax.rsqrt(spread + 1e-05) * gain + bias


def norm_back(values, gain, grad):
    average = jnp.mean(values, -1, keepdims=True)
    centred = values - average
    spread = jnp.mean(centred * centred, -1, keepdims=True)
    scale = lax.rsqrt(spread + 1e-05)
    unit = centred * scale
    scaled = grad * gain
    mean_one = jnp.mean(scaled, -1, keepdims=True)
    mean_two = jnp.mean(scaled * unit, -1, keepdims=True)
    return (
        scale * (scaled - mean_one - unit * mean_two),
        jnp.sum(grad * unit, 0),
        jnp.sum(grad, 0),
    )


def swap(values, axis, mask):
    size = lax.axis_size(axis)
    return lax.ppermute(values, axis, [(i, i ^ mask) for i in range(size)])


def pick(values, index, dim=0):
    return lax.dynamic_index_in_dim(values, index, dim, keepdims=False)


def dot(left, right, dims):
    return lax.dot_general(left, right, ((dims[0], dims[1]), ((), ())), preferred_element_type=F32)


def fetch_banks(mem_keys, mem_values, continues, groups, my_group, blocks, my_block):
    seq_count, rows, width = mem_keys.shape
    core, chips = my_group % 2, groups // 2
    my_chip = my_group // 2
    kept = jnp.where(core == 0, mem_keys, mem_values)
    sent = jnp.where(core == 0, mem_values, mem_keys)
    came = swap(sent, "grp", 1)
    pair = jnp.where(core == 0, jnp.stack([kept, came]), jnp.stack([came, kept]))
    per_chip = 2 * seq_count
    pair = pair.reshape(per_chip, chips, rows // chips, width)
    parts = [pick(pair, my_chip, 1)]
    for mask in range(1, chips):
        parts.append(swap(pick(pair, my_chip ^ mask, 1), "grp", 2 * mask))
    order = my_chip ^ jnp.arange(chips)
    every = jnp.take(jnp.stack(parts), order, axis=0).reshape(
        chips * per_chip, rows // chips, width
    )
    def needed(chip):
        banks = lax.dynamic_slice_in_dim(continues, chip * per_chip, per_chip)
        return jnp.take(every, banks, axis=0)

    parts = [needed(my_chip)]
    for mask in range(1, chips):
        parts.append(swap(needed(my_chip ^ mask), "grp", 2 * mask))
    held = jnp.stack(parts, 1).reshape(2, seq_count, rows, width)
    kept = pick(held, core)
    came = swap(pick(held, 1 - core), "grp", 1)
    keys = jnp.where(core == 0, kept, came)
    values = jnp.where(core == 0, came, kept)
    both = jnp.stack([keys, values]).reshape(2, seq_count, rows, blocks, width // blocks)
    parts = [pick(both, my_block, 3)]
    for mask in range(1, blocks):
        parts.append(swap(pick(both, my_block ^ mask, 3), "blk", mask))
    whole = jnp.stack(parts, 2).reshape(2, seq_count, blocks * rows, width // blocks)
    return whole[0], whole[1]


def reduce_blocks(values, blocks, my_block):
    bits = blocks.bit_length() - 1
    half = values.shape[1] // 2
    results = []
    for part in range(2):
        held = values[:, :half] if part == 0 else values[:, half:]
        order = range(bits) if part == 0 else reversed(range(bits))
        left = list(range(bits))
        held = held.reshape((2,) * bits + held.shape[1:])
        for bit in order:
            dim = left.index(bit)
            axis = len(left) - 1 - dim
            mine = (my_block >> bit) & 1
            sent = pick(held, 1 - mine, axis)
            came = swap(sent, "blk", 1 << bit)
            held = (pick(held, mine, axis).astype(F32) + came.astype(F32)).astype(BF16)
            left.remove(bit)
        results.append(held)
    return results


def reduce_groups(values, groups, my_group):
    bits = groups.bit_length() - 1
    rows = values.shape[0]
    low = (my_group >> 1) & 1
    halves = values.reshape((2, rows // 2) + values.shape[1:])
    came = swap(pick(halves, 1 - low), "grp", 2)
    held = (pick(halves, low).astype(F32) + came.astype(F32)).astype(BF16)
    for bit in range(2, bits):
        came = swap(held, "grp", 1 << bit)
        held = (held.astype(F32) + came.astype(F32)).astype(BF16)
    came = swap(held, "grp", 2)
    return jnp.where(low == 0, jnp.stack([held, came]), jnp.stack([came, held])).reshape(
        values.shape
    )


def join_cores(values, core):
    came = swap(values, "grp", 1)
    return jnp.where(core == 0, jnp.stack([values, came]), jnp.stack([came, values]))


def on_device(
    tokens,
    gain_one,
    bias_one,
    w_qkv,
    w_out,
    gain_two,
    bias_two,
    w_in,
    w_down,
    mem_keys,
    mem_values,
    continues,
    block_place,
    cotangent,
):
    seq_count, tok_rows, width = tokens.shape
    hidden_width = w_in.shape[1]
    blocks, groups = lax.axis_size("blk"), lax.axis_size("grp")
    my_block, my_group = lax.axis_index("blk"), lax.axis_index("grp")
    core = my_group % 2
    heads = HEADS // blocks
    part = width // blocks
    head_dim = width // HEADS
    score_scale = head_dim ** (-0.5)
    rows = seq_count * tok_rows
    seg_rows = blocks * tok_rows
    gain_one_f, bias_one_f = gain_one.astype(F32), bias_one.astype(F32)
    gain_two_f, bias_two_f = gain_two.astype(F32), bias_two.astype(F32)
    hidden = tokens.reshape(rows, width).astype(F32)

    pieces = [tokens] + [swap(tokens, "blk", mask) for mask in range(1, blocks)]
    places = [block_place[my_block ^ mask] for mask in range(blocks)]
    mem_k, mem_v = fetch_banks(
        mem_keys, mem_values, continues, groups, my_group, blocks, my_block
    )

    def to_positions(parts):
        masks = jnp.stack(places)
        order = jnp.argsort(masks)
        stacked = jnp.take(jnp.stack(parts, 1), order, axis=1)
        return stacked.reshape((seq_count, seg_rows) + parts[0].shape[2:])

    def from_positions(values, mask):
        return pick(
            values.reshape((seq_count, blocks, tok_rows) + values.shape[2:]), places[mask], 1
        )

    def from_heads(values, dim):
        parts = [from_positions(values, 0)]
        for mask in range(1, blocks):
            parts.append(swap(from_positions(values, mask), "blk", mask))
        order = my_block ^ jnp.arange(blocks)
        stacked = jnp.take(jnp.stack(parts, 0), order, axis=0)
        return jnp.moveaxis(stacked, 0, -2)

    all_rows = to_positions(pieces)
    normed_all = (
        layer_norm(all_rows.astype(F32), gain_one_f, bias_one_f)
        .astype(BF16)
        .reshape(seq_count * seg_rows, width)
    )
    w_heads = pick(w_qkv.reshape(width, 3, blocks, part), my_block, 2).reshape(width, 3 * part)
    projected = dot(normed_all, w_heads, ((1,), (0,))).astype(BF16)
    projected = projected.reshape(seq_count, seg_rows, 3, heads, head_dim)
    queries, keys, values = projected[:, :, 0], projected[:, :, 1], projected[:, :, 2]
    mem_k = mem_k.reshape(seq_count, -1, heads, head_dim)
    mem_v = mem_v.reshape(seq_count, -1, heads, head_dim)
    self_score = (
        jnp.transpose(jnp.sum(queries.astype(F32) * keys.astype(F32), -1), (0, 2, 1)) * score_scale
    )
    causal = jnp.arange(seg_rows)[None, :] <= jnp.arange(seg_rows)[:, None]

    def weights_of(some_keys, masked):
        scores = (
            jnp.einsum("sqhd,skhd->shqk", queries, some_keys, preferred_element_type=F32)
            * score_scale
        )
        scores = scores - self_score[:, :, :, None]
        if masked:
            scores = jnp.where(causal[None, None], scores, -1e30)
        return jnp.exp(scores)

    own_w = weights_of(keys, True)
    mem_w = weights_of(mem_k, False)
    totals = jnp.sum(own_w, -1) + jnp.sum(mem_w, -1)
    summed = jnp.einsum(
        "shqk,skhd->sqhd", own_w.astype(BF16), values, preferred_element_type=F32
    ) + jnp.einsum("shqk,skhd->sqhd", mem_w.astype(BF16), mem_v, preferred_element_type=F32)
    totals_rows = jnp.transpose(totals, (0, 2, 1))[:, :, :, None]
    attended_f = summed / totals_rows
    attended_heads = attended_f.astype(BF16).reshape(seq_count, seg_rows, part)
    attended = from_heads(attended_heads, 0).reshape(rows, width)

    residual = hidden + dot(attended, w_out, ((1,), (0,)))
    normed_two = layer_norm(residual, gain_two_f, bias_two_f).astype(BF16)
    inner = dot(normed_two, w_in, ((1,), (0,)))
    activated, gelu_pull = jax.vjp(jax.nn.gelu, inner)
    activated = activated.astype(BF16)
    mixed = (residual + dot(activated, w_down, ((1,), (0,)))).astype(BF16)
    cot = cotangent.reshape(rows, width)
    grad_act = dot(cot, w_down, ((1,), (1,)))
    grad_inner = gelu_pull(grad_act)[0].astype(BF16)
    grad_normed_two = dot(grad_inner, w_in, ((1,), (1,)))
    grad_res, grad_gain_two, grad_bias_two = norm_back(residual, gain_two_f, grad_normed_two)
    grad_residual = cot.astype(F32) + grad_res
    grad_branch = grad_residual.astype(BF16)
    grad_attended = dot(grad_branch, w_out, ((1,), (1,))).astype(BF16)
    by_block = grad_attended.reshape(seq_count, tok_rows, blocks, part)
    pieces = [pick(by_block, my_block, 2)]
    for mask in range(1, blocks):
        pieces.append(swap(pick(by_block, my_block ^ mask, 2), "blk", mask))
    grad_att = to_positions(pieces).reshape(seq_count, seg_rows, heads, head_dim).astype(F32)

    scaled = (grad_att / totals_rows).astype(BF16)
    correction = jnp.transpose(
        jnp.sum(grad_att * attended_f, -1) / totals_rows[:, :, :, 0], (0, 2, 1)
    )

    def score_grads(weights, some_values):
        grad_w = jnp.einsum("sqhd,skhd->shqk", scaled, some_values, preferred_element_type=F32)
        return weights * (grad_w - correction[:, :, :, None])

    own_g = score_grads(own_w, values)
    mem_g = score_grads(mem_w, mem_v)
    diag = jnp.sum(own_g, -1) + jnp.sum(mem_g, -1)
    diag = jnp.transpose(diag, (0, 2, 1))[:, :, :, None]
    own_b, mem_b = own_g.astype(BF16), mem_g.astype(BF16)
    grad_q = score_scale * (
        jnp.einsum("shqk,skhd->sqhd", own_b, keys, preferred_element_type=F32)
        + jnp.einsum("shqk,skhd->sqhd", mem_b, mem_k, preferred_element_type=F32)
        - diag * keys.astype(F32)
    )
    grad_k = score_scale * (
        jnp.einsum("shqk,sqhd->skhd", own_b, queries, preferred_element_type=F32)
        - diag * queries.astype(F32)
    )
    grad_v = jnp.einsum("shqk,sqhd->skhd", own_w.astype(BF16), scaled, preferred_element_type=F32)
    grad_heads = (
        jnp.stack([grad_q, grad_k, grad_v], 2)
        .astype(BF16)
        .reshape(seq_count, seg_rows, 3, part)
    )
    grad_proj = from_heads(grad_heads, 0).reshape(rows, 3 * width)
    grad_normed_one = dot(grad_proj, w_qkv, ((1,), (1,)))
    grad_hid, grad_gain_one, grad_bias_one = norm_back(hidden, gain_one_f, grad_normed_one)
    grad_tokens = (grad_residual + grad_hid).reshape(seq_count, tok_rows, width)

    def both_rows(values):
        return jnp.concatenate([values, swap(values, "grp", 1)], 0)

    def column_half(values, count, whose):
        return pick(values.reshape(values.shape[0], count, 2, -1), whose, 2).reshape(
            values.shape[0], -1
        )

    def halves_of(values, count):
        return jnp.concatenate(
            [
                column_half(values, count, core),
                swap(column_half(values, count, 1 - core), "grp", 1),
            ],
            0,
        )

    cot_two = both_rows(cot)
    act_half = halves_of(activated, blocks)
    down = dot(act_half, cot_two, ((0,), (0,))).astype(BF16).reshape(blocks, -1, width)
    normed_half = halves_of(normed_two, blocks)
    inner_two = both_rows(grad_inner)
    into = dot(normed_half, inner_two, ((0,), (0,))).astype(BF16).reshape(blocks, -1, hidden_width)
    branch_two = both_rows(grad_branch)
    attended_half = halves_of(attended, blocks)
    out = dot(attended_half, branch_two, ((0,), (0,))).astype(BF16).reshape(blocks, -1, width)

    def finish(values, shape):
        pieces = reduce_blocks(values, blocks, my_block)
        joined = reduce_groups(jnp.concatenate(pieces, 0), groups, my_group)
        return join_cores(joined, core).reshape(shape).astype(F32)

    grad_down = finish(down, (hidden_width // blocks, width))
    grad_in = finish(into, (part, hidden_width))
    grad_out = finish(out, (part, width))
    heads_rows = grad_heads.reshape(seq_count * seg_rows, 3 * part)
    qkv = dot(normed_all, heads_rows, ((0,), (0,))).astype(BF16)
    qkv = qkv.reshape(blocks, 2, part // 2, 3 * part)
    came = swap(pick(qkv, 1 - core, 1), "grp", 1)
    qkv = (pick(qkv, core, 1).astype(F32) + came.astype(F32)).astype(BF16)
    pieces = [pick(qkv, my_block)]
    for mask in range(1, blocks):
        pieces.append(swap(pick(qkv, my_block ^ mask), "blk", mask))
    order = my_block ^ jnp.arange(blocks)
    qkv = jnp.take(jnp.stack(pieces), order, axis=0).reshape(blocks, part // 2, 3, part)
    qkv = jnp.transpose(qkv, (1, 2, 0, 3)).reshape(part // 2, 3 * width)
    qkv = reduce_groups(qkv, groups, my_group)
    grad_qkv = join_cores(qkv, core).reshape(part, 3 * width).astype(F32)

    vectors = jnp.stack([grad_gain_one, grad_bias_one, grad_gain_two, grad_bias_two])
    for bit in range(groups.bit_length() - 1):
        vectors = vectors + swap(vectors, "grp", 1 << bit)
    for bit in range(blocks.bit_length() - 1):
        vectors = vectors + swap(vectors, "blk", 1 << bit)
    vectors = pick(vectors.reshape(4, blocks, part), my_block, 1)
    return (
        mixed.reshape(tokens.shape),
        grad_tokens,
        vectors[0],
        vectors[1],
        grad_qkv,
        grad_out,
        vectors[2],
        vectors[3],
        grad_in,
        grad_down,
    )


def solution(mesh):
    rows = P("grp", "blk", None)
    in_specs = (rows,) + (P(),) * 8 + (rows, rows, P(), P(), rows)
    out_specs = (rows, rows) + (P("blk"),) * 2 + (P("blk", None),) * 2
    out_specs = out_specs + (P("blk"),) * 2 + (P("blk", None),) * 2
    return jax.shard_map(
        on_device, mesh=mesh, in_specs=in_specs, out_specs=out_specs, check_vma=False
    )
```

```python
import functools

import jax
import jax.numpy as jnp
from jax import lax
from jax.experimental import pallas as pl
from jax.experimental.pallas import tpu as pltpu
from jax.sharding import PartitionSpec as P

HEADS = 16
F32 = jnp.float32
BF16 = jnp.bfloat16
MIB = 1 << 20
EPS = 1e-05
FAR = -1e30
GELU_A = 0.7978845608028654
GELU_B = 0.044715


def swap(values, axis, mask):
    size = lax.axis_size(axis)
    return lax.ppermute(values, axis, [(i, i ^ mask) for i in range(size)])


def pick(values, index, dim=0):
    return lax.dynamic_index_in_dim(values, index, dim, keepdims=False)


def nn(left, right):
    return lax.dot_general(left, right, (((1,), (0,)), ((), ())), preferred_element_type=F32)


def nt(left, right):
    return lax.dot_general(left, right, (((1,), (1,)), ((), ())), preferred_element_type=F32)


def tn(left, right):
    return lax.dot_general(left, right, (((0,), (0,)), ((), ())), preferred_element_type=F32)


def params(mib):
    return pltpu.CompilerParams(vmem_limit_bytes=mib * MIB)


def call(kernel, name, grid, ins, outs, scratch, scalars, mib, cost):
    def whole(shape):
        return pl.BlockSpec(shape, lambda *_: (0,) * len(shape))

    in_specs, arrays = [], []
    for item in ins:
        if isinstance(item, tuple):
            arrays.append(item[0])
            in_specs.append(pl.BlockSpec(item[1], item[2]))
        else:
            arrays.append(item)
            in_specs.append(whole(item.shape))
    out_shapes, out_specs = [], []
    for item in outs:
        out_shapes.append(jax.ShapeDtypeStruct(item[0], item[1]))
        out_specs.append(whole(item[0]) if len(item) == 2 else pl.BlockSpec(item[2], item[3]))
    spec = pltpu.PrefetchScalarGridSpec(
        num_scalar_prefetch=1,
        grid=grid,
        in_specs=in_specs,
        out_specs=out_specs,
        scratch_shapes=scratch,
    )
    return pl.pallas_call(
        kernel,
        grid_spec=spec,
        out_shape=out_shapes,
        compiler_params=params(mib),
        cost_estimate=pl.CostEstimate(flops=cost[0], bytes_accessed=cost[1], transcendentals=0),
        name=name,
    )(scalars, *arrays)


def norm_stats(values):
    average = jnp.mean(values, -1, keepdims=True)
    centred = values - average
    scale = lax.rsqrt(jnp.mean(centred * centred, -1, keepdims=True) + EPS)
    return centred * scale, scale


def norm_back(unit, scale, gain, grad):
    scaled = grad * gain
    mean_one = jnp.mean(scaled, -1, keepdims=True)
    mean_two = jnp.mean(scaled * unit, -1, keepdims=True)
    return scale * (scaled - mean_one - unit * mean_two)


def project_kernel(sc, rows, gain, bias, wq, wk, wv, normed, qkv):
    part = wq.shape[1]
    unit, _ = norm_stats(rows[...].astype(F32))
    low = (unit * gain[...].astype(F32) + bias[...].astype(F32)).astype(BF16)
    normed[...] = low
    for i, weight in enumerate((wq, wk, wv)):
        qkv[:, i * part : (i + 1) * part] = nn(low, weight[...]).astype(BF16)


def lane_masks():
    lane = lax.broadcasted_iota(jnp.int32, (1, 128), 1)
    return [lane < 64, lane >= 64]


def of_head(values, mask):
    return jnp.where(mask, values, jnp.zeros_like(values))


def by_head(first, second, masks):
    return jnp.where(masks[0], first, second)


BLOCK = 256


def own_kernel(blocks, sc, *refs):
    ins, outs = refs[: 3 * blocks], refs[3 * blocks :]
    q_out, k_out, v_out, t_out, l_out = outs[:5]
    held = outs[5]
    tok = ins[0].shape[1]
    scale = 64 ** (-0.5)
    for mask in range(blocks):
        place = sc[2 + mask]
        for i in range(3):
            values = ins[3 * mask + i][0]
            if i == 0:
                values = (values.astype(F32) * scale).astype(BF16)
            held[i, place] = values
    rows = blocks * tok
    queries = held[0].reshape(rows, 128)
    keys = held[1].reshape(rows, 128)
    values = held[2].reshape(rows, 128)
    q_out[0], k_out[0], v_out[0] = queries, keys, values
    masks = lane_masks()
    size = min(BLOCK, rows)
    lower = lax.broadcasted_iota(jnp.int32, (size, size), 0) >= lax.broadcasted_iota(
        jnp.int32, (size, size), 1
    )
    product = queries.astype(F32) * keys.astype(F32)
    head_keys = [of_head(keys, m) for m in masks]
    head_values = [of_head(values, m) for m in masks]
    selfs = [jnp.sum(of_head(product, m), -1, keepdims=True) for m in masks]
    for i in range(rows // size):
        here = slice(i * size, (i + 1) * size)
        total, sums = jnp.zeros((size, 128), F32), []
        for h in range(2):
            count = jnp.zeros((size, 1), F32)
            for j in range(i + 1):
                there = slice(j * size, (j + 1) * size)
                scores = nt(queries[here], head_keys[h][there]) - selfs[h][here]
                if i == j:
                    scores = jnp.where(lower, scores, FAR)
                weights = jnp.exp(scores)
                count = count + jnp.sum(weights, -1, keepdims=True)
                total = total + nn(weights.astype(BF16), head_values[h][there])
            sums.append(count)
        t_out[0, here] = total
        l_out[0, here] = by_head(sums[0], sums[1], masks)


def load_cached(pieces, mem):
    tok = pieces[0].shape[2]
    for mask, piece in enumerate(pieces):
        mem[:, mask * tok : (mask + 1) * tok] = piece[:, 0]


def cached_kernel(blocks, sc, *refs):
    q_in, k_in, t_in, l_in = refs[:4]
    pieces = refs[4 : 4 + blocks]
    att_out, l_out = refs[4 + blocks : 6 + blocks]
    sends = refs[6 + blocks : 6 + 2 * blocks]
    mem, low = refs[6 + 2 * blocks :]
    load_cached(pieces, mem)
    tok = pieces[0].shape[2]
    queries, keys = q_in[0], k_in[0]
    rows = queries.shape[0]
    masks = lane_masks()
    product = queries.astype(F32) * keys.astype(F32)
    selfs = [jnp.sum(of_head(product, m), -1, keepdims=True) for m in masks]
    head_keys = [of_head(mem[0], m) for m in masks]
    head_values = [of_head(mem[1], m) for m in masks]
    size = min(BLOCK, rows)
    for i in range(rows // size):
        here = slice(i * size, (i + 1) * size)
        total, sums = t_in[0, here], []
        for h in range(2):
            weights = jnp.exp(nt(queries[here], head_keys[h]) - selfs[h][here])
            sums.append(jnp.sum(weights, -1, keepdims=True))
            total = total + nn(weights.astype(BF16), head_values[h])
        count = l_in[0, here] + by_head(sums[0], sums[1], masks)
        attended = total / count
        att_out[0, here] = attended
        l_out[0, here] = count
        low[i * size // tok : (i + 1) * size // tok] = attended.astype(BF16).reshape(
            size // tok, tok, 128
        )
    for mask in range(blocks):
        sends[mask][0] = low[sc[2 + mask]]


def attention_back_kernel(blocks, halved, sc, *refs):
    q_in, k_in, v_in, att_in, l_in = refs[:5]
    pieces = refs[5 : 5 + blocks]
    grads = refs[5 + blocks : 5 + 2 * blocks]
    sends = refs[5 + 2 * blocks : 5 + 3 * blocks]
    rest = refs[5 + 3 * blocks :]
    if halved:
        to_core, rest = rest[0], rest[1:]
    mem, came, low = rest
    load_cached(pieces, mem)
    tok = pieces[0].shape[2]
    for mask in range(blocks):
        came[sc[2 + mask]] = grads[mask][0]
    queries, keys, values = q_in[0], k_in[0], v_in[0]
    rows = queries.shape[0]
    scale = 64 ** (-0.5)
    masks = lane_masks()
    grad = came[...].reshape(rows, 128).astype(F32)
    count = l_in[0]
    scaled_f = grad / count
    scaled = scaled_f.astype(BF16)
    weighed = grad * att_in[0] / count
    product = queries.astype(F32) * keys.astype(F32)
    selfs = [jnp.sum(of_head(product, m), -1, keepdims=True) for m in masks]
    fixes = [jnp.sum(of_head(weighed, m), -1, keepdims=True) for m in masks]
    own_k = [of_head(keys, m) for m in masks]
    own_v = [of_head(values, m) for m in masks]
    mem_k = [of_head(mem[0], m) for m in masks]
    mem_v = [of_head(mem[1], m) for m in masks]
    q_t = [of_head(queries, m).astype(F32).T.astype(BF16) for m in masks]
    s_t = [of_head(scaled, m).astype(F32).T.astype(BF16) for m in masks]
    size = min(BLOCK, rows)
    lower = lax.broadcasted_iota(jnp.int32, (size, size), 0) >= lax.broadcasted_iota(
        jnp.int32, (size, size), 1
    )
    steps = rows // size
    keys_t = [jnp.zeros((128, size), F32) for _ in range(steps)]
    values_t = [jnp.zeros((128, size), F32) for _ in range(steps)]
    diags = []
    for i in range(steps):
        here = slice(i * size, (i + 1) * size)
        total, sums = jnp.zeros((size, 128), F32), []
        for h in range(2):
            diag = jnp.zeros((size, 1), F32)
            for j in range(i + 1):
                there = slice(j * size, (j + 1) * size)
                scores = nt(queries[here], own_k[h][there]) - selfs[h][here]
                if i == j:
                    scores = jnp.where(lower, scores, FAR)
                weights = jnp.exp(scores)
                change = weights * (nt(scaled[here], own_v[h][there]) - fixes[h][here])
                diag = diag + jnp.sum(change, -1, keepdims=True)
                small = change.astype(BF16)
                total = total + nn(small, own_k[h][there])
                keys_t[j] = keys_t[j] + nn(q_t[h][:, here], small)
                values_t[j] = values_t[j] + nn(s_t[h][:, here], weights.astype(BF16))
            weights = jnp.exp(nt(queries[here], mem_k[h]) - selfs[h][here])
            change = weights * (nt(scaled[here], mem_v[h]) - fixes[h][here])
            diag = diag + jnp.sum(change, -1, keepdims=True)
            total = total + nn(change.astype(BF16), mem_k[h])
            sums.append(diag)
        diag = by_head(sums[0], sums[1], masks)
        diags.append(diag)
        grad_q = scale * (total - diag * keys[here].astype(F32))
        low[0, i * size // tok : (i + 1) * size // tok] = grad_q.astype(BF16).reshape(
            size // tok, tok, 128
        )
    for j in range(steps):
        there = slice(j * size, (j + 1) * size)
        grad_k = keys_t[j].T - diags[j] * queries[there].astype(F32)
        blocks_here = slice(j * size // tok, (j + 1) * size // tok)
        low[1, blocks_here] = grad_k.astype(BF16).reshape(size // tok, tok, 128)
        low[2, blocks_here] = values_t[j].T.astype(BF16).reshape(size // tok, tok, 128)
    for mask in range(blocks):
        for i in range(3):
            sends[mask][i, 0] = low[i, sc[2 + mask]]
    if halved:

        @pl.when(pl.program_id(1) != sc[1])
        def _():
            for mask in range(blocks):
                for i in range(3):
                    to_core[mask, i, 0] = low[i, sc[2 + mask]]


def feed_kernel(blocks, sc, *refs):
    att_in = refs[:blocks]
    rest = refs[blocks:]
    tokens, cot, w_out, gain, bias, w_in, w_down = rest[:7]
    mixed, grad_res, act_keep, inner_keep, to_core, normed_out, att_out, branch_keep, rows_core = rest[
        7:16
    ]
    sums = rest[16]
    grad_att = rest[17 : 17 + blocks]
    residual, normed, total, back = rest[17 + blocks :]
    step, steps = pl.program_id(0), pl.num_programs(0)
    part, width = att_in[0].shape[1], tokens.shape[1]
    my_block, core = sc[0], sc[1]

    def out_rows(mask):
        return pl.ds(pl.multiple_of((my_block ^ mask) * part, part), part)

    @pl.when(step == 0)
    def _():
        branch = tokens[...].astype(F32)
        for mask in range(blocks):
            branch = branch + nn(att_in[mask][...], w_out[out_rows(mask), :])
            att_out[:, out_rows(mask)] = att_in[mask][...]
        rows_core[:, width : 2 * width] = att_out[...]
        residual[...] = branch
        unit, _ = norm_stats(branch)
        low = (unit * gain[...].astype(F32) + bias[...].astype(F32)).astype(BF16)
        normed[...] = low
        normed_out[...] = low
        rows_core[:, :width] = low

    inner = nn(normed[...], w_in[...])
    square = inner * inner
    bend = jnp.tanh(GELU_A * inner * (1.0 + GELU_B * square))
    half = 0.5 * (1.0 + bend)
    act = (inner * half).astype(BF16)
    slope = half + (0.5 * GELU_A) * inner * (1.0 - bend * bend) * (1.0 + 3.0 * GELU_B * square)
    grad = (slope * nt(cot[...], w_down[...])).astype(BF16)
    into = nn(act, w_down[...])
    away = nt(grad, w_in[...])

    @pl.when(step == 0)
    def _():
        total[...] = into
        back[...] = away

    @pl.when(step > 0)
    def _():
        total[...] += into
        back[...] += away

    @pl.when(step % 2 == core)
    def _():
        act_keep[0] = act
        inner_keep[0] = grad

    @pl.when(step % 2 != core)
    def _():
        to_core[0, 0] = act
        to_core[1, 0] = grad

    @pl.when(step == steps - 1)
    def _():
        here = residual[...]
        mixed[...] = (here + total[...]).astype(BF16)
        unit, scale = norm_stats(here)
        away = back[...]
        sums[0:1] = jnp.sum(away * unit, 0, keepdims=True)
        sums[1:2] = jnp.sum(away, 0, keepdims=True)
        found = cot[...].astype(F32) + norm_back(unit, scale, gain[...].astype(F32), away)
        grad_res[...] = found
        low = found.astype(BF16)
        left, right = low[:, : width // 2], low[:, width // 2 :]
        branch_keep[...] = jnp.where(core == 0, left, right)
        rows_core[:, 2 * width :] = jnp.where(core == 0, right, left)
        for mask in range(blocks):
            grad_att[mask][...] = nt(low, w_out[out_rows(mask), :]).astype(BF16)


def weight_kernel(blocks, sc, *refs):
    (act, act_two, cot, cot_two, att, att_two, branch, branch_two) = refs[:8]
    normed, normed_two, inner, inner_two = refs[8:12]
    outs = refs[12:]
    step = pl.program_id(0)
    width = cot.shape[1]
    down = tn(act[0], cot[...]) + tn(act_two[0, 0], cot_two[...])
    out = tn(att[...], branch[...]) + tn(att_two[...], branch_two[...])
    part = out.shape[0]
    tile = down.shape[0]
    joined = [down.astype(BF16), out.astype(BF16)]
    half = (tile + part // 2) // 2

    def store_down(ref, lo):
        low, wide = joined
        hi = lo + half
        if lo < tile:
            ref[0, : min(hi, tile) - lo] = low[lo : min(hi, tile)]
        if hi > tile:
            first = max(lo, tile) - tile
            count = hi - tile - first
            at = half - count
            ref[0, at:, : width // 2] = wide[first : first + count]
            ref[0, at:, width // 2 :] = wide[part // 2 + first : part // 2 + first + count]

    ins = []
    for q in range(blocks):
        found = tn(normed[...], inner[q]) + tn(normed_two[...], inner_two[0, q])
        ins.append(found.astype(BF16))

    def store_in(ref, lo):
        tile_in = ins[0].shape[1]
        for q in range(blocks):
            ref[0, :, q * tile_in : (q + 1) * tile_in] = ins[q][lo : lo + part // 2]

    top = blocks // 2
    for i, (bit, lo) in enumerate(((1, 0), (top, 1))):
        @pl.when((step & bit) != 0)
        def _():
            store_down(outs[4 * i], lo * half)
            store_in(outs[4 * i + 2], lo * (part // 2))

        @pl.when((step & bit) == 0)
        def _():
            store_down(outs[4 * i + 1], lo * half)
            store_in(outs[4 * i + 3], lo * (part // 2))


def tokens_kernel(blocks, sc, tokens, grad_res, gain, *refs):
    pieces = refs[:blocks]
    weights = refs[blocks : blocks + 3]
    grad_tokens, sums, total = refs[blocks + 3 :]
    step, steps = pl.program_id(0), pl.num_programs(0)
    for mask in range(blocks):

        @pl.when(step == mask)
        def _():
            found = nt(pieces[mask][0], weights[0][...])
            found = found + nt(pieces[mask][1], weights[1][...])
            found = found + nt(pieces[mask][2], weights[2][...])
            if mask == 0:
                total[...] = found
            else:
                total[...] += found

    @pl.when(step == steps - 1)
    def _():
        unit, scale = norm_stats(tokens[...].astype(F32))
        grad = total[...]
        sums[0:1] = jnp.sum(grad * unit, 0, keepdims=True)
        sums[1:2] = jnp.sum(grad, 0, keepdims=True)
        grad_tokens[...] = grad_res[...] + norm_back(unit, scale, gain[...].astype(F32), grad)


def fetch_banks(mem_keys, mem_values, continues, groups, my_group, blocks, my_block):
    seq_count, rows, width = mem_keys.shape
    core, chips = my_group % 2, groups // 2
    my_chip = my_group // 2
    kept = jnp.where(core == 0, mem_keys, mem_values)
    sent = jnp.where(core == 0, mem_values, mem_keys)
    came = swap(sent, "grp", 1)
    pair = jnp.where(core == 0, jnp.stack([kept, came]), jnp.stack([came, kept]))
    per_chip = 2 * seq_count
    pair = pair.reshape(per_chip, chips, rows // chips, width)
    parts = [pick(pair, my_chip, 1)]
    for mask in range(1, chips):
        parts.append(swap(pick(pair, my_chip ^ mask, 1), "grp", 2 * mask))
    order = my_chip ^ jnp.arange(chips)
    every = jnp.take(jnp.stack(parts), order, axis=0).reshape(
        chips * per_chip, rows // chips, width
    )

    def needed(chip):
        banks = lax.dynamic_slice_in_dim(continues, chip * per_chip, per_chip)
        return jnp.take(every, banks, axis=0)

    parts = [needed(my_chip)]
    for mask in range(1, chips):
        parts.append(swap(needed(my_chip ^ mask), "grp", 2 * mask))
    held = jnp.stack(parts, 1).reshape(2, seq_count, rows, width)
    kept = pick(held, core)
    came = swap(pick(held, 1 - core), "grp", 1)
    keys = jnp.where(core == 0, kept, came)
    values = jnp.where(core == 0, came, kept)
    part = width // blocks
    both = jnp.stack([keys, values])

    def columns(block):
        return lax.dynamic_slice_in_dim(both, block * part, part, 3)

    parts = [columns(my_block)]
    for mask in range(1, blocks):
        parts.append(swap(columns(my_block ^ mask), "blk", mask))
    return parts


def add(*values):
    total = values[0].astype(F32)
    for value in values[1:]:
        total = total + value.astype(F32)
    return total.astype(BF16)


def reduce_blocks(sent, kept, first_bit, order, blocks):
    masks = [m for m in range(blocks) if not m & first_bit]
    came = swap(sent, "blk", first_bit)
    terms = {m: [kept[i], came[i]] for i, m in enumerate(masks)}
    for bit in order:
        away = [m for m in masks if m & bit]
        masks = [m for m in masks if not m & bit]
        if len(away) == 1:
            came = swap(add(*terms[away[0]]), "blk", bit)[None]
        else:
            came = swap(jnp.stack([add(*terms[m]) for m in away]), "blk", bit)
        for i, m in enumerate(masks):
            terms[m].append(came[i])
    return terms[0]


def reduce_groups(parts, groups, my_group):
    bits = groups.bit_length() - 1
    low = (my_group >> 1) & 1
    if len(parts) == 2:
        first, second = add(*parts[0]), add(*parts[1])
        mine = jnp.where(low == 0, first, second)
        other = jnp.where(low == 0, second, first)
    else:
        whole = add(*parts[0])
        halves = whole.reshape((2, whole.shape[0] // 2) + whole.shape[1:])
        mine, other = pick(halves, low), pick(halves, 1 - low)
    came = swap(other, "grp", 2)
    held = add(mine, came)
    for bit in range(2, bits):
        held = add(held, swap(held, "grp", 1 << bit))
    came = swap(held, "grp", 2)
    return jnp.where(low == 0, jnp.stack([held, came]), jnp.stack([came, held]))


def join_cores(values, core):
    came = swap(values, "grp", 1)
    return jnp.where(core == 0, jnp.stack([values, came]), jnp.stack([came, values]))


def on_device(
    tokens,
    gain_one,
    bias_one,
    w_qkv,
    w_out,
    gain_two,
    bias_two,
    w_in,
    w_down,
    mem_keys,
    mem_values,
    continues,
    block_place,
    cotangent,
):
    seq_count, tok, width = tokens.shape
    hidden_width = w_in.shape[1]
    blocks, groups = lax.axis_size("blk"), lax.axis_size("grp")
    my_block, my_group = lax.axis_index("blk"), lax.axis_index("grp")
    core = my_group % 2
    part = width // blocks
    pairs = part // 128
    halved = pairs > 1
    rows = seq_count * tok
    seg_rows = blocks * tok
    tile = hidden_width // (2 * blocks)
    places = [block_place[my_block ^ mask] for mask in range(blocks)]
    scalars = jnp.stack([my_block, core] + places).astype(jnp.int32)
    gain_one, bias_one = gain_one.reshape(1, width), bias_one.reshape(1, width)
    gain_two, bias_two = gain_two.reshape(1, width), bias_two.reshape(1, width)
    flat = tokens.reshape(rows, width)
    cot = cotangent.reshape(rows, width)

    pieces = [flat] + [swap(flat, "blk", mask) for mask in range(1, blocks)]
    cot_two = swap(cot, "grp", 1)
    mem = fetch_banks(mem_keys, mem_values, continues, groups, my_group, blocks, my_block)

    def head_weights(j, at=None):
        def index(i, sc):
            return (0, j * blocks + (sc[0] ^ i if at is None else sc[0]))

        return (w_qkv, (width, part), index)

    normed, qkv = [], []
    for piece in pieces:
        found = call(
            project_kernel,
            "project",
            (1,),
            [piece, gain_one, bias_one] + [head_weights(j, 0) for j in range(3)],
            [((rows, width), BF16), ((rows, 3 * part), BF16)],
            [],
            scalars,
            24,
            (6 * rows * width * part, 4 * rows * width + 6 * width * part),
        )
        normed.append(found[0])
        qkv.append(found[1].reshape(seq_count, tok, 3 * part))

    def heads_block(j):
        return (1, tok, 128), lambda s, p, sc: (s, 0, j * pairs + p)

    seg_block = (1, seg_rows, 128), lambda s, p, sc: (s, 0, p)
    seg_shape = (seq_count, seg_rows, part)
    tok_block = (1, tok, 128), lambda s, p, sc: (s, 0, p)
    mem_block = (2, 1, tok, 128), lambda s, p, sc: (0, s, 0, p)
    queries, keys, values, partial, counts = call(
        functools.partial(own_kernel, blocks),
        "own_keys",
        (seq_count, pairs),
        [(qkv[m],) + heads_block(j) for m in range(blocks) for j in range(3)],
        [(seg_shape, BF16) + seg_block] * 3 + [(seg_shape, F32) + seg_block] * 2,
        [pltpu.VMEM((3, blocks, tok, 128), BF16)],
        scalars,
        32,
        (2 * seq_count * seg_rows * seg_rows * part, 8 * seq_count * seg_rows * part),
    )
    found = call(
        functools.partial(cached_kernel, blocks),
        "cached_keys",
        (seq_count, pairs),
        [(a,) + seg_block for a in (queries, keys, partial, counts)]
        + [(a,) + mem_block for a in mem],
        [(seg_shape, F32) + seg_block] * 2
        + [((seq_count, tok, part), BF16) + tok_block] * blocks,
        [pltpu.VMEM((2, seg_rows, 128), BF16), pltpu.VMEM((blocks, tok, 128), BF16)],
        scalars,
        32,
        (4 * seq_count * seg_rows * seg_rows * part, 16 * seq_count * seg_rows * part),
    )
    attended_f, counts = found[:2]
    attended = [found[2]] + [swap(found[2 + m], "blk", m) for m in range(1, blocks)]
    attended = [a.reshape(rows, part) for a in attended]

    tile_block = (1, rows, tile), lambda j, sc: (j // 2, 0, 0)
    found = call(
        functools.partial(feed_kernel, blocks),
        "feed",
        (2 * blocks,),
        attended
        + [flat, cot, w_out, gain_two, bias_two]
        + [
            (w_in, (width, tile), lambda j, sc: (0, j)),
            (w_down, (tile, width), lambda j, sc: (j, 0)),
        ],
        [
            ((rows, width), BF16),
            ((rows, width), F32),
            ((blocks, rows, tile), BF16) + tile_block,
            ((blocks, rows, tile), BF16) + tile_block,
            ((2, blocks, rows, tile), BF16, (2, 1, rows, tile), lambda j, sc: (0, j // 2, 0, 0)),
            ((rows, width), BF16),
            ((rows, width), BF16),
            ((rows, width // 2), BF16),
            ((rows, 2 * width + width // 2), BF16),
            ((2, width), F32),
        ]
        + [((rows, part), BF16)] * blocks,
        [
            pltpu.VMEM((rows, width), F32),
            pltpu.VMEM((rows, width), BF16),
            pltpu.VMEM((rows, width), F32),
            pltpu.VMEM((rows, width), F32),
        ],
        scalars,
        48,
        (8 * rows * width * hidden_width, 4 * width * hidden_width + 30 * rows * width),
    )
    mixed, grad_res, act_keep, inner_keep, to_core, normed_two, att_all, branch, rows_core = found[:9]
    sums_two = found[9]
    grad_att = found[10:]
    grad_att = [grad_att[0]] + [swap(grad_att[m], "blk", m) for m in range(1, blocks)]
    grad_att = [g.reshape(seq_count, tok, part) for g in grad_att]
    rows_came = swap(rows_core, "grp", 1)
    tiles_came = swap(to_core, "grp", 1)

    height = tile + part // 2
    half_rows = height // 2
    top = blocks // 2

    def of_mask(shape, mask, wanted):
        def index(m, sc):
            if mask == 1:
                return (m >> 1, 0, 0)
            return (jnp.maximum(m - top, 0) if wanted else jnp.minimum(m, top - 1), 0, 0)

        return ((top,) + shape, BF16, (1,) + shape, index)

    down_shape, in_shape = (half_rows, width), (part // 2, blocks * tile)
    outs = []
    for mask in (1, top):
        for shape in (down_shape, in_shape):
            outs += [of_mask(shape, mask, True), of_mask(shape, mask, False)]

    def columns(base):
        return lambda m, sc: (0, base + (sc[0] ^ m))

    found = call(
        functools.partial(weight_kernel, blocks),
        "weights",
        (blocks,),
        [
            (act_keep, (1, rows, tile), lambda m, sc: (sc[0] ^ m, 0, 0)),
            (tiles_came, (1, 1, rows, tile), lambda m, sc: (0, sc[0] ^ m, 0, 0)),
            cot,
            cot_two,
            (att_all, (rows, part), columns(0)),
            (rows_came, (rows, part), columns(blocks)),
            branch,
            (rows_came, (rows, width // 2), lambda m, sc: (0, 4)),
            (normed_two, (rows, part), columns(0)),
            (rows_came, (rows, part), columns(0)),
            inner_keep,
            (tiles_came, (1, blocks, rows, tile), lambda m, sc: (1, 0, 0, 0)),
        ],
        outs,
        [],
        scalars,
        48,
        (8 * rows * width * hidden_width, 10 * width * hidden_width),
    )
    bits = [1 << i for i in range(blocks.bit_length() - 1)]
    down_parts = [
        reduce_blocks(found[0], found[1], 1, bits[1:], blocks),
        reduce_blocks(found[4], found[5], top, bits[:-1][::-1], blocks),
    ]
    in_parts = [
        reduce_blocks(found[2], found[3], 1, bits[1:], blocks),
        reduce_blocks(found[6], found[7], top, bits[:-1][::-1], blocks),
    ]

    def spread(parts):
        joined = reduce_groups(parts, groups, my_group)
        return join_cores(joined.reshape((-1,) + joined.shape[2:]), core)

    found = call(
        functools.partial(attention_back_kernel, blocks, halved),
        "attention_back",
        (seq_count, pairs),
        [(a,) + seg_block for a in (queries, keys, values, attended_f, counts)]
        + [(a,) + mem_block for a in mem]
        + [(a,) + tok_block for a in grad_att],
        [
            (
                (3, seq_count, tok, part),
                BF16,
                (3, 1, tok, 128),
                lambda s, p, sc: (0, s, 0, p),
            )
        ]
        * blocks
        + (
            [
                (
                    (blocks, 3, seq_count, tok, 128),
                    BF16,
                    (blocks, 3, 1, tok, 128),
                    lambda s, p, sc: (0, 0, s, 0, 0),
                )
            ]
            if halved
            else []
        ),
        [
            pltpu.VMEM((2, seg_rows, 128), BF16),
            pltpu.VMEM((blocks, tok, 128), BF16),
            pltpu.VMEM((3, blocks, tok, 128), BF16),
        ],
        scalars,
        48,
        (10 * seq_count * seg_rows * seg_rows * part, 24 * seq_count * seg_rows * part),
    )
    own_grads = [g.reshape(3, rows, part) for g in found[:blocks]]
    grads = [own_grads[0]] + [swap(own_grads[m], "blk", m) for m in range(1, blocks)]

    found_tokens = call(
        functools.partial(tokens_kernel, blocks),
        "tokens_back",
        (blocks,),
        [flat, grad_res, gain_one] + grads + [head_weights(j) for j in range(3)],
        [((rows, width), F32), ((2, width), F32)],
        [pltpu.VMEM((rows, width), F32)],
        scalars,
        32,
        (6 * rows * width * width, 6 * width * width + 12 * rows * width),
    )
    grad_tokens, sums_one = found_tokens

    own = jnp.concatenate([jnp.concatenate([g[i] for i in range(3)], 1) for g in own_grads], 0)
    normed_all = jnp.concatenate(normed, 0)
    qkv_grad = tn(normed_all, own)
    qkv_grad = qkv_grad.astype(BF16).reshape(blocks, part, 3 * part)
    if halved:
        halves = qkv_grad.reshape(blocks, 2, part // 2, 3 * part)
        came = swap(pick(halves, 1 - core, 1), "grp", 1)
        qkv_grad = add(pick(halves, core, 1), came)
    else:
        qkv_grad = add(qkv_grad, swap(qkv_grad, "grp", 1))
    parts = [pick(qkv_grad, my_block)]
    for mask in range(1, blocks):
        parts.append(swap(pick(qkv_grad, my_block ^ mask), "blk", mask))
    order = my_block ^ jnp.arange(blocks)
    parts = jnp.take(jnp.stack(parts), order, axis=0).reshape(blocks, -1, 3, part)
    parts = jnp.transpose(parts, (1, 2, 0, 3)).reshape(-1, 3 * width)
    joined = reduce_groups([[parts]], groups, my_group).reshape(-1, 3 * width)
    if halved:
        joined = join_cores(joined, core)
    grad_qkv = joined.reshape(part, 3 * width).astype(F32)

    both = spread(down_parts)
    grad_down = both[:, :tile].reshape(2 * tile, width).astype(F32)
    grad_out = both[:, tile:].reshape(2, part // 2, 2, width // 2)
    grad_out = jnp.transpose(grad_out, (2, 1, 0, 3)).reshape(part, width).astype(F32)
    both = spread(in_parts).reshape(2, part, blocks, tile)
    grad_in = jnp.transpose(both, (1, 2, 0, 3)).reshape(part, hidden_width).astype(F32)

    vectors = jnp.concatenate([sums_one, sums_two], 0)
    for bit in range(groups.bit_length() - 1):
        vectors = vectors + swap(vectors, "grp", 1 << bit)
    for bit in bits:
        vectors = vectors + swap(vectors, "blk", bit)
    vectors = pick(vectors.reshape(4, blocks, part), my_block, 1)
    return (
        mixed.reshape(tokens.shape),
        grad_tokens.reshape(tokens.shape),
        vectors[0],
        vectors[1],
        grad_qkv,
        grad_out,
        vectors[2],
        vectors[3],
        grad_in,
        grad_down,
    )


def solution(mesh):
    rows = P("grp", "blk", None)
    in_specs = (rows,) + (P(),) * 8 + (rows, rows, P(), P(), rows)
    out_specs = (rows, rows) + (P("blk"),) * 2 + (P("blk", None),) * 2
    out_specs = out_specs + (P("blk"),) * 2 + (P("blk", None),) * 2
    return jax.shard_map(
        on_device, mesh=mesh, in_specs=in_specs, out_specs=out_specs, check_vma=False
    )
```

```python
import functools

import jax
import jax.numpy as jnp
from jax import lax
from jax.experimental import pallas as pl
from jax.experimental.pallas import tpu as pltpu
from jax.sharding import PartitionSpec as P

HEADS = 16
F32 = jnp.float32
BF16 = jnp.bfloat16
MIB = 1 << 20
EPS = 1e-05
FAR = -1e30
GELU_A = 0.7978845608028654
GELU_B = 0.044715


def swap(values, axis, mask):
    size = lax.axis_size(axis)
    return lax.ppermute(values, axis, [(i, i ^ mask) for i in range(size)])


def pick(values, index, dim=0):
    return lax.dynamic_index_in_dim(values, index, dim, keepdims=False)


def nn(left, right):
    return lax.dot_general(left, right, (((1,), (0,)), ((), ())), preferred_element_type=F32)


def nt(left, right):
    return lax.dot_general(left, right, (((1,), (1,)), ((), ())), preferred_element_type=F32)


def tn(left, right):
    return lax.dot_general(left, right, (((0,), (0,)), ((), ())), preferred_element_type=F32)


def params(mib):
    return pltpu.CompilerParams(vmem_limit_bytes=mib * MIB)


ANYWHERE = pl.BlockSpec(memory_space=pl.ANY)
EVERY = range(100)
COMPUTE = (
    "project",
    "own_keys",
    "cached_keys",
    "feed",
    "attention_back",
    "grad_qkv",
    "grad_in",
    "grad_down",
    "tokens_back",
)
LONG = pl.CostEstimate(flops=10**11, bytes_accessed=10**6, transcendentals=0)
SHORT = pl.CostEstimate(flops=10**10, bytes_accessed=10**11, transcendentals=0)
OUT_HBM = {
    "project": (0,),
    "own_keys": EVERY,
    "cached_keys": (0, 1),
    "feed": (0, 1, 2, 4, 5, 6, 8, 9, 10, 11, 12, 13, 14, 15),
}
IN_HBM = {"cached_keys": (0, 1, 2, 3), "attention_back": EVERY, "grad_qkv": (0, 1, 2, 3)}


def call(kernel, name, grid, ins, outs, scratch, scalars, mib, tokens=()):
    def whole(shape):
        return pl.BlockSpec(shape, lambda *_: (0,) * len(shape))

    in_specs, arrays = [], []
    for item in ins:
        if isinstance(item, tuple):
            arrays.append(item[0])
            in_specs.append(pl.BlockSpec(item[1], item[2]))
        else:
            arrays.append(item)
            in_specs.append(whole(item.shape))
    out_shapes, out_specs = [], []
    for item in outs:
        out_shapes.append(jax.ShapeDtypeStruct(item[0], item[1]))
        out_specs.append(whole(item[0]) if len(item) == 2 else pl.BlockSpec(item[2], item[3]))
    count = len(arrays)

    pinned = IN_HBM.get(name, ())
    arrays = [
        pltpu.with_memory_space_constraint(a, pltpu.HBM) if i in pinned else a
        for i, a in enumerate(arrays)
    ]
    pinned = OUT_HBM.get(name, ())
    out_shapes = [
        pltpu.HBM(o.shape, o.dtype) if i in pinned else o for i, o in enumerate(out_shapes)
    ]

    def body(sc, *refs):
        kernel(sc, *refs[:count], *refs[count + len(tokens) :])

    spec = pltpu.PrefetchScalarGridSpec(
        num_scalar_prefetch=1,
        grid=grid,
        in_specs=in_specs + [ANYWHERE] * len(tokens),
        out_specs=out_specs,
        scratch_shapes=scratch,
    )
    return pl.pallas_call(
        body,
        grid_spec=spec,
        out_shape=out_shapes,
        compiler_params=params(mib),
        cost_estimate=LONG if name in COMPUTE else SHORT,
        name=name,
    )(scalars, *arrays, *tokens)


def gate(values, tokens):
    count = len(values)
    return pl.pallas_call(
        lambda *refs: None,
        in_specs=[ANYWHERE] * (count + len(tokens)),
        out_specs=[ANYWHERE] * count,
        out_shape=[jax.ShapeDtypeStruct(v.shape, v.dtype) for v in values],
        input_output_aliases={i: i for i in range(count)},
        name="gate",
    )(*values, *tokens)


def norm_stats(values):
    average = jnp.mean(values, -1, keepdims=True)
    centred = values - average
    scale = lax.rsqrt(jnp.mean(centred * centred, -1, keepdims=True) + EPS)
    return centred * scale, scale


def norm_back(unit, scale, gain, grad):
    scaled = grad * gain
    mean_one = jnp.mean(scaled, -1, keepdims=True)
    mean_two = jnp.mean(scaled * unit, -1, keepdims=True)
    return scale * (scaled - mean_one - unit * mean_two)


def project_kernel(sc, rows, gain, bias, wq, wk, wv, normed, qkv):
    part = wq.shape[1]
    unit, _ = norm_stats(rows[...].astype(F32))
    low = (unit * gain[...].astype(F32) + bias[...].astype(F32)).astype(BF16)
    normed[...] = low
    for i, weight in enumerate((wq, wk, wv)):
        qkv[:, i * part : (i + 1) * part] = nn(low, weight[...]).astype(BF16)


def lane_masks():
    lane = lax.broadcasted_iota(jnp.int32, (1, 128), 1)
    return [lane < 64, lane >= 64]


def of_head(values, mask):
    return jnp.where(mask, values, jnp.zeros_like(values))


def by_head(first, second, masks):
    return jnp.where(masks[0], first, second)


BLOCK = 256


def own_kernel(blocks, sc, *refs):
    ins, outs = refs[: 3 * blocks], refs[3 * blocks :]
    q_out, k_out, v_out, t_out, l_out = outs[:5]
    held = outs[5]
    tok = ins[0].shape[1]
    scale = 64 ** (-0.5)
    for mask in range(blocks):
        place = sc[2 + mask]
        for i in range(3):
            values = ins[3 * mask + i][0]
            if i == 0:
                values = (values.astype(F32) * scale).astype(BF16)
            held[i, place] = values
    rows = blocks * tok
    queries = held[0].reshape(rows, 128)
    keys = held[1].reshape(rows, 128)
    values = held[2].reshape(rows, 128)
    q_out[0], k_out[0], v_out[0] = queries, keys, values
    masks = lane_masks()
    size = min(BLOCK, rows)
    lower = lax.broadcasted_iota(jnp.int32, (size, size), 0) >= lax.broadcasted_iota(
        jnp.int32, (size, size), 1
    )
    product = queries.astype(F32) * keys.astype(F32)
    head_keys = [of_head(keys, m) for m in masks]
    head_values = [of_head(values, m) for m in masks]
    selfs = [jnp.sum(of_head(product, m), -1, keepdims=True) for m in masks]
    for i in range(rows // size):
        here = slice(i * size, (i + 1) * size)
        total, sums = jnp.zeros((size, 128), F32), []
        for h in range(2):
            count = jnp.zeros((size, 1), F32)
            for j in range(i + 1):
                there = slice(j * size, (j + 1) * size)
                scores = nt(queries[here], head_keys[h][there]) - selfs[h][here]
                if i == j:
                    scores = jnp.where(lower, scores, FAR)
                weights = jnp.exp(scores)
                count = count + jnp.sum(weights, -1, keepdims=True)
                total = total + nn(weights.astype(BF16), head_values[h][there])
            sums.append(count)
        t_out[0, here] = total
        l_out[0, here] = by_head(sums[0], sums[1], masks)


def load_cached(pieces, mem):
    tok = pieces[0].shape[2]
    for mask, piece in enumerate(pieces):
        mem[:, mask * tok : (mask + 1) * tok] = piece[:, 0]


def cached_kernel(blocks, sc, *refs):
    q_in, k_in, t_in, l_in = refs[:4]
    pieces = refs[4 : 4 + blocks]
    att_out, l_out = refs[4 + blocks : 6 + blocks]
    sends = refs[6 + blocks : 6 + 2 * blocks]
    mem, low = refs[6 + 2 * blocks :]
    load_cached(pieces, mem)
    tok = pieces[0].shape[2]
    queries, keys = q_in[0], k_in[0]
    rows = queries.shape[0]
    masks = lane_masks()
    product = queries.astype(F32) * keys.astype(F32)
    selfs = [jnp.sum(of_head(product, m), -1, keepdims=True) for m in masks]
    head_keys = [of_head(mem[0], m) for m in masks]
    head_values = [of_head(mem[1], m) for m in masks]
    size = min(BLOCK, rows)
    for i in range(rows // size):
        here = slice(i * size, (i + 1) * size)
        total, sums = t_in[0, here], []
        for h in range(2):
            weights = jnp.exp(nt(queries[here], head_keys[h]) - selfs[h][here])
            sums.append(jnp.sum(weights, -1, keepdims=True))
            total = total + nn(weights.astype(BF16), head_values[h])
        count = l_in[0, here] + by_head(sums[0], sums[1], masks)
        attended = total / count
        att_out[0, here] = attended
        l_out[0, here] = count
        low[i * size // tok : (i + 1) * size // tok] = attended.astype(BF16).reshape(
            size // tok, tok, 128
        )
    for mask in range(blocks):
        sends[mask][0] = low[sc[2 + mask]]


def attention_back_kernel(blocks, sc, *refs):
    q_in, k_in, v_in, att_in, l_in = refs[:5]
    pieces = refs[5 : 5 + blocks]
    grads = refs[5 + blocks : 5 + 2 * blocks]
    sends = refs[5 + 2 * blocks : 5 + 3 * blocks]
    mem, came, low = refs[5 + 3 * blocks :]
    load_cached(pieces, mem)
    tok = pieces[0].shape[2]
    for mask in range(blocks):
        came[sc[2 + mask]] = grads[mask][0]
    queries, keys, values = q_in[0], k_in[0], v_in[0]
    rows = queries.shape[0]
    scale = 64 ** (-0.5)
    masks = lane_masks()
    grad = came[...].reshape(rows, 128).astype(F32)
    count = l_in[0]
    scaled_f = grad / count
    scaled = scaled_f.astype(BF16)
    weighed = grad * att_in[0] / count
    product = queries.astype(F32) * keys.astype(F32)
    selfs = [jnp.sum(of_head(product, m), -1, keepdims=True) for m in masks]
    fixes = [jnp.sum(of_head(weighed, m), -1, keepdims=True) for m in masks]
    own_k = [of_head(keys, m) for m in masks]
    own_v = [of_head(values, m) for m in masks]
    mem_k = [of_head(mem[0], m) for m in masks]
    mem_v = [of_head(mem[1], m) for m in masks]
    q_t = [of_head(queries, m).astype(F32).T.astype(BF16) for m in masks]
    s_t = [of_head(scaled, m).astype(F32).T.astype(BF16) for m in masks]
    size = min(BLOCK, rows)
    lower = lax.broadcasted_iota(jnp.int32, (size, size), 0) >= lax.broadcasted_iota(
        jnp.int32, (size, size), 1
    )
    steps = rows // size
    keys_t = [jnp.zeros((128, size), F32) for _ in range(steps)]
    values_t = [jnp.zeros((128, size), F32) for _ in range(steps)]
    diags = []
    for i in range(steps):
        here = slice(i * size, (i + 1) * size)
        total, sums = jnp.zeros((size, 128), F32), []
        for h in range(2):
            diag = jnp.zeros((size, 1), F32)
            for j in range(i + 1):
                there = slice(j * size, (j + 1) * size)
                scores = nt(queries[here], own_k[h][there]) - selfs[h][here]
                if i == j:
                    scores = jnp.where(lower, scores, FAR)
                weights = jnp.exp(scores)
                change = weights * (nt(scaled[here], own_v[h][there]) - fixes[h][here])
                diag = diag + jnp.sum(change, -1, keepdims=True)
                small = change.astype(BF16)
                total = total + nn(small, own_k[h][there])
                keys_t[j] = keys_t[j] + nn(q_t[h][:, here], small)
                values_t[j] = values_t[j] + nn(s_t[h][:, here], weights.astype(BF16))
            weights = jnp.exp(nt(queries[here], mem_k[h]) - selfs[h][here])
            change = weights * (nt(scaled[here], mem_v[h]) - fixes[h][here])
            diag = diag + jnp.sum(change, -1, keepdims=True)
            total = total + nn(change.astype(BF16), mem_k[h])
            sums.append(diag)
        diag = by_head(sums[0], sums[1], masks)
        diags.append(diag)
        grad_q = scale * (total - diag * keys[here].astype(F32))
        low[0, i * size // tok : (i + 1) * size // tok] = grad_q.astype(BF16).reshape(
            size // tok, tok, 128
        )
    for j in range(steps):
        there = slice(j * size, (j + 1) * size)
        grad_k = keys_t[j].T - diags[j] * queries[there].astype(F32)
        blocks_here = slice(j * size // tok, (j + 1) * size // tok)
        low[1, blocks_here] = grad_k.astype(BF16).reshape(size // tok, tok, 128)
        low[2, blocks_here] = values_t[j].T.astype(BF16).reshape(size // tok, tok, 128)
    for mask in range(blocks):
        for i in range(3):
            sends[mask][i, 0] = low[i, sc[2 + mask]]


def feed_kernel(blocks, sc, *refs):
    att_in = refs[:blocks]
    rest = refs[blocks:]
    tokens, cot, w_out, gain, bias, w_in, w_down = rest[:7]
    mixed, grad_res, inner_keep, to_core, normed_out, att_out, branch_keep, sums = rest[7:15]
    acts = rest[15 : 15 + blocks]
    grad_att = rest[15 + blocks : 15 + 2 * blocks]
    residual, normed, total, back = rest[15 + 2 * blocks :]
    step, steps = pl.program_id(0), pl.num_programs(0)
    part, width, tile = att_in[0].shape[1], tokens.shape[1], w_in.shape[1]
    my_block, core = sc[0], sc[1]
    base = blocks * tile

    def out_rows(mask):
        return pl.ds(pl.multiple_of((my_block ^ mask) * part, part), part)

    @pl.when(step == 0)
    def _():
        branch = tokens[...].astype(F32)
        for mask in range(blocks):
            branch = branch + nn(att_in[mask][...], w_out[out_rows(mask), :])
            att_out[:, out_rows(mask)] = att_in[mask][...]
        to_core[:, base + width : base + 2 * width] = att_out[...]
        residual[...] = branch
        unit, _ = norm_stats(branch)
        low = (unit * gain[...].astype(F32) + bias[...].astype(F32)).astype(BF16)
        normed[...] = low
        normed_out[...] = low
        to_core[:, base : base + width] = low

    inner = nn(normed[...], w_in[...])
    square = inner * inner
    bend = jnp.tanh(GELU_A * inner * (1.0 + GELU_B * square))
    half = 0.5 * (1.0 + bend)
    act = (inner * half).astype(BF16)
    slope = half + (0.5 * GELU_A) * inner * (1.0 - bend * bend) * (1.0 + 3.0 * GELU_B * square)
    grad = (slope * nt(cot[...], w_down[...])).astype(BF16)
    into = nn(act, w_down[...])
    away = nt(grad, w_in[...])

    @pl.when(step == 0)
    def _():
        total[...] = into
        back[...] = away

    @pl.when(step > 0)
    def _():
        total[...] += into
        back[...] += away

    for j in range(2 * blocks):

        @pl.when(step == j)
        def _():
            acts[j // 2][:, (j % 2) * tile : (j % 2 + 1) * tile] = act

    columns = pl.ds(pl.multiple_of((my_block ^ (step // 2)) * tile, tile), tile)

    @pl.when(step % 2 == core)
    def _():
        inner_keep[:, columns] = grad

    @pl.when(step % 2 != core)
    def _():
        to_core[:, columns] = grad

    @pl.when(step == steps - 1)
    def _():
        here = residual[...]
        mixed[...] = (here + total[...]).astype(BF16)
        unit, scale = norm_stats(here)
        away = back[...]
        sums[0:1] = jnp.sum(away * unit, 0, keepdims=True)
        sums[1:2] = jnp.sum(away, 0, keepdims=True)
        found = cot[...].astype(F32) + norm_back(unit, scale, gain[...].astype(F32), away)
        grad_res[...] = found
        low = found.astype(BF16)
        left, right = low[:, : width // 2], low[:, width // 2 :]
        branch_keep[...] = jnp.where(core == 0, left, right)
        to_core[:, base + 2 * width :] = jnp.where(core == 0, right, left)
        for mask in range(blocks):
            grad_att[mask][...] = nt(low, w_out[out_rows(mask), :]).astype(BF16)


def in_kernel(blocks, sc, *refs):
    (normed, normed_two, inner, inner_two, att, att_two, branch, branch_two) = refs[:8]
    outs, held = refs[8:12], refs[12]
    part = normed.shape[1]
    tile = inner.shape[1] // blocks
    for q in range(blocks):
        columns = slice(q * tile, (q + 1) * tile)
        found = tn(normed[...], inner[:, columns]) + tn(normed_two[...], inner_two[:, columns])
        held[:part, columns] = found.astype(BF16)
    out = (tn(att[...], branch[...]) + tn(att_two[...], branch_two[...])).astype(BF16)
    width = out.shape[1]
    cuts = held.shape[1] // width
    high = part // cuts
    for i in range(cuts):
        held[part : part + high, i * width : (i + 1) * width] = out[i * high : (i + 1) * high]
    step = pl.program_id(0)
    half = held.shape[0] // 2
    for i, bit in enumerate((1, blocks // 2)):

        @pl.when((step & bit) != 0)
        def _():
            outs[2 * i][0] = held[i * half : (i + 1) * half]

        @pl.when((step & bit) == 0)
        def _():
            outs[2 * i + 1][0] = held[i * half : (i + 1) * half]


def down_kernel(blocks, sc, *refs):
    acts, cots, (sent, kept) = refs[:blocks], refs[blocks : 2 * blocks], refs[2 * blocks :]
    total = tn(acts[0][...], cots[0][...])
    for mask in range(1, blocks):
        total = total + tn(acts[mask][...], cots[mask][...])
    low = total.astype(BF16)

    @pl.when(pl.program_id(0) == 0)
    def _():
        sent[...] = low

    @pl.when(pl.program_id(0) == 1)
    def _():
        kept[...] = low


def qkv_kernel(blocks, halved, sc, *refs):
    normed, grads = refs[:blocks], refs[blocks : 2 * blocks]
    weights = refs[2 * blocks : 2 * blocks + 3]
    gain, bias, sums_two = refs[2 * blocks + 3 : 2 * blocks + 6]
    outs = refs[2 * blocks + 6 :]
    part = grads[0].shape[2]
    share = part // 2 if halved else part
    ahead = jnp.zeros((part, 1), F32)
    plain = jnp.zeros((part, 1), F32)
    for j in range(3):
        total = tn(normed[0][...], grads[0][j])
        count = jnp.sum(grads[0][j].astype(F32), 0, keepdims=True)
        for mask in range(1, blocks):
            total = total + tn(normed[mask][...], grads[mask][j])
            count = count + jnp.sum(grads[mask][j].astype(F32), 0, keepdims=True)
        weight = weights[j][...].astype(F32)
        ahead = ahead + jnp.sum(weight * total, -1, keepdims=True)
        plain = plain + jnp.sum(weight * count, -1, keepdims=True)
        low = total.astype(BF16)
        columns = slice(j * part, (j + 1) * part)
        if halved:
            first, second = low[:share], low[share:]
            outs[0][0, :share, columns] = jnp.where(sc[1] == 0, second, first)
            outs[1][0, :share, columns] = jnp.where(sc[1] == 0, first, second)
        else:
            outs[0][0, :share, columns] = low
    flat = [jnp.broadcast_to(v, (part, 128)).T[0:1] for v in (ahead, plain)]
    shift = (flat[0] - bias[...].astype(F32) * flat[1]) / gain[...].astype(F32)
    row = lax.broadcasted_iota(jnp.int32, (16, part), 0)
    vectors = jnp.zeros((16, part), F32)
    for i, vector in enumerate((shift, flat[1], sums_two[0:1], sums_two[1:2])):
        vectors = jnp.where(row == i, vector, vectors)
    vectors = vectors.astype(BF16)
    for out in outs:
        out[0, share:] = jnp.zeros((16, 3 * part), BF16)
    outs[-1][0, share:, :part] = vectors


def down_finish_kernel(sc, *refs):
    parts, grad_down = refs[:4], refs[4]
    core, low = sc[1], sc[sc.shape[0] - 1]
    for i in range(4):
        wanted = 2 * (core ^ (i // 2)) + (low ^ (i % 2))

        @pl.when(pl.program_id(0) == wanted)
        def _():
            grad_down[...] = parts[i][...].astype(F32)


def in_finish_kernel(blocks, sc, *refs):
    parts, (grad_in, grad_out, held) = refs[:4], refs[4:]
    step = pl.program_id(0)
    core, low = sc[1], sc[sc.shape[0] - 1]
    half, columns = parts[0].shape
    part, tile = grad_in.shape
    width = grad_out.shape[1]
    cuts = columns // width
    high = part // cuts

    @pl.when(step == 0)
    def _():
        for i in range(4):
            rows = pl.ds(pl.multiple_of((low ^ (i % 2)) * half, 16), half)
            held[i // 2, rows] = parts[i][...]

    which = jnp.where(step % 2 == core, 0, 1)
    at = pl.ds(pl.multiple_of((step // 2) * tile, tile), tile)
    grad_in[...] = held[which, :part, at].astype(F32)

    @pl.when(step < 2)
    def _():
        for i in range(cuts):
            grad_out[i * high : (i + 1) * high] = held[
                which, part : part + high, i * width : (i + 1) * width
            ].astype(F32)


def qkv_finish_kernel(blocks, halved, sc, *refs):
    parts, (grad_qkv, sums, held) = refs[:4], refs[4:]
    half, _, part = parts[0].shape
    share = grad_qkv.shape[0]
    core, low = sc[1], sc[sc.shape[0] - 1]
    mine = (pl.program_id(0) == core) if halved else True
    for i in range(4):
        for j in range(half):
            held[i // 2, (low ^ (i % 2)) * half + j] = parts[i][j].astype(F32)
    for mask in range(blocks):
        columns = pl.ds(pl.multiple_of((sc[0] ^ mask) * part, part), part)
        grad_qkv[:, columns] = jnp.where(mine, held[0, mask, :share], held[1, mask, :share])

    @pl.when((pl.program_id(0) == 0) & (pl.program_id(1) == 0))
    def _():
        total = jnp.zeros((8, part), F32)
        for i in range(2 if halved else 1):
            for mask in range(blocks):
                total = total + held[i, mask, share : share + 8]
        sums[...] = total


def tokens_kernel(blocks, sc, tokens, grad_res, gain, *refs):
    pieces = refs[:blocks]
    weights = refs[blocks : blocks + 3]
    grad_tokens, total = refs[blocks + 3 :]
    step, steps = pl.program_id(0), pl.num_programs(0)
    for mask in range(blocks):

        @pl.when(step == mask)
        def _():
            found = nt(pieces[mask][0], weights[0][...])
            found = found + nt(pieces[mask][1], weights[1][...])
            found = found + nt(pieces[mask][2], weights[2][...])
            if mask == 0:
                total[...] = found
            else:
                total[...] += found

    @pl.when(step == steps - 1)
    def _():
        unit, scale = norm_stats(tokens[...].astype(F32))
        grad_tokens[...] = grad_res[...] + norm_back(
            unit, scale, gain[...].astype(F32), total[...]
        )


def index_kernel(blocks, place, continues, scalars, banks):
    my_block, my_group = lax.axis_index("blk"), lax.axis_index("grp")
    chip, core = my_group // 2, my_group % 2
    scalars[0], scalars[1] = my_block, core
    for mask in range(blocks):
        scalars[2 + mask] = place[my_block ^ mask]
    scalars[2 + blocks] = chip % 2
    banks[0], banks[1] = chip, core
    for i in range(continues.shape[0]):
        banks[2 + i] = continues[i]


def indices(place, continues):
    smem = pl.BlockSpec(memory_space=pltpu.SMEM)
    blocks, banks = place.shape[0], continues.shape[0]
    return pl.pallas_call(
        functools.partial(index_kernel, blocks),
        in_specs=[smem, smem],
        out_specs=[smem, smem],
        out_shape=[
            jax.ShapeDtypeStruct((3 + blocks,), jnp.int32),
            jax.ShapeDtypeStruct((2 + banks,), jnp.int32),
        ],
        name="indices",
    )(place, continues)


def cross_kernel(sc, one, two, top, low):
    half = one.shape[1] // 2
    top[...], low[...] = one[:, :half], two[:, half:]


def join_kernel(sc, top, low, out):
    half = top.shape[1]
    out[:, :half], out[:, half:] = top[...], low[...]


def sum_kernel(sc, *refs):
    total = refs[0][...].astype(F32)
    for ref in refs[1:-1]:
        total = total + ref[...].astype(F32)
    refs[-1][...] = total.astype(BF16)


def stack_kernel(sc, *refs):
    for i, ref in enumerate(refs[:-1]):
        refs[-1][i] = ref[...]


def sums_kernel(count, sc, *refs):
    outs = refs[len(refs) - len(refs) // (count + 1) :]
    for i, out in enumerate(outs):
        total = refs[i * count][...].astype(F32)
        for ref in refs[i * count + 1 : (i + 1) * count]:
            total = total + ref[...].astype(F32)
        out[...] = total.astype(BF16)


def exchange_sum_kernel(sc, kept, came, away, held):
    for i in range(held.shape[0]):
        held[i] = (kept[2 * i].astype(F32) + came[2 * i].astype(F32)).astype(BF16)
        away[i] = (kept[2 * i + 1].astype(F32) + came[2 * i + 1].astype(F32)).astype(BF16)


def place_halves(sc, first, second, mine, other):
    low = sc[sc.shape[0] - 1] == 1
    mine[...] = jnp.where(low, second, first)
    other[...] = jnp.where(low, first, second)


def split_sum_kernel(count, sc, *refs):
    totals = []
    for i in range(2):
        total = refs[i * count][...].astype(F32)
        for ref in refs[i * count + 1 : (i + 1) * count]:
            total = total + ref[...].astype(F32)
        totals.append(total.astype(BF16))
    place_halves(sc, *totals, *refs[2 * count :])


def split_stack_kernel(sc, *refs):
    pieces, (mine, other) = refs[:-2], refs[-2:]
    half = len(pieces) // 2
    low = sc[sc.shape[0] - 1] == 1
    for i in range(half):
        first, second = pieces[i][...], pieces[half + i][...]
        mine[i] = jnp.where(low, second, first)
        other[i] = jnp.where(low, first, second)


def cut(chips, tok, width, piece):
    high = max(16, tok // chips)
    across = high * chips // tok
    wide = width // across
    return (
        pl.ds(pl.multiple_of((piece // across) * high, high), high),
        pl.ds(pl.multiple_of((piece % across) * wide, wide), wide),
    )


def piece_shape(chips, tok, width):
    high = max(16, tok // chips)
    return high, tok * width // (chips * high)


def split_kernel(chips, sc, keys, values, came, *outs):
    _, tok, width = keys.shape
    for mask in range(chips):
        rows, columns = cut(chips, tok, width, sc[0] ^ mask)
        own = jnp.where(sc[1] == 0, keys[:, rows, columns], values[:, rows, columns])
        outs[mask][0] = own
        outs[mask][1] = came[:, rows, columns]


def route_kernel(chips, sc, *refs):
    ins, outs, held = refs[:chips], refs[chips : 2 * chips], refs[2 * chips]
    count = ins[0].shape[1]
    per_chip = 2 * count
    for mask in range(chips):
        held[mask] = ins[mask][...]
    for mask in range(chips):
        for i in range(per_chip):
            bank = sc[2 + (sc[0] ^ mask) * per_chip + i]
            outs[mask][i] = held[
                (bank // per_chip) ^ sc[0], ((bank // count) % 2) ^ sc[1], bank % count
            ]


def gather_kernel(chips, sc, *refs):
    ins, (kept, sent) = refs[:chips], refs[chips:]
    count, tok, width = kept.shape
    high, wide = ins[0].shape[1:]
    across = width // wide
    for mask in range(chips):
        _, columns = cut(chips, tok, width, sc[0] ^ mask)
        rows = slice((mask // across) * high, (mask // across + 1) * high)
        for i in range(count):
            kept[i, rows, columns] = ins[mask][sc[1] * count + i]
            sent[i, rows, columns] = ins[mask][(1 - sc[1]) * count + i]


def columns_kernel(blocks, sc, kept, came, *outs):
    part = kept.shape[2] // blocks
    for mask in range(blocks):
        columns = pl.ds(pl.multiple_of((sc[0] ^ mask) * part, part), part)
        mine, other = kept[:, :, columns], came[:, :, columns]
        outs[mask][0] = jnp.where(sc[1] == 0, mine, other)
        outs[mask][1] = jnp.where(sc[1] == 0, other, mine)


def fetch_banks(mem_keys, mem_values, places, groups, my_group, blocks, scalars, meanwhile):
    count, tok, width = mem_keys.shape
    core, chips = my_group % 2, groups // 2
    came = swap(jnp.where(core == 0, mem_values, mem_keys), "grp", 1)
    piece = piece_shape(chips, tok, width)

    def line(parts):
        return [parts[0]] + [swap(parts[m], "grp", 2 * m) for m in range(1, chips)]

    parts = call(
        functools.partial(split_kernel, chips),
        "split_banks",
        (1,),
        [mem_keys, mem_values, came],
        [((2, count) + piece, BF16)] * chips,
        [],
        places,
        10,
    )
    meanwhile(0, parts)
    parts = call(
        functools.partial(route_kernel, chips),
        "route_banks",
        (1,),
        line(parts),
        [((2 * count,) + piece, BF16)] * chips,
        [pltpu.VMEM((chips, 2, count) + piece, BF16)],
        places,
        10,
        meanwhile(1, parts),
    )
    meanwhile(2, parts)
    kept, sent = call(
        functools.partial(gather_kernel, chips),
        "gather_banks",
        (1,),
        line(parts),
        [((count, tok, width), BF16)] * 2,
        [],
        places,
        10,
        meanwhile(3, parts),
    )
    parts = call(
        functools.partial(columns_kernel, blocks),
        "bank_columns",
        (1,),
        [kept, swap(sent, "grp", 1)],
        [((2, count, tok, width // blocks), BF16)] * blocks,
        [],
        scalars,
        10,
    )
    return [parts[0]] + [swap(parts[m], "blk", m) for m in range(1, blocks)]


class Order:
    def __init__(self, scalars, last=()):
        self.scalars, self.last = scalars, last

    def call(self, kernel, name, grid, ins, outs, scratch, mib):
        found = call(
            kernel, name, grid, ins, outs, scratch, self.scalars, mib, tuple(self.last)
        )
        self.last = (found[0],)
        return found

    def small(self, kernel, name, items, outs):
        ins = []
        for item in items:
            if isinstance(item, tuple) and len(item) == 2:
                array, at = item
                block = (None,) + array.shape[1:]
                zeros = (0,) * (array.ndim - 1)
                ins.append((array, block, lambda i, sc, at=at, zeros=zeros: (at,) + zeros))
            else:
                ins.append(item)
        return self.call(kernel, name, (1,), ins, [(o, BF16) for o in outs], [], 8)

    def gate(self, values):
        found = gate(values, self.last)
        self.last = (found[0],)
        return found


def on_device(
    tokens,
    gain_one,
    bias_one,
    w_qkv,
    w_out,
    gain_two,
    bias_two,
    w_in,
    w_down,
    mem_keys,
    mem_values,
    continues,
    block_place,
    cotangent,
):
    seq_count, tok, width = tokens.shape
    hidden_width = w_in.shape[1]
    blocks, groups = lax.axis_size("blk"), lax.axis_size("grp")
    my_block, my_group = lax.axis_index("blk"), lax.axis_index("grp")
    core = my_group % 2
    part = width // blocks
    pairs = part // 128
    halved = pairs > 1
    rows = seq_count * tok
    seg_rows = blocks * tok
    tile = hidden_width // (2 * blocks)
    scalars, banks = indices(block_place, continues)
    gain_one, bias_one = gain_one.reshape(1, width), bias_one.reshape(1, width)
    gain_two, bias_two = gain_two.reshape(1, width), bias_two.reshape(1, width)
    flat = tokens.reshape(rows, width)
    cot = cotangent.reshape(rows, width)

    def gather_rows(values, order):
        if blocks != 4:
            return [values] + [swap(values, "blk", mask) for mask in range(1, blocks)]
        one, two = swap(values, "blk", 1), swap(values, "blk", 2)
        half = (2, rows // 2, width)
        top, low = order.call(
            cross_kernel, "cross", (1,), [one, two], [(half, BF16)] * 2, [], 8
        )
        top, low = swap(top, "blk", 2), swap(low, "blk", 1)
        return [values, one, two, (top, low)]

    def head_weights(j, at=None):
        def index(i, sc):
            return (0, j * blocks + (sc[0] ^ i if at is None else sc[0]))

        return (w_qkv, (width, part), index)

    def heads_block(j):
        return (1, tok, 128), lambda s, p, sc: (s, 0, j * pairs + p)

    seg_block = (1, seg_rows, 128), lambda s, p, sc: (s, 0, p)
    seg_shape = (seq_count, seg_rows, part)
    tok_block = (1, tok, 128), lambda s, p, sc: (s, 0, p)
    mem_block = (2, 1, tok, 128), lambda s, p, sc: (0, s, 0, p)
    early = {}

    rows_block = (None, rows, width)

    def meanwhile(stage, parts):
        if stage == 0:
            both = call(
                stack_kernel,
                "stack",
                (1,),
                [flat, cot],
                [((2, rows, width), BF16)],
                [],
                scalars,
                8,
                (parts[0],),
            )
            early["both"] = both[0]
            return ()
        if stage == 1:
            return (early["both"],)
        if stage == 3:
            return (early["own"][0],)
        order = Order(scalars, (parts[0],))
        pieces = early["pieces"] = gather_rows(early["both"], order)
        normed, qkv = [], []
        for mask, piece in enumerate(pieces):
            if isinstance(piece, tuple):
                (piece,) = order.call(
                    join_kernel, "join", (1,), piece, [(early["both"].shape, BF16)], [], 8
                )
                pieces[mask] = piece
            found = order.call(
                project_kernel,
                "project",
                (1,),
                [(piece, rows_block, lambda i, sc: (0, 0, 0)), gain_one, bias_one]
                + [head_weights(j, 0) for j in range(3)],
                [((rows, width), BF16), ((rows, 3 * part), BF16)],
                [],
                12,
            )
            normed.append(found[0])
            qkv.append(found[1].reshape(seq_count, tok, 3 * part))
        early["normed"] = normed
        early["own"] = order.call(
            functools.partial(own_kernel, blocks),
            "own_keys",
            (seq_count, pairs),
            [(qkv[m],) + heads_block(j) for m in range(blocks) for j in range(3)],
            [(seg_shape, BF16) + seg_block] * 3 + [(seg_shape, F32) + seg_block] * 2,
            [pltpu.VMEM((3, blocks, tok, 128), BF16)],
            16,
        )
        return ()

    mem = fetch_banks(
        mem_keys, mem_values, banks, groups, my_group, blocks, scalars, meanwhile
    )
    queries, keys, values, partial, counts = early["own"]
    normed = early["normed"]
    found = call(
        functools.partial(cached_kernel, blocks),
        "cached_keys",
        (seq_count, pairs),
        [(a,) + seg_block for a in (queries, keys, partial, counts)]
        + [(a,) + mem_block for a in mem],
        [(seg_shape, F32) + seg_block] * 2
        + [((seq_count, tok, part), BF16) + tok_block] * blocks,
        [pltpu.VMEM((2, seg_rows, 128), BF16), pltpu.VMEM((blocks, tok, 128), BF16)],
        scalars,
        16,
    )
    attended_f, counts = found[:2]
    attended = [found[2]] + [swap(found[2 + m], "blk", m) for m in range(1, blocks)]
    attended = [a.reshape(rows, part) for a in attended]

    def ff_tile(j, sc):
        return 2 * (sc[0] ^ (j // 2)) + j % 2

    base = blocks * tile
    found = call(
        functools.partial(feed_kernel, blocks),
        "feed",
        (2 * blocks,),
        attended
        + [flat, cot, w_out, gain_two, bias_two]
        + [
            (w_in, (width, tile), lambda j, sc: (0, ff_tile(j, sc))),
            (w_down, (tile, width), lambda j, sc: (ff_tile(j, sc), 0)),
        ],
        [
            ((rows, width), BF16),
            ((rows, width), F32),
            ((rows, base), BF16),
            ((rows, base + 2 * width + width // 2), BF16),
            ((rows, width), BF16),
            ((rows, width), BF16),
            ((rows, width // 2), BF16),
            ((2, width), F32),
        ]
        + [((rows, 2 * tile), BF16)] * blocks
        + [((rows, part), BF16)] * blocks,
        [
            pltpu.VMEM((rows, width), F32),
            pltpu.VMEM((rows, width), BF16),
            pltpu.VMEM((rows, width), F32),
            pltpu.VMEM((rows, width), F32),
        ],
        scalars,
        28,
    )
    mixed, grad_res, inner_keep, to_core, normed_two, att_all, branch, sums_two = found[:8]
    acts, grad_att = found[8 : 8 + blocks], found[8 + blocks :]
    grad_att = [grad_att[0]] + [swap(grad_att[m], "blk", m) for m in range(1, blocks)]
    grad_att = [g.reshape(seq_count, tok, part) for g in grad_att]
    core_came = swap(to_core, "grp", 1)
    order = Order(scalars, tuple(grad_att[1:]) + (core_came,))
    acts = [acts[0]] + [swap(a, "blk", m + 1) for m, a in enumerate(order.gate(acts[1:]))]

    top = blocks // 2

    def of_mask(shape, mask, wanted):
        def index(m, sc):
            if mask == 1:
                return (m >> 1, 0, 0)
            return (jnp.maximum(m - top, 0) if wanted else jnp.minimum(m, top - 1), 0, 0)

        return ((top,) + shape, BF16, (1,) + shape, index)

    def columns(start):
        return lambda m, sc: (0, start // part + (sc[0] ^ m))

    in_rows = part + part * width // (2 * base)
    in_shape = (in_rows // 2, base)
    bits = [1 << i for i in range(blocks.bit_length() - 1)]
    results = {}
    paths = {}

    def go(names):
        for name in names:
            if name not in results:
                try:
                    next(paths[name])
                except StopIteration as stop:
                    results[name] = stop.value

    def total(*items):
        first = items[0]
        if not isinstance(first, tuple):
            shape = first.shape
        elif len(first) == 2:
            shape = first[0].shape[1:]
        else:
            shape = first[1]
        return order.small(sum_kernel, "sum", items, [shape])[0]

    def sum_chips(mine, other):
        held = total(mine, swap(other, "grp", 2))
        for bit in range(2, groups.bit_length() - 1):
            came = swap(held, "grp", 1 << bit)
            yield
            held = total(held, came)
        other = swap(held, "grp", 2)
        core_held = swap(held, "grp", 1)
        yield
        return held, other, core_held, swap(other, "grp", 1)

    found = order.call(
        functools.partial(attention_back_kernel, blocks),
        "attention_back",
        (seq_count, pairs),
        [(a,) + seg_block for a in (queries, keys, values, attended_f, counts)]
        + [(a,) + mem_block for a in mem]
        + [(a,) + tok_block for a in grad_att],
        [
            (
                (3, seq_count, tok, part),
                BF16,
                (3, 1, tok, 128),
                lambda s, p, sc: (0, s, 0, p),
            )
        ]
        * blocks,
        [
            pltpu.VMEM((2, seg_rows, 128), BF16),
            pltpu.VMEM((blocks, tok, 128), BF16),
            pltpu.VMEM((3, blocks, tok, 128), BF16),
        ],
        24,
    )
    own_grads = [g.reshape(3, rows, part) for g in found]

    found = order.call(
        functools.partial(in_kernel, blocks),
        "grad_in",
        (blocks,),
        [
            (normed_two, (rows, part), columns(0)),
            (core_came, (rows, part), columns(base)),
            inner_keep,
            (core_came, (rows, base), lambda m, sc: (0, 0)),
            (att_all, (rows, part), columns(0)),
            (core_came, (rows, part), columns(base + width)),
            branch,
            (core_came, (rows, width // 2), lambda m, sc: (0, 2 * (base + 2 * width) // width)),
        ],
        [of_mask(in_shape, mask, sent) for mask in (1, top) for sent in (True, False)],
        [pltpu.VMEM((in_rows, base), BF16)],
        28,
    )
    in_sent, in_kept = (found[0], found[2]), (found[1], found[3])

    def in_path():
        firsts, rests = (1, top), (bits[1:], bits[:-1][::-1])
        masks = [[m for m in range(blocks) if not m & bit] for bit in firsts]
        came = [swap(sent, "blk", bit) for sent, bit in zip(in_sent, firsts)]
        yield
        terms = [
            {m: [(in_kept[h], i), (came[h], i)] for i, m in enumerate(masks[h])} for h in range(2)
        ]
        for bit in range(len(bits) - 1):
            away = [[m for m in masks[h] if m & rests[h][bit]] for h in range(2)]
            masks = [[m for m in masks[h] if not m & rests[h][bit]] for h in range(2)]
            items = [v for h in range(2) for m in away[h] for v in terms[h][m]]
            count = len(away[0])
            sent = order.small(
                functools.partial(sums_kernel, len(items) // (2 * count)),
                "sums",
                items,
                [in_shape] * (2 * count),
            )
            for h in range(2):
                for i, m in enumerate(masks[h]):
                    came = swap(sent[h * count + i], "blk", rests[h][bit])
                    terms[h][m] = terms[h][m] + [came]
            yield
        items = [v for h in range(2) for v in terms[h][0]]
        mine, other = order.small(
            functools.partial(split_sum_kernel, len(items) // 2), "split", items, [in_shape] * 2
        )
        yield
        return (yield from sum_chips(mine, other))

    paths["i"] = in_path()
    go("i")

    found = order.call(
        functools.partial(down_kernel, blocks),
        "grad_down",
        (2,),
        [
            (a, (rows, tile), lambda i, sc: (0, jnp.where(i == 0, 1 - sc[1], sc[1])))
            for a in acts
        ]
        + [(p, rows_block, lambda i, sc: (1, 0, 0)) for p in early["pieces"]],
        [((tile, width), BF16)] * 2,
        [],
        28,
    )
    down_kept, down_came = found[1], swap(found[0], "grp", 1)

    def down_path():
        block = (tile // 2, width)
        items = [
            (v, block, lambda i, sc, h=h: (h, 0)) for h in range(2) for v in (down_kept, down_came)
        ]
        mine, other = order.small(
            functools.partial(split_sum_kernel, 2), "split", items, [block] * 2
        )
        yield
        return (yield from sum_chips(mine, other))

    paths["d"] = down_path()

    share = part // 2 if halved else part
    share_block = (1, share + 16, 3 * part), lambda m, sc: (m, 0, 0)

    def own_weights(j):
        return (w_qkv, (part, part), lambda m, sc: (sc[0] ^ m, j * blocks + sc[0]))

    found = order.call(
        functools.partial(qkv_kernel, blocks, halved),
        "grad_qkv",
        (blocks,),
        [(n, (rows, part), columns(0)) for n in normed]
        + own_grads
        + [own_weights(j) for j in range(3)]
        + [(gain_one, (1, part), columns(0)), (bias_one, (1, part), columns(0))]
        + [(sums_two, (2, part), columns(0))],
        [((blocks, share + 16, 3 * part), BF16) + share_block] * (2 if halved else 1),
        [],
        28,
    )
    qkv_sent, qkv_kept = found[0], found[-1]

    def qkv_path():
        came = swap(qkv_sent, "grp", 1)
        yield
        shape = qkv_kept.shape[1:]
        half = (blocks // 2,) + shape
        away, kept = order.small(
            exchange_sum_kernel, "sums", [qkv_kept, came], [half] * 2
        )
        came = swap(away, "blk", 1)
        yield
        held = {2 * i: [(kept, i), (came, i)] for i in range(blocks // 2)}
        for bit in bits[1:]:
            masks = [m for m in sorted(held) if m & bit]
            items = [v for m in masks for v in held[m]]
            (away,) = order.small(stack_kernel, "stack", items, [(len(items),) + shape])
            came = swap(away, "blk", bit)
            yield
            held = {m: v for m, v in held.items() if not m & bit}
            count = len(held[0])
            for i, m in enumerate(sorted(held)):
                held[m] = held[m] + [(came, i * count + k) for k in range(count)]
        mine, other = order.small(split_stack_kernel, "split", held[0], [half] * 2)
        yield
        return (yield from sum_chips(mine, other))

    paths["q"] = qkv_path()
    go("q")
    def tokens_path():
        held = order.gate(own_grads[1:])
        grads = [own_grads[0]] + [swap(held[m], "blk", m + 1) for m in range(blocks - 1)]
        yield
        return order.call(
            functools.partial(tokens_kernel, blocks),
            "tokens_back",
            (blocks,),
            [flat, grad_res, gain_one] + grads + [head_weights(j) for j in range(3)],
            [((rows, width), F32)],
            [pltpu.VMEM((rows, width), F32)],
            24,
        )

    def down_finish():
        return order.call(
            down_finish_kernel,
            "down_finish",
            (4,),
            list(results["d"]),
            [((2 * tile, width), F32, (tile // 2, width), lambda i, sc: (i, 0))],
            [],
            16,
        )
        yield

    def in_finish():
        return order.call(
            functools.partial(in_finish_kernel, blocks),
            "in_finish",
            (2 * blocks,),
            list(results["i"]),
            [
                ((part, hidden_width), F32, (part, tile), lambda j, sc: (0, j)),
                ((part, width), F32, (part, width // 2), lambda j, sc: (0, jnp.minimum(j, 1))),
            ],
            [pltpu.VMEM((2, in_rows, base), BF16)],
            16,
        )
        yield

    def qkv_finish():
        high = share + 16
        return order.call(
            functools.partial(qkv_finish_kernel, blocks, halved),
            "qkv_finish",
            (2 if halved else 1, 3),
            [(a, (blocks // 2, high, part), lambda k, i, sc: (0, 0, i)) for a in results["q"]],
            [
                ((part, 3 * width), F32, (share, width), lambda k, i, sc: (k, i)),
                ((8, part), F32),
            ],
            [pltpu.VMEM((2, blocks, high, part), F32)],
            16,
        )
        yield

    paths["t"] = tokens_path()
    paths["F"], paths["G"], paths["H"] = down_finish(), qkv_finish(), in_finish()
    if groups == 8 and blocks == 4:
        go("diqdiqdiqtqdFitiqHqG")
    while len(results) < len(paths):
        for name in sorted(paths):
            if name.islower() or "d" in results and "i" in results and "q" in results:
                go(name)
    (grad_down,) = results["F"]
    grad_qkv, sums = results["G"]
    grad_in, grad_out = results["H"]
    (grad_tokens,) = results["t"]
    return (
        mixed.reshape(tokens.shape),
        grad_tokens.reshape(tokens.shape),
        sums[0],
        sums[1],
        grad_qkv,
        grad_out,
        sums[2],
        sums[3],
        grad_in,
        grad_down,
    )


def solution(mesh):
    rows = P("grp", "blk", None)
    in_specs = (rows,) + (P(),) * 8 + (rows, rows, P(), P(), rows)
    out_specs = (rows, rows) + (P("blk"),) * 2 + (P("blk", None),) * 2
    out_specs = out_specs + (P("blk"),) * 2 + (P("blk", None),) * 2
    return jax.shard_map(
        on_device, mesh=mesh, in_specs=in_specs, out_specs=out_specs, check_vma=False
    )
```

```python
import functools

import jax
import jax.numpy as jnp
from jax import lax
from jax.experimental import pallas as pl
from jax.experimental.pallas import tpu as pltpu
from jax.sharding import PartitionSpec as P

HEADS = 16
F32 = jnp.float32
BF16 = jnp.bfloat16
MIB = 1 << 20
EPS = 1e-05
FAR = -1e30
GELU_A = 0.7978845608028654
GELU_B = 0.044715


def swap(values, axis, mask):
    size = lax.axis_size(axis)
    return lax.ppermute(values, axis, [(i, i ^ mask) for i in range(size)])


def pick(values, index, dim=0):
    return lax.dynamic_index_in_dim(values, index, dim, keepdims=False)


def nn(left, right):
    return lax.dot_general(left, right, (((1,), (0,)), ((), ())), preferred_element_type=F32)


def nt(left, right):
    return lax.dot_general(left, right, (((1,), (1,)), ((), ())), preferred_element_type=F32)


def tn(left, right):
    return lax.dot_general(left, right, (((0,), (0,)), ((), ())), preferred_element_type=F32)


def params(mib):
    return pltpu.CompilerParams(vmem_limit_bytes=mib * MIB)


ANYWHERE = pl.BlockSpec(memory_space=pl.ANY)
EVERY = range(100)
TOKEN = (8, 128)
COSTS = {'': (3000000000, 10000000000), 'grad_in': (10000000000, 1000000), 'grad_qkv': (10000000000, 1000000), 'attention_back': (10000000000, 1000000), 'feed': (100000000000, 1000000), 'tokens_back': (100000000000, 1000000), 'project': (1000000000, 1000000000), 'own_keys': (1000000000, 1000000000), 'cached_keys': (1000000000, 1000000000), 'bank_columns': (1000000000, 1000000000), 'cross': (1000000000, 1000000000), 'join': (1000000000, 1000000000), 'copy': (1000000000, 1000000000), 'choose_banks': (1000000000, 1000000000), 'grad_down': (3000000000, 10000000000)}
PLAN = "ABNWYdqidiqdqtitiqFtHqG"


def cost_of(name):
    flops, size = COSTS.get(name, COSTS[""])
    return pl.CostEstimate(flops=flops, bytes_accessed=size, transcendentals=0)


OUT_HBM = {
    "project": range(0, 20, 2),
    "own_keys": (2,),
    "cached_keys": (0, 1),
    "feed": (0, 1, 2, 4, 5, 6, 8, 9, 10, 11, 12, 13, 14, 15),
}
IN_HBM = {
    "bank_columns": (0, 1),
    "rows_stack": (0, 1),
    "project": range(2, 10),
    "attention_back": EVERY,
    "grad_qkv": (0, 1, 2, 3),
    "grad_out": EVERY,
}


def call(kernel, name, grid, ins, outs, scratch, scalars, mib, tokens=()):
    def whole(shape):
        return pl.BlockSpec(shape, lambda *_: (0,) * len(shape))

    in_specs, arrays = [], []
    for item in ins:
        if isinstance(item, tuple):
            arrays.append(item[0])
            in_specs.append(pl.BlockSpec(item[1], item[2]))
        else:
            arrays.append(item)
            in_specs.append(whole(item.shape))
    out_shapes, out_specs = [], []
    for item in outs:
        out_shapes.append(jax.ShapeDtypeStruct(item[0], item[1]))
        out_specs.append(whole(item[0]) if len(item) == 2 else pl.BlockSpec(item[2], item[3]))
    count = len(arrays)

    pinned = IN_HBM.get(name, ())
    arrays = [
        pltpu.with_memory_space_constraint(a, pltpu.HBM) if i in pinned else a
        for i, a in enumerate(arrays)
    ]
    pinned = OUT_HBM.get(name, ())
    out_shapes = [
        pltpu.HBM(o.shape, o.dtype) if i in pinned else o for i, o in enumerate(out_shapes)
    ]

    out_shapes = out_shapes + [jax.ShapeDtypeStruct(TOKEN, jnp.int32)]
    out_specs = out_specs + [whole(TOKEN)]
    last = count + len(tokens) + len(outs)

    def body(sc, *refs):
        kernel(sc, *refs[:count], *refs[count + len(tokens) : last], *refs[last + 1 :])
        refs[last][...] = jnp.zeros(TOKEN, jnp.int32)

    spec = pltpu.PrefetchScalarGridSpec(
        num_scalar_prefetch=1,
        grid=grid,
        in_specs=in_specs + [ANYWHERE] * len(tokens),
        out_specs=out_specs,
        scratch_shapes=scratch,
    )
    return pl.pallas_call(
        body,
        grid_spec=spec,
        out_shape=out_shapes,
        compiler_params=params(mib),
        cost_estimate=cost_of(name),
        name=name,
    )(scalars, *arrays, *tokens)


def corner(value):
    block = (1,) * (value.ndim - 2) + (min(16, value.shape[-2]), 128)
    return pl.BlockSpec(block, lambda *_: (0,) * value.ndim)


def gate(values, tokens):
    count = len(values)

    def body(*refs):
        refs[-1][...] = jnp.zeros(TOKEN, jnp.int32)

    return pl.pallas_call(
        body,
        grid=(1,),
        in_specs=[ANYWHERE] * count + [corner(t) for t in tokens],
        out_specs=[ANYWHERE] * count + [pl.BlockSpec(memory_space=pltpu.VMEM)],
        out_shape=[jax.ShapeDtypeStruct(v.shape, v.dtype) for v in values]
        + [jax.ShapeDtypeStruct(TOKEN, jnp.int32)],
        input_output_aliases={i: i for i in range(count)},
        cost_estimate=cost_of("gate"),
        name="gate",
    )(*values, *tokens)


def norm_stats(values):
    average = jnp.mean(values, -1, keepdims=True)
    centred = values - average
    scale = lax.rsqrt(jnp.mean(centred * centred, -1, keepdims=True) + EPS)
    return centred * scale, scale


def norm_back(unit, scale, gain, grad):
    scaled = grad * gain
    mean_one = jnp.mean(scaled, -1, keepdims=True)
    mean_two = jnp.mean(scaled * unit, -1, keepdims=True)
    return scale * (scaled - mean_one - unit * mean_two)


def project_kernel(count, sc, *refs):
    rows, gains, weights = refs[:count], refs[count], refs[count + 1 : count + 4]
    outs = refs[count + 4 :]
    gain, bias = gains[0:1].astype(F32), gains[1:2].astype(F32)
    part = weights[0].shape[1]
    for i in range(count):
        unit, _ = norm_stats(rows[i][...].astype(F32))
        low = (unit * gain + bias).astype(BF16)
        outs[2 * i][...] = low
        for j, weight in enumerate(weights):
            outs[2 * i + 1][:, j * part : (j + 1) * part] = nn(low, weight[...]).astype(BF16)


def lane_masks():
    lane = lax.broadcasted_iota(jnp.int32, (1, 128), 1)
    return [lane < 64, lane >= 64]


def of_head(values, mask):
    return jnp.where(mask, values, jnp.zeros_like(values))


def by_head(first, second, masks):
    return jnp.where(masks[0], first, second)


BLOCK = 256


def own_kernel(blocks, sc, *refs):
    ins, outs = refs[: 3 * blocks], refs[3 * blocks :]
    q_out, k_out, v_out, t_out, l_out = outs[:5]
    held = outs[5]
    tok = ins[0].shape[1]
    scale = 64 ** (-0.5)
    for mask in range(blocks):
        place = sc[2 + mask]
        for i in range(3):
            values = ins[3 * mask + i][0]
            if i == 0:
                values = (values.astype(F32) * scale).astype(BF16)
            held[i, place] = values
    rows = blocks * tok
    queries = held[0].reshape(rows, 128)
    keys = held[1].reshape(rows, 128)
    values = held[2].reshape(rows, 128)
    q_out[0], k_out[0], v_out[0] = queries, keys, values
    masks = lane_masks()
    size = min(BLOCK, rows)
    lower = lax.broadcasted_iota(jnp.int32, (size, size), 0) >= lax.broadcasted_iota(
        jnp.int32, (size, size), 1
    )
    product = queries.astype(F32) * keys.astype(F32)
    head_keys = [of_head(keys, m) for m in masks]
    head_values = [of_head(values, m) for m in masks]
    selfs = [jnp.sum(of_head(product, m), -1, keepdims=True) for m in masks]
    for i in range(rows // size):
        here = slice(i * size, (i + 1) * size)
        total, sums = jnp.zeros((size, 128), F32), []
        for h in range(2):
            count = jnp.zeros((size, 1), F32)
            for j in range(i + 1):
                there = slice(j * size, (j + 1) * size)
                scores = nt(queries[here], head_keys[h][there]) - selfs[h][here]
                if i == j:
                    scores = jnp.where(lower, scores, FAR)
                weights = jnp.exp(scores)
                count = count + jnp.sum(weights, -1, keepdims=True)
                total = total + nn(weights.astype(BF16), head_values[h][there])
            sums.append(count)
        t_out[0, here] = total
        l_out[0, here] = by_head(sums[0], sums[1], masks)


def load_cached(pieces, mem):
    tok = pieces[0].shape[2]
    for mask, piece in enumerate(pieces):
        mem[:, mask * tok : (mask + 1) * tok] = piece[:, 0]


def cached_kernel(blocks, sc, *refs):
    q_in, k_in, t_in, l_in = refs[:4]
    pieces = refs[4 : 4 + blocks]
    att_out, l_out = refs[4 + blocks : 6 + blocks]
    sends = refs[6 + blocks : 6 + 2 * blocks]
    mem, low = refs[6 + 2 * blocks :]
    load_cached(pieces, mem)
    tok = pieces[0].shape[2]
    queries, keys = q_in[0], k_in[0]
    rows = queries.shape[0]
    masks = lane_masks()
    product = queries.astype(F32) * keys.astype(F32)
    selfs = [jnp.sum(of_head(product, m), -1, keepdims=True) for m in masks]
    head_keys = [of_head(mem[0], m) for m in masks]
    head_values = [of_head(mem[1], m) for m in masks]
    size = min(BLOCK, rows)
    for i in range(rows // size):
        here = slice(i * size, (i + 1) * size)
        total, sums = t_in[0, here], []
        for h in range(2):
            weights = jnp.exp(nt(queries[here], head_keys[h]) - selfs[h][here])
            sums.append(jnp.sum(weights, -1, keepdims=True))
            total = total + nn(weights.astype(BF16), head_values[h])
        count = l_in[0, here] + by_head(sums[0], sums[1], masks)
        attended = total / count
        att_out[0, here] = attended
        l_out[0, here] = count
        low[i * size // tok : (i + 1) * size // tok] = attended.astype(BF16).reshape(
            size // tok, tok, 128
        )
    for mask in range(blocks):
        sends[mask][0] = low[sc[2 + mask]]


def attention_back_kernel(blocks, sc, *refs):
    q_in, k_in, v_in, att_in, l_in = refs[:5]
    pieces = refs[5 : 5 + blocks]
    grads = refs[5 + blocks : 5 + 2 * blocks]
    sends = refs[5 + 2 * blocks : 5 + 3 * blocks]
    mem, came, low = refs[5 + 3 * blocks :]
    load_cached(pieces, mem)
    tok = pieces[0].shape[2]
    for mask in range(blocks):
        came[sc[2 + mask]] = grads[mask][0]
    queries, keys, values = q_in[0], k_in[0], v_in[0]
    rows = queries.shape[0]
    scale = 64 ** (-0.5)
    masks = lane_masks()
    grad = came[...].reshape(rows, 128).astype(F32)
    count = l_in[0]
    scaled_f = grad / count
    scaled = scaled_f.astype(BF16)
    weighed = grad * att_in[0] / count
    product = queries.astype(F32) * keys.astype(F32)
    selfs = [jnp.sum(of_head(product, m), -1, keepdims=True) for m in masks]
    fixes = [jnp.sum(of_head(weighed, m), -1, keepdims=True) for m in masks]
    own_k = [of_head(keys, m) for m in masks]
    own_v = [of_head(values, m) for m in masks]
    mem_k = [of_head(mem[0], m) for m in masks]
    mem_v = [of_head(mem[1], m) for m in masks]
    q_t = [of_head(queries, m).astype(F32).T.astype(BF16) for m in masks]
    s_t = [of_head(scaled, m).astype(F32).T.astype(BF16) for m in masks]
    size = min(BLOCK, rows)
    lower = lax.broadcasted_iota(jnp.int32, (size, size), 0) >= lax.broadcasted_iota(
        jnp.int32, (size, size), 1
    )
    steps = rows // size
    keys_t = [jnp.zeros((128, size), F32) for _ in range(steps)]
    values_t = [jnp.zeros((128, size), F32) for _ in range(steps)]
    diags = []
    for i in range(steps):
        here = slice(i * size, (i + 1) * size)
        total, sums = jnp.zeros((size, 128), F32), []
        for h in range(2):
            diag = jnp.zeros((size, 1), F32)
            for j in range(i + 1):
                there = slice(j * size, (j + 1) * size)
                scores = nt(queries[here], own_k[h][there]) - selfs[h][here]
                if i == j:
                    scores = jnp.where(lower, scores, FAR)
                weights = jnp.exp(scores)
                change = weights * (nt(scaled[here], own_v[h][there]) - fixes[h][here])
                diag = diag + jnp.sum(change, -1, keepdims=True)
                small = change.astype(BF16)
                total = total + nn(small, own_k[h][there])
                keys_t[j] = keys_t[j] + nn(q_t[h][:, here], small)
                values_t[j] = values_t[j] + nn(s_t[h][:, here], weights.astype(BF16))
            weights = jnp.exp(nt(queries[here], mem_k[h]) - selfs[h][here])
            change = weights * (nt(scaled[here], mem_v[h]) - fixes[h][here])
            diag = diag + jnp.sum(change, -1, keepdims=True)
            total = total + nn(change.astype(BF16), mem_k[h])
            sums.append(diag)
        diag = by_head(sums[0], sums[1], masks)
        diags.append(diag)
        grad_q = scale * (total - diag * keys[here].astype(F32))
        low[0, i * size // tok : (i + 1) * size // tok] = grad_q.astype(BF16).reshape(
            size // tok, tok, 128
        )
    for j in range(steps):
        there = slice(j * size, (j + 1) * size)
        grad_k = keys_t[j].T - diags[j] * queries[there].astype(F32)
        blocks_here = slice(j * size // tok, (j + 1) * size // tok)
        low[1, blocks_here] = grad_k.astype(BF16).reshape(size // tok, tok, 128)
        low[2, blocks_here] = values_t[j].T.astype(BF16).reshape(size // tok, tok, 128)
    for mask in range(blocks):
        for i in range(3):
            sends[mask][i, 0] = low[i, sc[2 + mask]]


def feed_kernel(blocks, sc, *refs):
    att_in = refs[:blocks]
    rest = refs[blocks:]
    tokens, cot, w_out, gains, w_in, w_down = rest[:6]
    rest = rest[6:]
    gain, bias = gains[2:3].astype(F32), gains[3:4].astype(F32)
    mixed, grad_res, inner_keep, to_core, normed_out, att_out, branch_keep, sums = rest[:8]
    acts = rest[8 : 8 + blocks]
    grad_att = rest[8 + blocks : 8 + 2 * blocks]
    residual, normed, total, back = rest[8 + 2 * blocks :]
    step, steps = pl.program_id(0), pl.num_programs(0)
    part, width, tile = att_in[0].shape[1], tokens.shape[1], w_in.shape[1]
    my_block, core = sc[0], sc[1]
    base = blocks * tile

    def out_rows(mask):
        return pl.ds(pl.multiple_of((my_block ^ mask) * part, part), part)

    @pl.when(step == 0)
    def _():
        branch = tokens[...].astype(F32)
        for mask in range(blocks):
            branch = branch + nn(att_in[mask][...], w_out[out_rows(mask), :])
            att_out[:, out_rows(mask)] = att_in[mask][...]
        to_core[:, base + width : base + 2 * width] = att_out[...]
        residual[...] = branch
        unit, _ = norm_stats(branch)
        low = (unit * gain + bias).astype(BF16)
        normed[...] = low
        normed_out[...] = low
        to_core[:, base : base + width] = low

    inner = nn(normed[...], w_in[...])
    square = inner * inner
    bend = jnp.tanh(GELU_A * inner * (1.0 + GELU_B * square))
    half = 0.5 * (1.0 + bend)
    act = (inner * half).astype(BF16)
    slope = half + (0.5 * GELU_A) * inner * (1.0 - bend * bend) * (1.0 + 3.0 * GELU_B * square)
    grad = (slope * nt(cot[...], w_down[...])).astype(BF16)
    into = nn(act, w_down[...])
    away = nt(grad, w_in[...])

    @pl.when(step == 0)
    def _():
        total[...] = into
        back[...] = away

    @pl.when(step > 0)
    def _():
        total[...] += into
        back[...] += away

    for j in range(2 * blocks):

        @pl.when(step == j)
        def _():
            acts[j // 2][:, (j % 2) * tile : (j % 2 + 1) * tile] = act

    columns = pl.ds(pl.multiple_of((my_block ^ (step // 2)) * tile, tile), tile)

    @pl.when(step % 2 == core)
    def _():
        inner_keep[:, columns] = grad

    @pl.when(step % 2 != core)
    def _():
        to_core[:, columns] = grad

    @pl.when(step == steps - 1)
    def _():
        here = residual[...]
        mixed[...] = (here + total[...]).astype(BF16)
        unit, scale = norm_stats(here)
        away = back[...]
        sums[0:1] = jnp.sum(away * unit, 0, keepdims=True)
        sums[1:2] = jnp.sum(away, 0, keepdims=True)
        found = cot[...].astype(F32) + norm_back(unit, scale, gain, away)
        grad_res[...] = found
        low = found.astype(BF16)
        left, right = low[:, : width // 2], low[:, width // 2 :]
        branch_keep[...] = jnp.where(core == 0, left, right)
        to_core[:, base + 2 * width :] = jnp.where(core == 0, right, left)
        for mask in range(blocks):
            grad_att[mask][...] = nt(low, w_out[out_rows(mask), :]).astype(BF16)


def in_kernel(blocks, sc, *refs):
    (normed, normed_two, inner, inner_two, att, att_two, branch, branch_two) = refs[:8]
    outs, held = refs[8:12], refs[12]
    part = normed.shape[1]
    tile = inner.shape[1] // blocks
    for q in range(blocks):
        columns = slice(q * tile, (q + 1) * tile)
        found = tn(normed[...], inner[:, columns]) + tn(normed_two[...], inner_two[:, columns])
        held[:part, columns] = found.astype(BF16)
    out = (tn(att[...], branch[...]) + tn(att_two[...], branch_two[...])).astype(BF16)
    width = out.shape[1]
    cuts = held.shape[1] // width
    high = part // cuts
    for i in range(cuts):
        held[part : part + high, i * width : (i + 1) * width] = out[i * high : (i + 1) * high]
    step = pl.program_id(0)
    half = held.shape[0] // 2
    for i, bit in enumerate((1, blocks // 2)):

        @pl.when((step & bit) != 0)
        def _():
            outs[2 * i][0] = held[i * half : (i + 1) * half]

        @pl.when((step & bit) == 0)
        def _():
            outs[2 * i + 1][0] = held[i * half : (i + 1) * half]


def down_kernel(blocks, sc, *refs):
    acts, cots, (sent, kept) = refs[:blocks], refs[blocks : 2 * blocks], refs[2 * blocks :]
    total = tn(acts[0][...], cots[0][...])
    for mask in range(1, blocks):
        total = total + tn(acts[mask][...], cots[mask][...])
    low = total.astype(BF16)

    @pl.when(pl.program_id(0) == 0)
    def _():
        sent[...] = low

    @pl.when(pl.program_id(0) == 1)
    def _():
        kept[...] = low


def qkv_kernel(blocks, halved, sc, *refs):
    normed, grads = refs[:blocks], refs[blocks : 2 * blocks]
    weights = refs[2 * blocks : 2 * blocks + 3]
    gains, sums_two = refs[2 * blocks + 3 : 2 * blocks + 5]
    outs = refs[2 * blocks + 5 :]
    part = grads[0].shape[2]
    share = part // 2 if halved else part
    ahead = jnp.zeros((part, 1), F32)
    plain = jnp.zeros((part, 1), F32)
    for j in range(3):
        total = tn(normed[0][...], grads[0][j])
        count = jnp.sum(grads[0][j].astype(F32), 0, keepdims=True)
        for mask in range(1, blocks):
            total = total + tn(normed[mask][...], grads[mask][j])
            count = count + jnp.sum(grads[mask][j].astype(F32), 0, keepdims=True)
        weight = weights[j][...].astype(F32)
        ahead = ahead + jnp.sum(weight * total, -1, keepdims=True)
        plain = plain + jnp.sum(weight * count, -1, keepdims=True)
        low = total.astype(BF16)
        columns = slice(j * part, (j + 1) * part)
        if halved:
            first, second = low[:share], low[share:]
            outs[0][0, :share, columns] = jnp.where(sc[1] == 0, second, first)
            outs[1][0, :share, columns] = jnp.where(sc[1] == 0, first, second)
        else:
            outs[0][0, :share, columns] = low
    flat = [jnp.broadcast_to(v, (part, 128)).T[0:1] for v in (ahead, plain)]
    shift = (flat[0] - gains[1:2].astype(F32) * flat[1]) / gains[0:1].astype(F32)
    row = lax.broadcasted_iota(jnp.int32, (16, part), 0)
    vectors = jnp.zeros((16, part), F32)
    for i, vector in enumerate((shift, flat[1], sums_two[0:1], sums_two[1:2])):
        vectors = jnp.where(row == i, vector, vectors)
    vectors = vectors.astype(BF16)
    for out in outs:
        out[0, share:] = jnp.zeros((16, 3 * part), BF16)
    outs[-1][0, share:, :part] = vectors


def down_finish_kernel(sc, *refs):
    parts, grad_down = refs[:4], refs[4]
    core, low = sc[1], sc[sc.shape[0] - 1]
    for i in range(4):
        wanted = 2 * (core ^ (i // 2)) + (low ^ (i % 2))

        @pl.when(pl.program_id(0) == wanted)
        def _():
            grad_down[...] = parts[i][...].astype(F32)


def in_finish_kernel(blocks, sc, *refs):
    parts, (grad_in, grad_out, held) = refs[:4], refs[4:]
    step = pl.program_id(0)
    core, low = sc[1], sc[sc.shape[0] - 1]
    half, columns = parts[0].shape
    part, tile = grad_in.shape
    width = grad_out.shape[1]
    cuts = columns // width
    high = part // cuts

    @pl.when(step == 0)
    def _():
        for i in range(4):
            rows = pl.ds(pl.multiple_of((low ^ (i % 2)) * half, 16), half)
            held[i // 2, rows] = parts[i][...]

    which = jnp.where(step % 2 == core, 0, 1)
    at = pl.ds(pl.multiple_of((step // 2) * tile, tile), tile)
    grad_in[...] = held[which, :part, at].astype(F32)

    @pl.when(step < 2)
    def _():
        for i in range(cuts):
            grad_out[i * high : (i + 1) * high] = held[
                which, part : part + high, i * width : (i + 1) * width
            ].astype(F32)


def qkv_finish_kernel(blocks, halved, sc, *refs):
    parts, (grad_qkv, sums, held) = refs[:4], refs[4:]
    half, _, part = parts[0].shape
    share = grad_qkv.shape[0]
    core, low = sc[1], sc[sc.shape[0] - 1]
    mine = (pl.program_id(0) == core) if halved else True
    for i in range(4):
        for j in range(half):
            held[i // 2, (low ^ (i % 2)) * half + j] = parts[i][j].astype(F32)
    for mask in range(blocks):
        columns = pl.ds(pl.multiple_of((sc[0] ^ mask) * part, part), part)
        grad_qkv[:, columns] = jnp.where(mine, held[0, mask, :share], held[1, mask, :share])

    @pl.when((pl.program_id(0) == 0) & (pl.program_id(1) == 0))
    def _():
        total = jnp.zeros((8, part), F32)
        for i in range(2 if halved else 1):
            for mask in range(blocks):
                total = total + held[i, mask, share : share + 8]
        sums[...] = total


def tokens_kernel(blocks, sc, tokens, grad_res, gains, *refs):
    pieces = refs[:blocks]
    weights = refs[blocks : blocks + 3]
    grad_tokens, total = refs[blocks + 3 :]
    step, steps = pl.program_id(0), pl.num_programs(0)
    for mask in range(blocks):

        @pl.when(step == mask)
        def _():
            found = nt(pieces[mask][0], weights[0][...])
            found = found + nt(pieces[mask][1], weights[1][...])
            found = found + nt(pieces[mask][2], weights[2][...])
            if mask == 0:
                total[...] = found
            else:
                total[...] += found

    @pl.when(step == steps - 1)
    def _():
        unit, scale = norm_stats(tokens[...].astype(F32))
        grad_tokens[...] = grad_res[...] + norm_back(
            unit, scale, gains[0:1].astype(F32), total[...]
        )


def index_kernel(blocks, place, continues, scalars, banks):
    my_block, my_group = lax.axis_index("blk"), lax.axis_index("grp")
    chip, core = my_group // 2, my_group % 2
    scalars[0], scalars[1] = my_block, core
    for mask in range(blocks):
        scalars[2 + mask] = place[my_block ^ mask]
    scalars[2 + blocks] = chip % 2
    banks[0], banks[1] = chip, core
    for i in range(continues.shape[0]):
        banks[2 + i] = continues[i]


def indices(place, continues):
    smem = pl.BlockSpec(memory_space=pltpu.SMEM)
    blocks, banks = place.shape[0], continues.shape[0]
    return pl.pallas_call(
        functools.partial(index_kernel, blocks),
        in_specs=[smem, smem],
        out_specs=[smem, smem],
        out_shape=[
            jax.ShapeDtypeStruct((3 + blocks,), jnp.int32),
            jax.ShapeDtypeStruct((2 + banks,), jnp.int32),
        ],
        name="indices",
    )(place, continues)


def cross_kernel(sc, one, two, top, low):
    half = one.shape[1] // 2
    top[...], low[...] = one[:, :half], two[:, half:]


def join_kernel(sc, top, low, out):
    half = top.shape[1]
    out[:, :half], out[:, half:] = top[...], low[...]


def nothing_kernel(sc):
    pass


def copy_kernel(sc, values, out):
    out[...] = values[...]


def sum_kernel(sc, *refs):
    total = refs[0][...].astype(F32)
    for ref in refs[1:-1]:
        total = total + ref[...].astype(F32)
    refs[-1][...] = total.astype(BF16)


def stack_kernel(sc, *refs):
    for i, ref in enumerate(refs[:-1]):
        refs[-1][i] = ref[...]


def sums_kernel(count, sc, *refs):
    outs = refs[len(refs) - len(refs) // (count + 1) :]
    for i, out in enumerate(outs):
        total = refs[i * count][...].astype(F32)
        for ref in refs[i * count + 1 : (i + 1) * count]:
            total = total + ref[...].astype(F32)
        out[...] = total.astype(BF16)


def exchange_sum_kernel(sc, kept, came, away, held):
    for i in range(held.shape[0]):
        held[i] = (kept[2 * i].astype(F32) + came[2 * i].astype(F32)).astype(BF16)
        away[i] = (kept[2 * i + 1].astype(F32) + came[2 * i + 1].astype(F32)).astype(BF16)


def place_halves(sc, first, second, mine, other):
    low = sc[sc.shape[0] - 1] == 1
    mine[...] = jnp.where(low, second, first)
    other[...] = jnp.where(low, first, second)


def split_sum_kernel(count, sc, *refs):
    totals = []
    for i in range(2):
        total = refs[i * count][...].astype(F32)
        for ref in refs[i * count + 1 : (i + 1) * count]:
            total = total + ref[...].astype(F32)
        totals.append(total.astype(BF16))
    place_halves(sc, *totals, *refs[2 * count :])


def split_stack_kernel(sc, *refs):
    pieces, (mine, other) = refs[:-2], refs[-2:]
    half = len(pieces) // 2
    low = sc[sc.shape[0] - 1] == 1
    for i in range(half):
        first, second = pieces[i][...], pieces[half + i][...]
        mine[i] = jnp.where(low, second, first)
        other[i] = jnp.where(low, first, second)


def cut(chips, tok, width, piece):
    high = max(16, tok // chips)
    across = high * chips // tok
    wide = width // across
    return (
        pl.ds(pl.multiple_of((piece // across) * high, high), high),
        pl.ds(pl.multiple_of((piece % across) * wide, wide), wide),
    )


def piece_shape(chips, tok, width):
    high = max(16, tok // chips)
    return high, tok * width // (chips * high)


def split_kernel(chips, sc, keys, values, came, *outs):
    _, tok, width = keys.shape
    for mask in range(chips):
        rows, columns = cut(chips, tok, width, sc[0] ^ mask)
        own = jnp.where(sc[1] == 0, keys[:, rows, columns], values[:, rows, columns])
        outs[mask][0] = own
        outs[mask][1] = came[:, rows, columns]


def route_kernel(chips, sc, *refs):
    ins, outs, held = refs[:chips], refs[chips : 2 * chips], refs[2 * chips]
    count = ins[0].shape[1]
    per_chip = 2 * count
    for mask in range(chips):
        held[mask] = ins[mask][...]
    for mask in range(chips):
        for i in range(per_chip):
            bank = sc[2 + (sc[0] ^ mask) * per_chip + i]
            outs[mask][i] = held[
                (bank // per_chip) ^ sc[0], ((bank // count) % 2) ^ sc[1], bank % count
            ]


def head_columns_kernel(blocks, keys, values, *outs):
    part = keys.shape[2] // blocks
    outs[-1][...] = jnp.zeros(TOKEN, jnp.int32)
    for mask in range(blocks):
        columns = pl.ds(pl.multiple_of((lax.axis_index("blk") ^ mask) * part, part), part)
        outs[mask][0] = keys[:, :, columns]
        outs[mask][1] = values[:, :, columns]


def choose_kernel(chips, sc, *refs):
    ins, outs, held = refs[: 2 * chips], refs[2 * chips : 3 * chips], refs[3 * chips]
    count = ins[0].shape[1]
    for i in range(2 * chips):
        held[i // chips, i % chips] = ins[i][...]
    for mask in range(chips):
        for i in range(count):
            bank = sc[2 + (sc[0] ^ mask) * 2 * count + sc[1] * count + i]
            core, chip = (bank // count) % 2, bank // (2 * count)
            for j in range(2):
                outs[mask][j, i] = held[core ^ sc[1], chip ^ sc[0], j, bank % count]


def gather_kernel(chips, sc, *refs):
    ins, (kept, sent) = refs[:chips], refs[chips:]
    count, tok, width = kept.shape
    high, wide = ins[0].shape[1:]
    across = width // wide
    for mask in range(chips):
        _, columns = cut(chips, tok, width, sc[0] ^ mask)
        rows = slice((mask // across) * high, (mask // across + 1) * high)
        for i in range(count):
            kept[i, rows, columns] = ins[mask][sc[1] * count + i]
            sent[i, rows, columns] = ins[mask][(1 - sc[1]) * count + i]


def columns_kernel(blocks, sc, kept, came, *outs):
    part = kept.shape[2] // blocks
    for mask in range(blocks):
        columns = pl.ds(pl.multiple_of((sc[0] ^ mask) * part, part), part)
        mine, other = kept[:, :, columns], came[:, :, columns]
        outs[mask][0] = jnp.where(sc[1] == 0, mine, other)
        outs[mask][1] = jnp.where(sc[1] == 0, other, mine)


def fetch_shares(order, mem_keys, mem_values, places, blocks, zero, first, turn, second):
    count, tok, width = mem_keys.shape
    share = ((2, count, tok, width // blocks), BF16)
    *parts, token = pl.pallas_call(
        functools.partial(head_columns_kernel, blocks),
        in_specs=[pl.BlockSpec(memory_space=pltpu.VMEM)] * 2,
        out_specs=[pl.BlockSpec(memory_space=pltpu.VMEM)] * (blocks + 1),
        out_shape=[jax.ShapeDtypeStruct(*share)] * blocks
        + [jax.ShapeDtypeStruct(TOKEN, jnp.int32)],
        compiler_params=params(10),
        cost_estimate=cost_of("bank_columns"),
        name="bank_columns",
    )(mem_keys, mem_values)
    order.last = (token,)
    zero()
    moved = [swap(parts[m], "blk", m) for m in range(1, blocks)]
    own = swap(parts[0], "grp", 1)
    order.last = order.last + tuple(moved) + (own,)
    first()
    parts = [parts[0]] + [swap(p, "grp", 2 * (m + 1)) for m, p in enumerate(moved)]
    turn()
    others = [own] + [swap(p, "grp", 1) for p in parts[1:]]
    parts = order.call(
        functools.partial(choose_kernel, blocks),
        "choose_banks",
        (1,),
        parts + others,
        [share] * blocks,
        [pltpu.VMEM((2, blocks) + share[0], BF16)],
        14,
        places,
    )
    second()
    return [parts[0]] + [swap(parts[m], "grp", 2 * m) for m in range(1, blocks)]


def fetch_banks(order, mem_keys, mem_values, places, groups, my_group, blocks, first, second):
    count, tok, width = mem_keys.shape
    core, chips = my_group % 2, groups // 2
    came = swap(jnp.where(core == 0, mem_values, mem_keys), "grp", 1)
    piece = piece_shape(chips, tok, width)

    def line(parts):
        return [parts[0]] + [swap(parts[m], "grp", 2 * m) for m in range(1, chips)]

    parts = order.call(
        functools.partial(split_kernel, chips),
        "split_banks",
        (1,),
        [mem_keys, mem_values, came],
        [((2, count) + piece, BF16)] * chips,
        [],
        10,
        places,
    )
    first()
    parts = order.call(
        functools.partial(route_kernel, chips),
        "route_banks",
        (1,),
        line(parts),
        [((2 * count,) + piece, BF16)] * chips,
        [pltpu.VMEM((chips, 2, count) + piece, BF16)],
        10,
        places,
    )
    second()
    kept, sent = order.call(
        functools.partial(gather_kernel, chips),
        "gather_banks",
        (1,),
        line(parts),
        [((count, tok, width), BF16)] * 2,
        [],
        10,
        places,
    )
    parts = order.call(
        functools.partial(columns_kernel, blocks),
        "bank_columns",
        (1,),
        [kept, swap(sent, "grp", 1)],
        [((2, count, tok, width // blocks), BF16)] * blocks,
        [],
        10,
    )
    return [parts[0]] + [swap(parts[m], "blk", m) for m in range(1, blocks)]


class Order:
    def __init__(self, scalars, last=()):
        self.scalars, self.last = scalars, last

    def call(self, kernel, name, grid, ins, outs, scratch, mib, scalars=None):
        found = call(
            kernel,
            name,
            grid,
            ins,
            outs,
            scratch,
            self.scalars if scalars is None else scalars,
            mib,
            tuple(self.last),
        )
        self.last = (found[-1],)
        return found[:-1]

    def small(self, kernel, name, items, outs):
        ins = []
        for item in items:
            if isinstance(item, tuple) and len(item) == 2:
                array, at = item
                block = (None,) + array.shape[1:]
                zeros = (0,) * (array.ndim - 1)
                ins.append((array, block, lambda i, sc, at=at, zeros=zeros: (at,) + zeros))
            else:
                ins.append(item)
        return self.call(kernel, name, (1,), ins, [(o, BF16) for o in outs], [], 8)

    def copy(self, value):
        return self.small(copy_kernel, "copy", [value], [value.shape])[0]

    def gate(self, values):
        *found, token = gate(values, self.last)
        self.last = (token,)
        return found


def on_device(
    tokens,
    gain_one,
    bias_one,
    w_qkv,
    w_out,
    gain_two,
    bias_two,
    w_in,
    w_down,
    mem_keys,
    mem_values,
    continues,
    block_place,
    cotangent,
):
    seq_count, tok, width = tokens.shape
    hidden_width = w_in.shape[1]
    blocks, groups = lax.axis_size("blk"), lax.axis_size("grp")
    my_block, my_group = lax.axis_index("blk"), lax.axis_index("grp")
    core = my_group % 2
    part = width // blocks
    pairs = part // 128
    halved = pairs > 1
    rows = seq_count * tok
    seg_rows = blocks * tok
    tile = hidden_width // (2 * blocks)
    scalars, banks = indices(block_place, continues)
    gains = jnp.stack([gain_one, bias_one, gain_two, bias_two])
    flat = tokens.reshape(rows, width)
    cot = cotangent.reshape(rows, width)

    def head_weights(j, at=None):
        def index(i, sc):
            return (0, j * blocks + (sc[0] ^ i if at is None else sc[0]))

        return (w_qkv, (width, part), index)

    def heads_block(j):
        return (1, tok, 128), lambda s, p, sc: (s, 0, j * pairs + p)

    seg_block = (1, seg_rows, 128), lambda s, p, sc: (s, 0, p)
    seg_shape = (seq_count, seg_rows, part)
    tok_block = (1, tok, 128), lambda s, p, sc: (s, 0, p)
    mem_block = (2, 1, tok, 128), lambda s, p, sc: (0, s, 0, p)
    early = {}


    order = Order(scalars)
    rows_block = (None, rows, width)
    normed, qkv, pieces = [], [], []

    def project(some):
        found = order.call(
            functools.partial(project_kernel, len(some)),
            "project",
            (1,),
            [(p, rows_block, lambda i, sc: (0, 0, 0)) for p in some]
            + [gains]
            + [head_weights(j, 0) for j in range(3)],
            [((rows, width), BF16), ((rows, 3 * part), BF16)] * len(some),
            [],
            20,
        )
        pieces.extend(some)
        normed.extend(found[::2])
        qkv.extend(f.reshape(seq_count, tok, 3 * part) for f in found[1::2])

    def own_keys():
        early["own"] = order.call(
            functools.partial(own_kernel, blocks),
            "own_keys",
            (seq_count, pairs),
            [(qkv[m],) + heads_block(j) for m in range(blocks) for j in range(3)],
            [(seg_shape, BF16) + seg_block] * 3 + [(seg_shape, F32) + seg_block] * 2,
            [pltpu.VMEM((3, blocks, tok, 128), BF16)],
            16,
        )

    row_shape = (rows, width)
    both_shape = (2, rows, width)
    half_shape = (2, rows // 2, width)

    def zero():
        early["both"] = order.call(
            stack_kernel, "rows_stack", (1,), [flat, cot], [(both_shape, BF16)], [], 8
        )[0]

    def first():
        (both,) = order.gate([early["both"]])
        masks = (1, 2) if blocks == 4 else range(1, blocks)
        early["both"], early["rows"] = both, [swap(both, "blk", m) for m in masks]

    def turn():
        if blocks == 4:
            top, low = order.call(
                cross_kernel, "cross", (1,), early["rows"], [(half_shape, BF16)] * 2, [], 8
            )
            early["last"] = [swap(top, "blk", 2), swap(low, "blk", 1)]

    def second():
        project([early["both"]] + early["rows"])
        if blocks == 4:
            (piece,) = order.call(
                join_kernel, "join", (1,), early["last"], [(both_shape, BF16)], [], 8
            )
            project([piece])
        own_keys()

    if blocks == groups // 2:
        mem = fetch_shares(order, mem_keys, mem_values, banks, blocks, zero, first, turn, second)
    else:
        mem = fetch_banks(
            order,
            mem_keys,
            mem_values,
            banks,
            groups,
            my_group,
            blocks,
            lambda: (zero(), first(), turn()),
            second,
        )
    queries, keys, values, partial, counts = early["own"]
    found = order.call(
        functools.partial(cached_kernel, blocks),
        "cached_keys",
        (seq_count, pairs),
        [(a,) + seg_block for a in (queries, keys, partial, counts)]
        + [(a,) + mem_block for a in mem],
        [(seg_shape, F32) + seg_block] * 2
        + [((seq_count, tok, part), BF16) + tok_block] * blocks,
        [pltpu.VMEM((2, seg_rows, 128), BF16), pltpu.VMEM((blocks, tok, 128), BF16)],
        16,
    )
    attended_f, counts = found[:2]
    attended = [found[2]] + [swap(found[2 + m], "blk", m) for m in range(1, blocks)]
    attended = [a.reshape(rows, part) for a in attended]

    def ff_tile(j, sc):
        return 2 * (sc[0] ^ (j // 2)) + j % 2

    base = blocks * tile
    found = order.call(
        functools.partial(feed_kernel, blocks),
        "feed",
        (2 * blocks,),
        attended
        + [flat, cot, w_out, gains]
        + [
            (w_in, (width, tile), lambda j, sc: (0, ff_tile(j, sc))),
            (w_down, (tile, width), lambda j, sc: (ff_tile(j, sc), 0)),
        ],
        [
            ((rows, width), BF16),
            ((rows, width), F32),
            ((rows, base), BF16),
            ((rows, base + 2 * width + width // 2), BF16),
            ((rows, width), BF16),
            ((rows, width), BF16),
            ((rows, width // 2), BF16),
            ((2, width), F32),
        ]
        + [((rows, 2 * tile), BF16)] * blocks
        + [((rows, part), BF16)] * blocks,
        [
            pltpu.VMEM((rows, width), F32),
            pltpu.VMEM((rows, width), BF16),
            pltpu.VMEM((rows, width), F32),
            pltpu.VMEM((rows, width), F32),
        ],
        28,
    )
    mixed, grad_res, inner_keep, to_core, normed_two, att_all, branch, sums_two = found[:8]
    acts, grad_att = found[8 : 8 + blocks], found[8 + blocks :]
    grad_att = [grad_att[0]] + [swap(grad_att[m], "blk", m) for m in range(1, blocks)]
    grad_att = [g.reshape(seq_count, tok, part) for g in grad_att]
    core_came = swap(to_core, "grp", 1)
    order.last = order.last + tuple(grad_att[1:]) + (core_came,)
    made = {}

    def acts_path():
        made["acts"] = [acts[0]] + [
            swap(a, "blk", m + 1) for m, a in enumerate(order.gate(acts[1:]))
        ]
        return True
        yield

    top = blocks // 2

    def of_mask(shape, mask, wanted):
        def index(m, sc):
            if mask == 1:
                return (m >> 1, 0, 0)
            return (jnp.maximum(m - top, 0) if wanted else jnp.minimum(m, top - 1), 0, 0)

        return ((top,) + shape, BF16, (1,) + shape, index)

    def columns(start):
        return lambda m, sc: (0, start // part + (sc[0] ^ m))

    in_rows = part + part * width // (2 * base)
    in_shape = (in_rows // 2, base)
    bits = [1 << i for i in range(blocks.bit_length() - 1)]
    results = {}

    def go(names):
        for name in names:
            if name == ".":
                order.call(nothing_kernel, "pause", (1,), [], [], [], 4)
            elif name not in results:
                try:
                    next(paths[name])
                except StopIteration as stop:
                    results[name] = stop.value

    def total(*items):
        first = items[0]
        if not isinstance(first, tuple):
            shape = first.shape
        elif len(first) == 2:
            shape = first[0].shape[1:]
        else:
            shape = first[1]
        return order.small(sum_kernel, "sum", items, [shape])[0]

    def sum_chips(mine, other):
        came = swap(other, "grp", 2)
        yield
        held = total(mine, came)
        for bit in range(2, groups.bit_length() - 1):
            came = swap(held, "grp", 1 << bit)
            yield
            held = total(held, came)
        other = swap(held, "grp", 2)
        return held, other, swap(held, "grp", 1), swap(other, "grp", 1)

    def back_path():
        found = order.call(
        functools.partial(attention_back_kernel, blocks),
        "attention_back",
        (seq_count, pairs),
        [(a,) + seg_block for a in (queries, keys, values, attended_f, counts)]
        + [(a,) + mem_block for a in mem]
        + [(a,) + tok_block for a in grad_att],
        [
            (
                (3, seq_count, tok, part),
                BF16,
                (3, 1, tok, 128),
                lambda s, p, sc: (0, s, 0, p),
            )
        ]
        * blocks,
        [
            pltpu.VMEM((2, seg_rows, 128), BF16),
            pltpu.VMEM((blocks, tok, 128), BF16),
            pltpu.VMEM((3, blocks, tok, 128), BF16),
        ],
        24,
    )
        made["grads"] = [g.reshape(3, rows, part) for g in found]
        return True
        yield

    def in_start():
        found = order.call(
        functools.partial(in_kernel, blocks),
        "grad_in",
        (blocks,),
        [
            (normed_two, (rows, part), columns(0)),
            (core_came, (rows, part), columns(base)),
            inner_keep,
            (core_came, (rows, base), lambda m, sc: (0, 0)),
            (att_all, (rows, part), columns(0)),
            (core_came, (rows, part), columns(base + width)),
            branch,
            (core_came, (rows, width // 2), lambda m, sc: (0, 2 * (base + 2 * width) // width)),
        ],
        [of_mask(in_shape, mask, sent) for mask in (1, top) for sent in (True, False)],
        [pltpu.VMEM((in_rows, base), BF16)],
        28,
    )
        made["kept"] = found[1], found[3]
        made["came"] = swap(found[0], "blk", 1), swap(found[2], "blk", top)
        return True
        yield

    def in_path():
        firsts, rests = (1, top), (bits[1:], bits[:-1][::-1])
        masks = [[m for m in range(blocks) if not m & bit] for bit in firsts]
        in_kept, came = made["kept"], made["came"]
        terms = [
            {m: [(in_kept[h], i), (came[h], i)] for i, m in enumerate(masks[h])} for h in range(2)
        ]
        for bit in range(len(bits) - 1):
            away = [[m for m in masks[h] if m & rests[h][bit]] for h in range(2)]
            masks = [[m for m in masks[h] if not m & rests[h][bit]] for h in range(2)]
            items = [v for h in range(2) for m in away[h] for v in terms[h][m]]
            count = len(away[0])
            sent = order.small(
                functools.partial(sums_kernel, len(items) // (2 * count)),
                "sums",
                items,
                [in_shape] * (2 * count),
            )
            for h in range(2):
                for i, m in enumerate(masks[h]):
                    came = swap(sent[h * count + i], "blk", rests[h][bit])
                    terms[h][m] = terms[h][m] + [came]
            yield
        items = [v for h in range(2) for v in terms[h][0]]
        mine, other = order.small(
            functools.partial(split_sum_kernel, len(items) // 2), "split", items, [in_shape] * 2
        )
        return (yield from sum_chips(mine, other))

    def down_start():
        found = order.call(
        functools.partial(down_kernel, blocks),
        "grad_down",
        (2,),
        [
            (a, (rows, tile), lambda i, sc: (0, jnp.where(i == 0, 1 - sc[1], sc[1])))
            for a in made["acts"]
        ]
        + [(p, rows_block, lambda i, sc: (1, 0, 0)) for p in pieces],
        [((tile, width), BF16)] * 2,
        [],
        28,
    )
        made["down"] = found[1], swap(found[0], "grp", 1)
        return True
        yield

    def down_path():
        down_kept, down_came = made["down"]
        block = (tile // 2, width)
        items = [
            (v, block, lambda i, sc, h=h: (h, 0)) for h in range(2) for v in (down_kept, down_came)
        ]
        mine, other = order.small(
            functools.partial(split_sum_kernel, 2), "split", items, [block] * 2
        )
        return (yield from sum_chips(mine, other))

    share = part // 2 if halved else part
    share_block = (1, share + 16, 3 * part), lambda m, sc: (m, 0, 0)

    def own_weights(j):
        return (w_qkv, (part, part), lambda m, sc: (sc[0] ^ m, j * blocks + sc[0]))

    def qkv_start():
        found = order.call(
        functools.partial(qkv_kernel, blocks, halved),
        "grad_qkv",
        (blocks,),
        [(n, (rows, part), columns(0)) for n in normed]
        + made["grads"]
        + [own_weights(j) for j in range(3)]
        + [(gains, (4, part), columns(0))]
        + [(sums_two, (2, part), columns(0))],
        [((blocks, share + 16, 3 * part), BF16) + share_block] * (2 if halved else 1),
        [],
        28,
    )
        made["qkv"] = found[-1], swap(found[0], "grp", 1)
        return True
        yield

    def qkv_path():
        qkv_kept, came = made["qkv"]
        shape = qkv_kept.shape[1:]
        half = (blocks // 2,) + shape
        away, kept = order.small(
            exchange_sum_kernel, "sums", [qkv_kept, came], [half] * 2
        )
        came = swap(away, "blk", 1)
        yield
        held = {2 * i: [(kept, i), (came, i)] for i in range(blocks // 2)}
        for bit in bits[1:]:
            masks = [m for m in sorted(held) if m & bit]
            items = [v for m in masks for v in held[m]]
            (away,) = order.small(stack_kernel, "stack", items, [(len(items),) + shape])
            came = swap(away, "blk", bit)
            yield
            held = {m: v for m, v in held.items() if not m & bit}
            count = len(held[0])
            for i, m in enumerate(sorted(held)):
                held[m] = held[m] + [(came, i * count + k) for k in range(count)]
        mine, other = order.small(split_stack_kernel, "split", held[0], [half] * 2)
        return (yield from sum_chips(mine, other))

    def tokens_path():
        shape = (3, rows, part)
        held = {m: [g] for m, g in enumerate(made["grads"])}
        for bit in bits:
            items = [v for m in sorted(held) if m & bit for v in held[m]]
            (away,) = order.small(stack_kernel, "stack", items, [(len(items),) + shape])
            came = swap(away, "blk", bit)
            yield
            held = {m: v for m, v in held.items() if not m & bit}
            count = len(held[0])
            for i, m in enumerate(sorted(held)):
                held[m] = held[m] + [(came, i * count + k) for k in range(count)]
        grads = held[0][:1] + [
            (g, (None,) + shape, lambda i, sc, at=at: (at, 0, 0, 0)) for g, at in held[0][1:]
        ]
        return order.call(
            functools.partial(tokens_kernel, blocks),
            "tokens_back",
            (blocks,),
            [flat, grad_res, gains] + grads + [head_weights(j) for j in range(3)],
            [((rows, width), F32)],
            [pltpu.VMEM((rows, width), F32)],
            24,
        )

    def down_finish():
        return order.call(
            down_finish_kernel,
            "down_finish",
            (4,),
            list(results["d"]),
            [((2 * tile, width), F32, (tile // 2, width), lambda i, sc: (i, 0))],
            [],
            16,
        )
        yield

    def in_finish():
        return order.call(
            functools.partial(in_finish_kernel, blocks),
            "in_finish",
            (2 * blocks,),
            list(results["i"]),
            [
                ((part, hidden_width), F32, (part, tile), lambda j, sc: (0, j)),
                ((part, width), F32, (part, width // 2), lambda j, sc: (0, jnp.minimum(j, 1))),
            ],
            [pltpu.VMEM((2, in_rows, base), BF16)],
            16,
        )
        yield

    def qkv_finish():
        high = share + 16
        return order.call(
            functools.partial(qkv_finish_kernel, blocks, halved),
            "qkv_finish",
            (2 if halved else 1, 3),
            [(a, (blocks // 2, high, part), lambda k, i, sc: (0, 0, i)) for a in results["q"]],
            [
                ((part, 3 * width), F32, (share, width), lambda k, i, sc: (k, i)),
                ((8, part), F32),
            ],
            [pltpu.VMEM((2, blocks, high, part), F32)],
            16,
        )
        yield

    paths = {
        "A": acts_path(),
        "B": back_path(),
        "N": in_start(),
        "W": down_start(),
        "Y": qkv_start(),
        "d": down_path(),
        "i": in_path(),
        "q": qkv_path(),
        "t": tokens_path(),
        "F": down_finish(),
        "H": in_finish(),
        "G": qkv_finish(),
    }
    go(PLAN if groups == 8 and blocks == 4 else "ABNWY")
    while len(results) < len(paths):
        for name in paths:
            needs = {"F": "d", "H": "i", "G": "q"}.get(name)
            if needs is None or needs in results:
                go(name)
    (grad_down,) = results["F"]
    grad_qkv, sums = results["G"]
    grad_in, grad_out = results["H"]
    (grad_tokens,) = results["t"]
    return (
        mixed.reshape(tokens.shape),
        grad_tokens.reshape(tokens.shape),
        sums[0],
        sums[1],
        grad_qkv,
        grad_out,
        sums[2],
        sums[3],
        grad_in,
        grad_down,
    )


def solution(mesh):
    rows = P("grp", "blk", None)
    in_specs = (rows,) + (P(),) * 8 + (rows, rows, P(), P(), rows)
    out_specs = (rows, rows) + (P("blk"),) * 2 + (P("blk", None),) * 2
    out_specs = out_specs + (P("blk"),) * 2 + (P("blk", None),) * 2
    return jax.shard_map(
        on_device, mesh=mesh, in_specs=in_specs, out_specs=out_specs, check_vma=False
    )
```

```python
import functools

import jax
import jax.numpy as jnp
from jax import lax
from jax.experimental import pallas as pl
from jax.experimental.pallas import tpu as pltpu
from jax.sharding import PartitionSpec as P

HEADS = 16
F32 = jnp.float32
BF16 = jnp.bfloat16
MIB = 1 << 20
EPS = 1e-05
FAR = -1e30
GELU_A = 0.7978845608028654
GELU_B = 0.044715


def swap(values, axis, mask):
    size = lax.axis_size(axis)
    return lax.ppermute(values, axis, [(i, i ^ mask) for i in range(size)])


def pick(values, index, dim=0):
    return lax.dynamic_index_in_dim(values, index, dim, keepdims=False)


def nn(left, right):
    return lax.dot_general(left, right, (((1,), (0,)), ((), ())), preferred_element_type=F32)


def nt(left, right):
    return lax.dot_general(left, right, (((1,), (1,)), ((), ())), preferred_element_type=F32)


def tn(left, right):
    return lax.dot_general(left, right, (((0,), (0,)), ((), ())), preferred_element_type=F32)


def params(mib):
    return pltpu.CompilerParams(vmem_limit_bytes=mib * MIB)


ANYWHERE = pl.BlockSpec(memory_space=pl.ANY)
EVERY = range(100)
TOKEN = (8, 128)
COSTS = {'': (3000000000, 10000000000), 'grad_in': (10000000000, 1000000), 'grad_qkv': (10000000000, 1000000), 'attention_back': (10000000000, 1000000), 'feed': (100000000000, 1000000), 'tokens_back': (100000000000, 1000000), 'project': (1000000000, 1000000000), 'own_keys': (1000000000, 1000000000), 'cached_keys': (1000000000, 1000000000), 'bank_columns': (1000000000, 1000000000), 'cross': (1000000000, 1000000000), 'join': (1000000000, 1000000000), 'copy': (1000000000, 1000000000), 'choose_banks': (1000000000, 1000000000), 'grad_down': (3000000000, 10000000000)}
PLAN = "ABNWYdqidiqdqtitiqFtqiHqG"


def cost_of(name):
    flops, size = COSTS.get(name, COSTS[""])
    return pl.CostEstimate(flops=flops, bytes_accessed=size, transcendentals=0)


OUT_HBM = {
    "project": range(0, 20, 2),
    "own_keys": (2,),
    "cached_keys": (0, 1),
    "feed": (0, 1, 2, 4, 5, 6, 8, 9, 10, 11, 12, 13, 14, 15),
}
IN_HBM = {
    "bank_columns": (0, 1),
    "rows_stack": (0, 1),
    "project": range(2, 10),
    "attention_back": EVERY,
    "grad_qkv": (0, 1, 2, 3),
    "grad_out": EVERY,
}


def call(kernel, name, grid, ins, outs, scratch, scalars, mib, tokens=()):
    def whole(shape):
        return pl.BlockSpec(shape, lambda *_: (0,) * len(shape))

    in_specs, arrays = [], []
    for item in ins:
        if isinstance(item, tuple):
            arrays.append(item[0])
            in_specs.append(pl.BlockSpec(item[1], item[2]))
        else:
            arrays.append(item)
            in_specs.append(whole(item.shape))
    out_shapes, out_specs = [], []
    for item in outs:
        out_shapes.append(jax.ShapeDtypeStruct(item[0], item[1]))
        out_specs.append(whole(item[0]) if len(item) == 2 else pl.BlockSpec(item[2], item[3]))
    count = len(arrays)

    pinned = IN_HBM.get(name, ())
    arrays = [
        pltpu.with_memory_space_constraint(a, pltpu.HBM) if i in pinned else a
        for i, a in enumerate(arrays)
    ]
    pinned = OUT_HBM.get(name, ())
    out_shapes = [
        pltpu.HBM(o.shape, o.dtype) if i in pinned else o for i, o in enumerate(out_shapes)
    ]

    out_shapes = out_shapes + [jax.ShapeDtypeStruct(TOKEN, jnp.int32)]
    out_specs = out_specs + [whole(TOKEN)]
    last = count + len(tokens) + len(outs)

    def body(sc, *refs):
        kernel(sc, *refs[:count], *refs[count + len(tokens) : last], *refs[last + 1 :])
        refs[last][...] = jnp.zeros(TOKEN, jnp.int32)

    spec = pltpu.PrefetchScalarGridSpec(
        num_scalar_prefetch=1,
        grid=grid,
        in_specs=in_specs + [ANYWHERE] * len(tokens),
        out_specs=out_specs,
        scratch_shapes=scratch,
    )
    return pl.pallas_call(
        body,
        grid_spec=spec,
        out_shape=out_shapes,
        compiler_params=params(mib),
        cost_estimate=cost_of(name),
        name=name,
    )(scalars, *arrays, *tokens)


def corner(value):
    block = (1,) * (value.ndim - 2) + (min(16, value.shape[-2]), 128)
    return pl.BlockSpec(block, lambda *_: (0,) * value.ndim)


def gate(values, tokens):
    count = len(values)

    def body(*refs):
        refs[-1][...] = jnp.zeros(TOKEN, jnp.int32)

    return pl.pallas_call(
        body,
        grid=(1,),
        in_specs=[ANYWHERE] * count + [corner(t) for t in tokens],
        out_specs=[ANYWHERE] * count + [pl.BlockSpec(memory_space=pltpu.VMEM)],
        out_shape=[jax.ShapeDtypeStruct(v.shape, v.dtype) for v in values]
        + [jax.ShapeDtypeStruct(TOKEN, jnp.int32)],
        input_output_aliases={i: i for i in range(count)},
        cost_estimate=cost_of("gate"),
        name="gate",
    )(*values, *tokens)


def norm_stats(values):
    average = jnp.mean(values, -1, keepdims=True)
    centred = values - average
    scale = lax.rsqrt(jnp.mean(centred * centred, -1, keepdims=True) + EPS)
    return centred * scale, scale


def norm_back(unit, scale, gain, grad):
    scaled = grad * gain
    mean_one = jnp.mean(scaled, -1, keepdims=True)
    mean_two = jnp.mean(scaled * unit, -1, keepdims=True)
    return scale * (scaled - mean_one - unit * mean_two)


def project_kernel(count, sc, *refs):
    rows, gains, weights = refs[:count], refs[count], refs[count + 1 : count + 4]
    outs = refs[count + 4 :]
    gain, bias = gains[0:1].astype(F32), gains[1:2].astype(F32)
    part = weights[0].shape[1]
    for i in range(count):
        unit, _ = norm_stats(rows[i][...].astype(F32))
        low = (unit * gain + bias).astype(BF16)
        outs[2 * i][...] = low
        for j, weight in enumerate(weights):
            outs[2 * i + 1][:, j * part : (j + 1) * part] = nn(low, weight[...]).astype(BF16)


def lane_masks():
    lane = lax.broadcasted_iota(jnp.int32, (1, 128), 1)
    return [lane < 64, lane >= 64]


def of_head(values, mask):
    return jnp.where(mask, values, jnp.zeros_like(values))


def by_head(first, second, masks):
    return jnp.where(masks[0], first, second)


BLOCK = 256


def own_kernel(blocks, sc, *refs):
    ins, outs = refs[: 3 * blocks], refs[3 * blocks :]
    q_out, k_out, v_out, t_out, l_out = outs[:5]
    held = outs[5]
    tok = ins[0].shape[1]
    scale = 64 ** (-0.5)
    for mask in range(blocks):
        place = sc[2 + mask]
        for i in range(3):
            values = ins[3 * mask + i][0]
            if i == 0:
                values = (values.astype(F32) * scale).astype(BF16)
            held[i, place] = values
    rows = blocks * tok
    queries = held[0].reshape(rows, 128)
    keys = held[1].reshape(rows, 128)
    values = held[2].reshape(rows, 128)
    q_out[0], k_out[0], v_out[0] = queries, keys, values
    masks = lane_masks()
    size = min(BLOCK, rows)
    lower = lax.broadcasted_iota(jnp.int32, (size, size), 0) >= lax.broadcasted_iota(
        jnp.int32, (size, size), 1
    )
    product = queries.astype(F32) * keys.astype(F32)
    head_keys = [of_head(keys, m) for m in masks]
    head_values = [of_head(values, m) for m in masks]
    selfs = [jnp.sum(of_head(product, m), -1, keepdims=True) for m in masks]
    for i in range(rows // size):
        here = slice(i * size, (i + 1) * size)
        total, sums = jnp.zeros((size, 128), F32), []
        for h in range(2):
            count = jnp.zeros((size, 1), F32)
            for j in range(i + 1):
                there = slice(j * size, (j + 1) * size)
                scores = nt(queries[here], head_keys[h][there]) - selfs[h][here]
                if i == j:
                    scores = jnp.where(lower, scores, FAR)
                weights = jnp.exp(scores)
                count = count + jnp.sum(weights, -1, keepdims=True)
                total = total + nn(weights.astype(BF16), head_values[h][there])
            sums.append(count)
        t_out[0, here] = total
        l_out[0, here] = by_head(sums[0], sums[1], masks)


def load_cached(pieces, mem):
    tok = pieces[0].shape[2]
    for mask, piece in enumerate(pieces):
        mem[:, mask * tok : (mask + 1) * tok] = piece[:, 0]


def cached_kernel(blocks, sc, *refs):
    q_in, k_in, t_in, l_in = refs[:4]
    pieces = refs[4 : 4 + blocks]
    att_out, l_out = refs[4 + blocks : 6 + blocks]
    sends = refs[6 + blocks : 6 + 2 * blocks]
    mem, low = refs[6 + 2 * blocks :]
    load_cached(pieces, mem)
    tok = pieces[0].shape[2]
    queries, keys = q_in[0], k_in[0]
    rows = queries.shape[0]
    masks = lane_masks()
    product = queries.astype(F32) * keys.astype(F32)
    selfs = [jnp.sum(of_head(product, m), -1, keepdims=True) for m in masks]
    head_keys = [of_head(mem[0], m) for m in masks]
    head_values = [of_head(mem[1], m) for m in masks]
    size = min(BLOCK, rows)
    for i in range(rows // size):
        here = slice(i * size, (i + 1) * size)
        total, sums = t_in[0, here], []
        for h in range(2):
            weights = jnp.exp(nt(queries[here], head_keys[h]) - selfs[h][here])
            sums.append(jnp.sum(weights, -1, keepdims=True))
            total = total + nn(weights.astype(BF16), head_values[h])
        count = l_in[0, here] + by_head(sums[0], sums[1], masks)
        attended = total / count
        att_out[0, here] = attended
        l_out[0, here] = count
        low[i * size // tok : (i + 1) * size // tok] = attended.astype(BF16).reshape(
            size // tok, tok, 128
        )
    for mask in range(blocks):
        sends[mask][0] = low[sc[2 + mask]]


def attention_back_kernel(blocks, sc, *refs):
    q_in, k_in, v_in, att_in, l_in = refs[:5]
    pieces = refs[5 : 5 + blocks]
    grads = refs[5 + blocks : 5 + 2 * blocks]
    sends = refs[5 + 2 * blocks : 5 + 3 * blocks]
    mem, came, low = refs[5 + 3 * blocks :]
    load_cached(pieces, mem)
    tok = pieces[0].shape[2]
    for mask in range(blocks):
        came[sc[2 + mask]] = grads[mask][0]
    queries, keys, values = q_in[0], k_in[0], v_in[0]
    rows = queries.shape[0]
    scale = 64 ** (-0.5)
    masks = lane_masks()
    grad = came[...].reshape(rows, 128).astype(F32)
    count = l_in[0]
    scaled_f = grad / count
    scaled = scaled_f.astype(BF16)
    weighed = grad * att_in[0] / count
    product = queries.astype(F32) * keys.astype(F32)
    selfs = [jnp.sum(of_head(product, m), -1, keepdims=True) for m in masks]
    fixes = [jnp.sum(of_head(weighed, m), -1, keepdims=True) for m in masks]
    own_k = [of_head(keys, m) for m in masks]
    own_v = [of_head(values, m) for m in masks]
    mem_k = [of_head(mem[0], m) for m in masks]
    mem_v = [of_head(mem[1], m) for m in masks]
    q_t = [of_head(queries, m).astype(F32).T.astype(BF16) for m in masks]
    s_t = [of_head(scaled, m).astype(F32).T.astype(BF16) for m in masks]
    size = min(BLOCK, rows)
    lower = lax.broadcasted_iota(jnp.int32, (size, size), 0) >= lax.broadcasted_iota(
        jnp.int32, (size, size), 1
    )
    steps = rows // size
    keys_t = [jnp.zeros((128, size), F32) for _ in range(steps)]
    values_t = [jnp.zeros((128, size), F32) for _ in range(steps)]
    diags = []
    for i in range(steps):
        here = slice(i * size, (i + 1) * size)
        total, sums = jnp.zeros((size, 128), F32), []
        for h in range(2):
            diag = jnp.zeros((size, 1), F32)
            for j in range(i + 1):
                there = slice(j * size, (j + 1) * size)
                scores = nt(queries[here], own_k[h][there]) - selfs[h][here]
                if i == j:
                    scores = jnp.where(lower, scores, FAR)
                weights = jnp.exp(scores)
                change = weights * (nt(scaled[here], own_v[h][there]) - fixes[h][here])
                diag = diag + jnp.sum(change, -1, keepdims=True)
                small = change.astype(BF16)
                total = total + nn(small, own_k[h][there])
                keys_t[j] = keys_t[j] + nn(q_t[h][:, here], small)
                values_t[j] = values_t[j] + nn(s_t[h][:, here], weights.astype(BF16))
            weights = jnp.exp(nt(queries[here], mem_k[h]) - selfs[h][here])
            change = weights * (nt(scaled[here], mem_v[h]) - fixes[h][here])
            diag = diag + jnp.sum(change, -1, keepdims=True)
            total = total + nn(change.astype(BF16), mem_k[h])
            sums.append(diag)
        diag = by_head(sums[0], sums[1], masks)
        diags.append(diag)
        grad_q = scale * (total - diag * keys[here].astype(F32))
        low[0, i * size // tok : (i + 1) * size // tok] = grad_q.astype(BF16).reshape(
            size // tok, tok, 128
        )
    for j in range(steps):
        there = slice(j * size, (j + 1) * size)
        grad_k = keys_t[j].T - diags[j] * queries[there].astype(F32)
        blocks_here = slice(j * size // tok, (j + 1) * size // tok)
        low[1, blocks_here] = grad_k.astype(BF16).reshape(size // tok, tok, 128)
        low[2, blocks_here] = values_t[j].T.astype(BF16).reshape(size // tok, tok, 128)
    for mask in range(blocks):
        for i in range(3):
            sends[mask][i, 0] = low[i, sc[2 + mask]]


def feed_kernel(blocks, sc, *refs):
    att_in = refs[:blocks]
    rest = refs[blocks:]
    tokens, cot, w_out, gains, w_in, w_down = rest[:6]
    rest = rest[6:]
    gain, bias = gains[2:3].astype(F32), gains[3:4].astype(F32)
    mixed, grad_res, inner_keep, to_core, normed_out, att_out, branch_keep, sums = rest[:8]
    acts = rest[8 : 8 + blocks]
    grad_att = rest[8 + blocks : 8 + 2 * blocks]
    residual, normed, total, back = rest[8 + 2 * blocks :]
    step, steps = pl.program_id(0), pl.num_programs(0)
    part, width, tile = att_in[0].shape[1], tokens.shape[1], w_in.shape[1]
    my_block, core = sc[0], sc[1]
    base = blocks * tile

    def out_rows(mask):
        return pl.ds(pl.multiple_of((my_block ^ mask) * part, part), part)

    @pl.when(step == 0)
    def _():
        branch = tokens[...].astype(F32)
        for mask in range(blocks):
            branch = branch + nn(att_in[mask][...], w_out[out_rows(mask), :])
            att_out[:, out_rows(mask)] = att_in[mask][...]
        to_core[:, base + width : base + 2 * width] = att_out[...]
        residual[...] = branch
        unit, _ = norm_stats(branch)
        low = (unit * gain + bias).astype(BF16)
        normed[...] = low
        normed_out[...] = low
        to_core[:, base : base + width] = low

    inner = nn(normed[...], w_in[...])
    square = inner * inner
    bend = jnp.tanh(GELU_A * inner * (1.0 + GELU_B * square))
    half = 0.5 * (1.0 + bend)
    act = (inner * half).astype(BF16)
    slope = half + (0.5 * GELU_A) * inner * (1.0 - bend * bend) * (1.0 + 3.0 * GELU_B * square)
    grad = (slope * nt(cot[...], w_down[...])).astype(BF16)
    into = nn(act, w_down[...])
    away = nt(grad, w_in[...])

    @pl.when(step == 0)
    def _():
        total[...] = into
        back[...] = away

    @pl.when(step > 0)
    def _():
        total[...] += into
        back[...] += away

    for j in range(2 * blocks):

        @pl.when(step == j)
        def _():
            acts[j // 2][:, (j % 2) * tile : (j % 2 + 1) * tile] = act

    columns = pl.ds(pl.multiple_of((my_block ^ (step // 2)) * tile, tile), tile)

    @pl.when(step % 2 == core)
    def _():
        inner_keep[:, columns] = grad

    @pl.when(step % 2 != core)
    def _():
        to_core[:, columns] = grad

    @pl.when(step == steps - 1)
    def _():
        here = residual[...]
        mixed[...] = (here + total[...]).astype(BF16)
        unit, scale = norm_stats(here)
        away = back[...]
        sums[0:1] = jnp.sum(away * unit, 0, keepdims=True)
        sums[1:2] = jnp.sum(away, 0, keepdims=True)
        found = cot[...].astype(F32) + norm_back(unit, scale, gain, away)
        grad_res[...] = found
        low = found.astype(BF16)
        left, right = low[:, : width // 2], low[:, width // 2 :]
        branch_keep[...] = jnp.where(core == 0, left, right)
        to_core[:, base + 2 * width :] = jnp.where(core == 0, right, left)
        for mask in range(blocks):
            grad_att[mask][...] = nt(low, w_out[out_rows(mask), :]).astype(BF16)


def in_kernel(blocks, sc, *refs):
    (normed, normed_two, inner, inner_two, att, att_two, branch, branch_two) = refs[:8]
    outs, held = refs[8:12], refs[12]
    part = normed.shape[1]
    tile = inner.shape[1] // blocks
    for q in range(blocks):
        columns = slice(q * tile, (q + 1) * tile)
        found = tn(normed[...], inner[:, columns]) + tn(normed_two[...], inner_two[:, columns])
        held[:part, columns] = found.astype(BF16)
    out = (tn(att[...], branch[...]) + tn(att_two[...], branch_two[...])).astype(BF16)
    width = out.shape[1]
    cuts = held.shape[1] // width
    high = part // cuts
    for i in range(cuts):
        held[part : part + high, i * width : (i + 1) * width] = out[i * high : (i + 1) * high]
    step = pl.program_id(0)
    half = held.shape[0] // 2
    for i, bit in enumerate((1, blocks // 2)):

        @pl.when((step & bit) != 0)
        def _():
            outs[2 * i][0] = held[i * half : (i + 1) * half]

        @pl.when((step & bit) == 0)
        def _():
            outs[2 * i + 1][0] = held[i * half : (i + 1) * half]


def down_kernel(blocks, sc, *refs):
    acts, cots, (sent, kept) = refs[:blocks], refs[blocks : 2 * blocks], refs[2 * blocks :]
    total = tn(acts[0][...], cots[0][...])
    for mask in range(1, blocks):
        total = total + tn(acts[mask][...], cots[mask][...])
    low = total.astype(BF16)

    @pl.when(pl.program_id(0) == 0)
    def _():
        sent[...] = low

    @pl.when(pl.program_id(0) == 1)
    def _():
        kept[...] = low


def qkv_kernel(blocks, halved, sc, *refs):
    normed, grads = refs[:blocks], refs[blocks : 2 * blocks]
    weights = refs[2 * blocks : 2 * blocks + 3]
    gains, sums_two = refs[2 * blocks + 3 : 2 * blocks + 5]
    outs = refs[2 * blocks + 5 :]
    part = grads[0].shape[2]
    share = part // 2 if halved else part
    ahead = jnp.zeros((part, 1), F32)
    plain = jnp.zeros((part, 1), F32)
    for j in range(3):
        total = tn(normed[0][...], grads[0][j])
        count = jnp.sum(grads[0][j].astype(F32), 0, keepdims=True)
        for mask in range(1, blocks):
            total = total + tn(normed[mask][...], grads[mask][j])
            count = count + jnp.sum(grads[mask][j].astype(F32), 0, keepdims=True)
        weight = weights[j][...].astype(F32)
        ahead = ahead + jnp.sum(weight * total, -1, keepdims=True)
        plain = plain + jnp.sum(weight * count, -1, keepdims=True)
        low = total.astype(BF16)
        columns = slice(j * part, (j + 1) * part)
        if halved:
            first, second = low[:share], low[share:]
            outs[0][0, :share, columns] = jnp.where(sc[1] == 0, second, first)
            outs[1][0, :share, columns] = jnp.where(sc[1] == 0, first, second)
        else:
            outs[0][0, :share, columns] = low
    flat = [jnp.broadcast_to(v, (part, 128)).T[0:1] for v in (ahead, plain)]
    shift = (flat[0] - gains[1:2].astype(F32) * flat[1]) / gains[0:1].astype(F32)
    row = lax.broadcasted_iota(jnp.int32, (16, part), 0)
    vectors = jnp.zeros((16, part), F32)
    for i, vector in enumerate((shift, flat[1], sums_two[0:1], sums_two[1:2])):
        vectors = jnp.where(row == i, vector, vectors)
    vectors = vectors.astype(BF16)
    for out in outs:
        out[0, share:] = jnp.zeros((16, 3 * part), BF16)
    outs[-1][0, share:, :part] = vectors


def down_finish_kernel(sc, *refs):
    parts, grad_down = refs[:4], refs[4]
    core, low = sc[1], sc[sc.shape[0] - 1]
    for i in range(4):
        wanted = 2 * (core ^ (i // 2)) + (low ^ (i % 2))

        @pl.when(pl.program_id(0) == wanted)
        def _():
            grad_down[...] = parts[i][...].astype(F32)


def in_finish_kernel(blocks, sc, *refs):
    parts, (grad_in, grad_out, held) = refs[:4], refs[4:]
    step = pl.program_id(0)
    core, low = sc[1], sc[sc.shape[0] - 1]
    half, columns = parts[0].shape
    part, tile = grad_in.shape
    width = grad_out.shape[1]
    cuts = columns // width
    high = part // cuts

    @pl.when(step == 0)
    def _():
        for i in range(4):
            rows = pl.ds(pl.multiple_of((low ^ (i % 2)) * half, 16), half)
            held[i // 2, rows] = parts[i][...]

    which = jnp.where(step % 2 == core, 0, 1)
    at = pl.ds(pl.multiple_of((step // 2) * tile, tile), tile)
    grad_in[...] = held[which, :part, at].astype(F32)

    @pl.when(step < 2)
    def _():
        for i in range(cuts):
            grad_out[i * high : (i + 1) * high] = held[
                which, part : part + high, i * width : (i + 1) * width
            ].astype(F32)


def qkv_finish_kernel(blocks, halved, sc, *refs):
    parts, grad_qkv, sums = refs[:4], refs[4], refs[5:]
    half, high, wide = parts[0].shape
    share, width = grad_qkv.shape[0], grad_qkv.shape[1] // 3
    part = wide // 3
    core, low = sc[1], sc[sc.shape[0] - 1]
    for i in range(4 if halved else 2):

        @pl.when(pl.program_id(0) == ((core ^ (i // 2)) if halved else 0))
        def _():
            for j in range(half):
                mask = (low ^ (i % 2)) * half + j
                for k in range(3):
                    first = k * width + (sc[0] ^ mask) * part
                    columns = pl.ds(pl.multiple_of(first, part), part)
                    piece = parts[i][j, :share, k * part : (k + 1) * part]
                    grad_qkv[:, columns] = piece.astype(F32)

    @pl.when(pl.program_id(0) == 0)
    def _():
        total = jnp.zeros((high - share, part), F32)
        for i in range(4 if halved else 2):
            for j in range(half):
                total = total + parts[i][j, share:, :part].astype(F32)
        for i, out in enumerate(sums):
            out[...] = total[i]


def tokens_kernel(blocks, sc, tokens, grad_res, gains, *refs):
    pieces = refs[:blocks]
    weights = refs[blocks : blocks + 3]
    grad_tokens, total = refs[blocks + 3 :]
    step, steps = pl.program_id(0), pl.num_programs(0)
    for mask in range(blocks):

        @pl.when(step == mask)
        def _():
            found = nt(pieces[mask][0], weights[0][...])
            found = found + nt(pieces[mask][1], weights[1][...])
            found = found + nt(pieces[mask][2], weights[2][...])
            if mask == 0:
                total[...] = found
            else:
                total[...] += found

    @pl.when(step == steps - 1)
    def _():
        unit, scale = norm_stats(tokens[...].astype(F32))
        grad_tokens[...] = grad_res[...] + norm_back(
            unit, scale, gains[0:1].astype(F32), total[...]
        )


def index_kernel(blocks, place, continues, scalars, banks):
    my_block, my_group = lax.axis_index("blk"), lax.axis_index("grp")
    chip, core = my_group // 2, my_group % 2
    scalars[0], scalars[1] = my_block, core
    for mask in range(blocks):
        scalars[2 + mask] = place[my_block ^ mask]
    scalars[2 + blocks] = chip % 2
    banks[0], banks[1] = chip, core
    for i in range(continues.shape[0]):
        banks[2 + i] = continues[i]


def indices(place, continues):
    smem = pl.BlockSpec(memory_space=pltpu.SMEM)
    blocks, banks = place.shape[0], continues.shape[0]
    return pl.pallas_call(
        functools.partial(index_kernel, blocks),
        in_specs=[smem, smem],
        out_specs=[smem, smem],
        out_shape=[
            jax.ShapeDtypeStruct((3 + blocks,), jnp.int32),
            jax.ShapeDtypeStruct((2 + banks,), jnp.int32),
        ],
        name="indices",
    )(place, continues)


def cross_kernel(sc, one, two, top, low):
    half = one.shape[1] // 2
    top[...], low[...] = one[:, :half], two[:, half:]


def join_kernel(sc, top, low, out):
    half = top.shape[1]
    out[:, :half], out[:, half:] = top[...], low[...]


def nothing_kernel(sc):
    pass


def copy_kernel(sc, values, out):
    out[...] = values[...]


def sum_kernel(sc, *refs):
    total = refs[0][...].astype(F32)
    for ref in refs[1:-1]:
        total = total + ref[...].astype(F32)
    refs[-1][...] = total.astype(BF16)


def stack_kernel(sc, *refs):
    for i, ref in enumerate(refs[:-1]):
        refs[-1][i] = ref[...]


def sums_kernel(count, sc, *refs):
    outs = refs[len(refs) - len(refs) // (count + 1) :]
    for i, out in enumerate(outs):
        total = refs[i * count][...].astype(F32)
        for ref in refs[i * count + 1 : (i + 1) * count]:
            total = total + ref[...].astype(F32)
        out[...] = total.astype(BF16)


def exchange_sum_kernel(sc, kept, came, away, held):
    for i in range(held.shape[0]):
        held[i] = (kept[2 * i].astype(F32) + came[2 * i].astype(F32)).astype(BF16)
        away[i] = (kept[2 * i + 1].astype(F32) + came[2 * i + 1].astype(F32)).astype(BF16)


def place_halves(sc, first, second, mine, other):
    low = sc[sc.shape[0] - 1] == 1
    mine[...] = jnp.where(low, second, first)
    other[...] = jnp.where(low, first, second)


def split_sum_kernel(count, sc, *refs):
    totals = []
    for i in range(2):
        total = refs[i * count][...].astype(F32)
        for ref in refs[i * count + 1 : (i + 1) * count]:
            total = total + ref[...].astype(F32)
        totals.append(total.astype(BF16))
    place_halves(sc, *totals, *refs[2 * count :])


def split_stack_kernel(sc, *refs):
    pieces, (mine, other) = refs[:-2], refs[-2:]
    half = len(pieces) // 2
    low = sc[sc.shape[0] - 1] == 1
    for i in range(half):
        first, second = pieces[i][...], pieces[half + i][...]
        mine[i] = jnp.where(low, second, first)
        other[i] = jnp.where(low, first, second)


def cut(chips, tok, width, piece):
    high = max(16, tok // chips)
    across = high * chips // tok
    wide = width // across
    return (
        pl.ds(pl.multiple_of((piece // across) * high, high), high),
        pl.ds(pl.multiple_of((piece % across) * wide, wide), wide),
    )


def piece_shape(chips, tok, width):
    high = max(16, tok // chips)
    return high, tok * width // (chips * high)


def split_kernel(chips, sc, keys, values, came, *outs):
    _, tok, width = keys.shape
    for mask in range(chips):
        rows, columns = cut(chips, tok, width, sc[0] ^ mask)
        own = jnp.where(sc[1] == 0, keys[:, rows, columns], values[:, rows, columns])
        outs[mask][0] = own
        outs[mask][1] = came[:, rows, columns]


def route_kernel(chips, sc, *refs):
    ins, outs, held = refs[:chips], refs[chips : 2 * chips], refs[2 * chips]
    count = ins[0].shape[1]
    per_chip = 2 * count
    for mask in range(chips):
        held[mask] = ins[mask][...]
    for mask in range(chips):
        for i in range(per_chip):
            bank = sc[2 + (sc[0] ^ mask) * per_chip + i]
            outs[mask][i] = held[
                (bank // per_chip) ^ sc[0], ((bank // count) % 2) ^ sc[1], bank % count
            ]


def head_columns_kernel(blocks, keys, values, *outs):
    part = keys.shape[2] // blocks
    outs[-1][...] = jnp.zeros(TOKEN, jnp.int32)
    for mask in range(blocks):
        columns = pl.ds(pl.multiple_of((lax.axis_index("blk") ^ mask) * part, part), part)
        outs[mask][0] = keys[:, :, columns]
        outs[mask][1] = values[:, :, columns]


def choose_kernel(chips, sc, *refs):
    ins, outs, held = refs[: 2 * chips], refs[2 * chips : 3 * chips], refs[3 * chips]
    count = ins[0].shape[1]
    for i in range(2 * chips):
        held[i // chips, i % chips] = ins[i][...]
    for mask in range(chips):
        for i in range(count):
            bank = sc[2 + (sc[0] ^ mask) * 2 * count + sc[1] * count + i]
            core, chip = (bank // count) % 2, bank // (2 * count)
            for j in range(2):
                outs[mask][j, i] = held[core ^ sc[1], chip ^ sc[0], j, bank % count]


def gather_kernel(chips, sc, *refs):
    ins, (kept, sent) = refs[:chips], refs[chips:]
    count, tok, width = kept.shape
    high, wide = ins[0].shape[1:]
    across = width // wide
    for mask in range(chips):
        _, columns = cut(chips, tok, width, sc[0] ^ mask)
        rows = slice((mask // across) * high, (mask // across + 1) * high)
        for i in range(count):
            kept[i, rows, columns] = ins[mask][sc[1] * count + i]
            sent[i, rows, columns] = ins[mask][(1 - sc[1]) * count + i]


def columns_kernel(blocks, sc, kept, came, *outs):
    part = kept.shape[2] // blocks
    for mask in range(blocks):
        columns = pl.ds(pl.multiple_of((sc[0] ^ mask) * part, part), part)
        mine, other = kept[:, :, columns], came[:, :, columns]
        outs[mask][0] = jnp.where(sc[1] == 0, mine, other)
        outs[mask][1] = jnp.where(sc[1] == 0, other, mine)


def fetch_shares(order, mem_keys, mem_values, places, blocks, zero, first, turn, second):
    count, tok, width = mem_keys.shape
    share = ((2, count, tok, width // blocks), BF16)
    *parts, token = pl.pallas_call(
        functools.partial(head_columns_kernel, blocks),
        in_specs=[pl.BlockSpec(memory_space=pltpu.VMEM)] * 2,
        out_specs=[pl.BlockSpec(memory_space=pltpu.VMEM)] * (blocks + 1),
        out_shape=[jax.ShapeDtypeStruct(*share)] * blocks
        + [jax.ShapeDtypeStruct(TOKEN, jnp.int32)],
        compiler_params=params(10),
        cost_estimate=cost_of("bank_columns"),
        name="bank_columns",
    )(mem_keys, mem_values)
    order.last = (token,)
    zero()
    moved = [swap(parts[m], "blk", m) for m in range(1, blocks)]
    own = swap(parts[0], "grp", 1)
    order.last = order.last + tuple(moved) + (own,)
    first()
    parts = [parts[0]] + [swap(p, "grp", 2 * (m + 1)) for m, p in enumerate(moved)]
    turn()
    others = [own] + [swap(p, "grp", 1) for p in parts[1:]]
    parts = order.call(
        functools.partial(choose_kernel, blocks),
        "choose_banks",
        (1,),
        parts + others,
        [share] * blocks,
        [pltpu.VMEM((2, blocks) + share[0], BF16)],
        14,
        places,
    )
    second()
    return [parts[0]] + [swap(parts[m], "grp", 2 * m) for m in range(1, blocks)]


def fetch_banks(order, mem_keys, mem_values, places, groups, my_group, blocks, first, second):
    count, tok, width = mem_keys.shape
    core, chips = my_group % 2, groups // 2
    came = swap(jnp.where(core == 0, mem_values, mem_keys), "grp", 1)
    piece = piece_shape(chips, tok, width)

    def line(parts):
        return [parts[0]] + [swap(parts[m], "grp", 2 * m) for m in range(1, chips)]

    parts = order.call(
        functools.partial(split_kernel, chips),
        "split_banks",
        (1,),
        [mem_keys, mem_values, came],
        [((2, count) + piece, BF16)] * chips,
        [],
        10,
        places,
    )
    first()
    parts = order.call(
        functools.partial(route_kernel, chips),
        "route_banks",
        (1,),
        line(parts),
        [((2 * count,) + piece, BF16)] * chips,
        [pltpu.VMEM((chips, 2, count) + piece, BF16)],
        10,
        places,
    )
    second()
    kept, sent = order.call(
        functools.partial(gather_kernel, chips),
        "gather_banks",
        (1,),
        line(parts),
        [((count, tok, width), BF16)] * 2,
        [],
        10,
        places,
    )
    parts = order.call(
        functools.partial(columns_kernel, blocks),
        "bank_columns",
        (1,),
        [kept, swap(sent, "grp", 1)],
        [((2, count, tok, width // blocks), BF16)] * blocks,
        [],
        10,
    )
    return [parts[0]] + [swap(parts[m], "blk", m) for m in range(1, blocks)]


class Order:
    def __init__(self, scalars, last=()):
        self.scalars, self.last = scalars, last

    def call(self, kernel, name, grid, ins, outs, scratch, mib, scalars=None):
        found = call(
            kernel,
            name,
            grid,
            ins,
            outs,
            scratch,
            self.scalars if scalars is None else scalars,
            mib,
            tuple(self.last),
        )
        self.last = (found[-1],)
        return found[:-1]

    def small(self, kernel, name, items, outs):
        ins = []
        for item in items:
            if isinstance(item, tuple) and len(item) == 2:
                array, at = item
                block = (None,) + array.shape[1:]
                zeros = (0,) * (array.ndim - 1)
                ins.append((array, block, lambda i, sc, at=at, zeros=zeros: (at,) + zeros))
            else:
                ins.append(item)
        return self.call(kernel, name, (1,), ins, [(o, BF16) for o in outs], [], 8)

    def copy(self, value):
        return self.small(copy_kernel, "copy", [value], [value.shape])[0]

    def gate(self, values):
        *found, token = gate(values, self.last)
        self.last = (token,)
        return found


def on_device(
    tokens,
    gain_one,
    bias_one,
    w_qkv,
    w_out,
    gain_two,
    bias_two,
    w_in,
    w_down,
    mem_keys,
    mem_values,
    continues,
    block_place,
    cotangent,
):
    seq_count, tok, width = tokens.shape
    hidden_width = w_in.shape[1]
    blocks, groups = lax.axis_size("blk"), lax.axis_size("grp")
    my_block, my_group = lax.axis_index("blk"), lax.axis_index("grp")
    core = my_group % 2
    part = width // blocks
    pairs = part // 128
    halved = pairs > 1
    rows = seq_count * tok
    seg_rows = blocks * tok
    tile = hidden_width // (2 * blocks)
    scalars, banks = indices(block_place, continues)
    gains = jnp.stack([gain_one, bias_one, gain_two, bias_two])
    flat = tokens.reshape(rows, width)
    cot = cotangent.reshape(rows, width)

    def head_weights(j, at=None):
        def index(i, sc):
            return (0, j * blocks + (sc[0] ^ i if at is None else sc[0]))

        return (w_qkv, (width, part), index)

    def heads_block(j):
        return (1, tok, 128), lambda s, p, sc: (s, 0, j * pairs + p)

    seg_block = (1, seg_rows, 128), lambda s, p, sc: (s, 0, p)
    seg_shape = (seq_count, seg_rows, part)
    tok_block = (1, tok, 128), lambda s, p, sc: (s, 0, p)
    mem_block = (2, 1, tok, 128), lambda s, p, sc: (0, s, 0, p)
    early = {}


    order = Order(scalars)
    rows_block = (None, rows, width)
    normed, qkv, pieces = [], [], []

    def project(some):
        found = order.call(
            functools.partial(project_kernel, len(some)),
            "project",
            (1,),
            [(p, rows_block, lambda i, sc: (0, 0, 0)) for p in some]
            + [gains]
            + [head_weights(j, 0) for j in range(3)],
            [((rows, width), BF16), ((rows, 3 * part), BF16)] * len(some),
            [],
            20,
        )
        pieces.extend(some)
        normed.extend(found[::2])
        qkv.extend(f.reshape(seq_count, tok, 3 * part) for f in found[1::2])

    def own_keys():
        early["own"] = order.call(
            functools.partial(own_kernel, blocks),
            "own_keys",
            (seq_count, pairs),
            [(qkv[m],) + heads_block(j) for m in range(blocks) for j in range(3)],
            [(seg_shape, BF16) + seg_block] * 3 + [(seg_shape, F32) + seg_block] * 2,
            [pltpu.VMEM((3, blocks, tok, 128), BF16)],
            16,
        )

    row_shape = (rows, width)
    both_shape = (2, rows, width)
    half_shape = (2, rows // 2, width)

    def zero():
        early["both"] = order.call(
            stack_kernel, "rows_stack", (1,), [flat, cot], [(both_shape, BF16)], [], 8
        )[0]

    def first():
        (both,) = order.gate([early["both"]])
        masks = (1, 2) if blocks == 4 else range(1, blocks)
        early["both"], early["rows"] = both, [swap(both, "blk", m) for m in masks]

    def turn():
        if blocks == 4:
            top, low = order.call(
                cross_kernel, "cross", (1,), early["rows"], [(half_shape, BF16)] * 2, [], 8
            )
            early["last"] = [swap(top, "blk", 2), swap(low, "blk", 1)]

    def second():
        project([early["both"]] + early["rows"])
        if blocks == 4:
            (piece,) = order.call(
                join_kernel, "join", (1,), early["last"], [(both_shape, BF16)], [], 8
            )
            project([piece])
        own_keys()

    if blocks == groups // 2:
        mem = fetch_shares(order, mem_keys, mem_values, banks, blocks, zero, first, turn, second)
    else:
        mem = fetch_banks(
            order,
            mem_keys,
            mem_values,
            banks,
            groups,
            my_group,
            blocks,
            lambda: (zero(), first(), turn()),
            second,
        )
    queries, keys, values, partial, counts = early["own"]
    found = order.call(
        functools.partial(cached_kernel, blocks),
        "cached_keys",
        (seq_count, pairs),
        [(a,) + seg_block for a in (queries, keys, partial, counts)]
        + [(a,) + mem_block for a in mem],
        [(seg_shape, F32) + seg_block] * 2
        + [((seq_count, tok, part), BF16) + tok_block] * blocks,
        [pltpu.VMEM((2, seg_rows, 128), BF16), pltpu.VMEM((blocks, tok, 128), BF16)],
        16,
    )
    attended_f, counts = found[:2]
    attended = [found[2]] + [swap(found[2 + m], "blk", m) for m in range(1, blocks)]
    attended = [a.reshape(rows, part) for a in attended]

    def ff_tile(j, sc):
        return 2 * (sc[0] ^ (j // 2)) + j % 2

    base = blocks * tile
    found = order.call(
        functools.partial(feed_kernel, blocks),
        "feed",
        (2 * blocks,),
        attended
        + [flat, cot, w_out, gains]
        + [
            (w_in, (width, tile), lambda j, sc: (0, ff_tile(j, sc))),
            (w_down, (tile, width), lambda j, sc: (ff_tile(j, sc), 0)),
        ],
        [
            ((rows, width), BF16),
            ((rows, width), F32),
            ((rows, base), BF16),
            ((rows, base + 2 * width + width // 2), BF16),
            ((rows, width), BF16),
            ((rows, width), BF16),
            ((rows, width // 2), BF16),
            ((2, width), F32),
        ]
        + [((rows, 2 * tile), BF16)] * blocks
        + [((rows, part), BF16)] * blocks,
        [
            pltpu.VMEM((rows, width), F32),
            pltpu.VMEM((rows, width), BF16),
            pltpu.VMEM((rows, width), F32),
            pltpu.VMEM((rows, width), F32),
        ],
        28,
    )
    mixed, grad_res, inner_keep, to_core, normed_two, att_all, branch, sums_two = found[:8]
    acts, grad_att = found[8 : 8 + blocks], found[8 + blocks :]
    grad_att = [grad_att[0]] + [swap(grad_att[m], "blk", m) for m in range(1, blocks)]
    grad_att = [g.reshape(seq_count, tok, part) for g in grad_att]
    core_came = swap(to_core, "grp", 1)
    order.last = order.last + tuple(grad_att[1:]) + (core_came,)
    made = {}

    def acts_path():
        made["acts"] = [acts[0]] + [
            swap(a, "blk", m + 1) for m, a in enumerate(order.gate(acts[1:]))
        ]
        return True
        yield

    top = blocks // 2

    def of_mask(shape, mask, wanted):
        def index(m, sc):
            if mask == 1:
                return (m >> 1, 0, 0)
            return (jnp.maximum(m - top, 0) if wanted else jnp.minimum(m, top - 1), 0, 0)

        return ((top,) + shape, BF16, (1,) + shape, index)

    def columns(start):
        return lambda m, sc: (0, start // part + (sc[0] ^ m))

    in_rows = part + part * width // (2 * base)
    in_shape = (in_rows // 2, base)
    bits = [1 << i for i in range(blocks.bit_length() - 1)]
    results = {}

    def go(names):
        for name in names:
            if name == ".":
                order.call(nothing_kernel, "pause", (1,), [], [], [], 4)
            elif name not in results:
                try:
                    next(paths[name])
                except StopIteration as stop:
                    results[name] = stop.value

    def total(*items):
        first = items[0]
        if not isinstance(first, tuple):
            shape = first.shape
        elif len(first) == 2:
            shape = first[0].shape[1:]
        else:
            shape = first[1]
        return order.small(sum_kernel, "sum", items, [shape])[0]

    def sum_chips(mine, other, late=True):
        came = swap(other, "grp", 2)
        yield
        held = total(mine, came)
        for bit in range(2, groups.bit_length() - 1):
            came = swap(held, "grp", 1 << bit)
            yield
            held = total(held, came)
        other = swap(held, "grp", 2)
        core_held = swap(held, "grp", 1)
        if late:
            yield
            other = order.copy(other)
        return held, other, core_held, swap(other, "grp", 1)

    def back_path():
        found = order.call(
        functools.partial(attention_back_kernel, blocks),
        "attention_back",
        (seq_count, pairs),
        [(a,) + seg_block for a in (queries, keys, values, attended_f, counts)]
        + [(a,) + mem_block for a in mem]
        + [(a,) + tok_block for a in grad_att],
        [
            (
                (3, seq_count, tok, part),
                BF16,
                (3, 1, tok, 128),
                lambda s, p, sc: (0, s, 0, p),
            )
        ]
        * blocks,
        [
            pltpu.VMEM((2, seg_rows, 128), BF16),
            pltpu.VMEM((blocks, tok, 128), BF16),
            pltpu.VMEM((3, blocks, tok, 128), BF16),
        ],
        24,
    )
        made["grads"] = [g.reshape(3, rows, part) for g in found]
        return True
        yield

    def in_start():
        found = order.call(
        functools.partial(in_kernel, blocks),
        "grad_in",
        (blocks,),
        [
            (normed_two, (rows, part), columns(0)),
            (core_came, (rows, part), columns(base)),
            inner_keep,
            (core_came, (rows, base), lambda m, sc: (0, 0)),
            (att_all, (rows, part), columns(0)),
            (core_came, (rows, part), columns(base + width)),
            branch,
            (core_came, (rows, width // 2), lambda m, sc: (0, 2 * (base + 2 * width) // width)),
        ],
        [of_mask(in_shape, mask, sent) for mask in (1, top) for sent in (True, False)],
        [pltpu.VMEM((in_rows, base), BF16)],
        28,
    )
        made["kept"] = found[1], found[3]
        made["came"] = swap(found[0], "blk", 1), swap(found[2], "blk", top)
        return True
        yield

    def in_path():
        firsts, rests = (1, top), (bits[1:], bits[:-1][::-1])
        masks = [[m for m in range(blocks) if not m & bit] for bit in firsts]
        in_kept, came = made["kept"], made["came"]
        terms = [
            {m: [(in_kept[h], i), (came[h], i)] for i, m in enumerate(masks[h])} for h in range(2)
        ]
        for bit in range(len(bits) - 1):
            away = [[m for m in masks[h] if m & rests[h][bit]] for h in range(2)]
            masks = [[m for m in masks[h] if not m & rests[h][bit]] for h in range(2)]
            items = [v for h in range(2) for m in away[h] for v in terms[h][m]]
            count = len(away[0])
            sent = order.small(
                functools.partial(sums_kernel, len(items) // (2 * count)),
                "sums",
                items,
                [in_shape] * (2 * count),
            )
            for h in range(2):
                for i, m in enumerate(masks[h]):
                    came = swap(sent[h * count + i], "blk", rests[h][bit])
                    terms[h][m] = terms[h][m] + [came]
            yield
        items = [v for h in range(2) for v in terms[h][0]]
        mine, other = order.small(
            functools.partial(split_sum_kernel, len(items) // 2), "split", items, [in_shape] * 2
        )
        return (yield from sum_chips(mine, other))

    def down_start():
        found = order.call(
        functools.partial(down_kernel, blocks),
        "grad_down",
        (2,),
        [
            (a, (rows, tile), lambda i, sc: (0, jnp.where(i == 0, 1 - sc[1], sc[1])))
            for a in made["acts"]
        ]
        + [(p, rows_block, lambda i, sc: (1, 0, 0)) for p in pieces],
        [((tile, width), BF16)] * 2,
        [],
        28,
    )
        made["down"] = found[1], swap(found[0], "grp", 1)
        return True
        yield

    def down_path():
        down_kept, down_came = made["down"]
        block = (tile // 2, width)
        items = [
            (v, block, lambda i, sc, h=h: (h, 0)) for h in range(2) for v in (down_kept, down_came)
        ]
        mine, other = order.small(
            functools.partial(split_sum_kernel, 2), "split", items, [block] * 2
        )
        return (yield from sum_chips(mine, other, False))

    share = part // 2 if halved else part
    share_block = (1, share + 16, 3 * part), lambda m, sc: (m, 0, 0)

    def own_weights(j):
        return (w_qkv, (part, part), lambda m, sc: (sc[0] ^ m, j * blocks + sc[0]))

    def qkv_start():
        found = order.call(
        functools.partial(qkv_kernel, blocks, halved),
        "grad_qkv",
        (blocks,),
        [(n, (rows, part), columns(0)) for n in normed]
        + made["grads"]
        + [own_weights(j) for j in range(3)]
        + [(gains, (4, part), columns(0))]
        + [(sums_two, (2, part), columns(0))],
        [((blocks, share + 16, 3 * part), BF16) + share_block] * (2 if halved else 1),
        [],
        28,
    )
        made["qkv"] = found[-1], swap(found[0], "grp", 1)
        return True
        yield

    def qkv_path():
        qkv_kept, came = made["qkv"]
        shape = qkv_kept.shape[1:]
        half = (blocks // 2,) + shape
        away, kept = order.small(
            exchange_sum_kernel, "sums", [qkv_kept, came], [half] * 2
        )
        came = swap(away, "blk", 1)
        yield
        held = {2 * i: [(kept, i), (came, i)] for i in range(blocks // 2)}
        for bit in bits[1:]:
            masks = [m for m in sorted(held) if m & bit]
            items = [v for m in masks for v in held[m]]
            (away,) = order.small(stack_kernel, "stack", items, [(len(items),) + shape])
            came = swap(away, "blk", bit)
            yield
            held = {m: v for m, v in held.items() if not m & bit}
            count = len(held[0])
            for i, m in enumerate(sorted(held)):
                held[m] = held[m] + [(came, i * count + k) for k in range(count)]
        mine, other = order.small(split_stack_kernel, "split", held[0], [half] * 2)
        return (yield from sum_chips(mine, other))

    def tokens_path():
        shape = (3, rows, part)
        held = {m: [g] for m, g in enumerate(made["grads"])}
        for bit in bits:
            items = [v for m in sorted(held) if m & bit for v in held[m]]
            (away,) = order.small(stack_kernel, "stack", items, [(len(items),) + shape])
            came = swap(away, "blk", bit)
            yield
            held = {m: v for m, v in held.items() if not m & bit}
            count = len(held[0])
            for i, m in enumerate(sorted(held)):
                held[m] = held[m] + [(came, i * count + k) for k in range(count)]
        grads = held[0][:1] + [
            (g, (None,) + shape, lambda i, sc, at=at: (at, 0, 0, 0)) for g, at in held[0][1:]
        ]
        return order.call(
            functools.partial(tokens_kernel, blocks),
            "tokens_back",
            (blocks,),
            [flat, grad_res, gains] + grads + [head_weights(j) for j in range(3)],
            [((rows, width), F32)],
            [pltpu.VMEM((rows, width), F32)],
            24,
        )

    def down_finish():
        return order.call(
            down_finish_kernel,
            "down_finish",
            (4,),
            list(results["d"]),
            [((2 * tile, width), F32, (tile // 2, width), lambda i, sc: (i, 0))],
            [],
            16,
        )
        yield

    def in_finish():
        return order.call(
            functools.partial(in_finish_kernel, blocks),
            "in_finish",
            (2 * blocks,),
            list(results["i"]),
            [
                ((part, hidden_width), F32, (part, tile), lambda j, sc: (0, j)),
                ((part, width), F32, (part, width // 2), lambda j, sc: (0, jnp.minimum(j, 1))),
            ],
            [pltpu.VMEM((2, in_rows, base), BF16)],
            16,
        )
        yield

    def qkv_finish():
        return order.call(
            functools.partial(qkv_finish_kernel, blocks, halved),
            "qkv_finish",
            (2 if halved else 1,),
            list(results["q"]),
            [((part, 3 * width), F32, (share, 3 * width), lambda k, sc: (k, 0))]
            + [((part,), F32)] * 4,
            [],
            16,
        )
        yield

    paths = {
        "A": acts_path(),
        "B": back_path(),
        "N": in_start(),
        "W": down_start(),
        "Y": qkv_start(),
        "d": down_path(),
        "i": in_path(),
        "q": qkv_path(),
        "t": tokens_path(),
        "F": down_finish(),
        "H": in_finish(),
        "G": qkv_finish(),
    }
    go(PLAN if groups == 8 and blocks == 4 else "ABNWY")
    while len(results) < len(paths):
        for name in paths:
            needs = {"F": "d", "H": "i", "G": "q"}.get(name)
            if needs is None or needs in results:
                go(name)
    (grad_down,) = results["F"]
    grad_qkv, *sums = results["G"]
    grad_in, grad_out = results["H"]
    (grad_tokens,) = results["t"]
    return (
        mixed.reshape(tokens.shape),
        grad_tokens.reshape(tokens.shape),
        sums[0],
        sums[1],
        grad_qkv,
        grad_out,
        sums[2],
        sums[3],
        grad_in,
        grad_down,
    )


def solution(mesh):
    rows = P("grp", "blk", None)
    in_specs = (rows,) + (P(),) * 8 + (rows, rows, P(), P(), rows)
    out_specs = (rows, rows) + (P("blk"),) * 2 + (P("blk", None),) * 2
    out_specs = out_specs + (P("blk"),) * 2 + (P("blk", None),) * 2
    return jax.shard_map(
        on_device, mesh=mesh, in_specs=in_specs, out_specs=out_specs, check_vma=False
    )
```

```python
import functools

import jax
import jax.numpy as jnp
from jax import lax
from jax.experimental import pallas as pl
from jax.experimental.pallas import tpu as pltpu
from jax.sharding import PartitionSpec as P

HEADS = 16
F32 = jnp.float32
BF16 = jnp.bfloat16
MIB = 1 << 20
EPS = 1e-05
FAR = -1e30
GELU_A = 0.7978845608028654
GELU_B = 0.044715


def swap(values, axis, mask):
    size = lax.axis_size(axis)
    return lax.ppermute(values, axis, [(i, i ^ mask) for i in range(size)])


def pick(values, index, dim=0):
    return lax.dynamic_index_in_dim(values, index, dim, keepdims=False)


def nn(left, right):
    return lax.dot_general(left, right, (((1,), (0,)), ((), ())), preferred_element_type=F32)


def nt(left, right):
    return lax.dot_general(left, right, (((1,), (1,)), ((), ())), preferred_element_type=F32)


def tn(left, right):
    return lax.dot_general(left, right, (((0,), (0,)), ((), ())), preferred_element_type=F32)


def params(mib):
    return pltpu.CompilerParams(vmem_limit_bytes=mib * MIB)


ANYWHERE = pl.BlockSpec(memory_space=pl.ANY)
EVERY = range(100)
TOKEN = (8, 128)
COSTS = {'': (3000000000, 10000000000), 'grad_in': (10000000000, 1000000), 'grad_qkv': (10000000000, 1000000), 'attention_back': (10000000000, 1000000), 'feed': (100000000000, 1000000), 'tokens_back': (100000000000, 1000000), 'project': (1000000000, 1000000000), 'own_keys': (1000000000, 1000000000), 'cached_keys': (1000000000, 1000000000), 'bank_columns': (1000000000, 1000000000), 'cross': (1000000000, 1000000000), 'join': (1000000000, 1000000000), 'copy': (1000000000, 1000000000), 'choose_banks': (1000000000, 1000000000), 'grad_down': (3000000000, 10000000000)}
PLAN = "ABNWYdqidiqqtidtiqFtqiHqG"


def cost_of(name):
    flops, size = COSTS.get(name, COSTS[""])
    return pl.CostEstimate(flops=flops, bytes_accessed=size, transcendentals=0)


OUT_HBM = {
    "project": range(0, 20, 2),
    "own_keys": (2,),
    "cached_keys": (0, 1),
    "feed": (0, 1, 2, 4, 5, 6, 8, 9, 10, 11, 12, 13, 14, 15),
}
IN_HBM = {
    "bank_columns": (0, 1),
    "rows_stack": (0, 1),
    "project": range(2, 10),
    "attention_back": EVERY,
    "grad_qkv": (0, 1, 2, 3),
    "grad_out": EVERY,
}


def call(kernel, name, grid, ins, outs, scratch, scalars, mib, tokens=()):
    def whole(shape):
        return pl.BlockSpec(shape, lambda *_: (0,) * len(shape))

    in_specs, arrays = [], []
    for item in ins:
        if isinstance(item, tuple):
            arrays.append(item[0])
            in_specs.append(pl.BlockSpec(item[1], item[2]))
        else:
            arrays.append(item)
            in_specs.append(whole(item.shape))
    out_shapes, out_specs = [], []
    for item in outs:
        out_shapes.append(jax.ShapeDtypeStruct(item[0], item[1]))
        out_specs.append(whole(item[0]) if len(item) == 2 else pl.BlockSpec(item[2], item[3]))
    count = len(arrays)

    pinned = IN_HBM.get(name, ())
    arrays = [
        pltpu.with_memory_space_constraint(a, pltpu.HBM) if i in pinned else a
        for i, a in enumerate(arrays)
    ]
    pinned = OUT_HBM.get(name, ())
    out_shapes = [
        pltpu.HBM(o.shape, o.dtype) if i in pinned else o for i, o in enumerate(out_shapes)
    ]

    out_shapes = out_shapes + [jax.ShapeDtypeStruct(TOKEN, jnp.int32)]
    out_specs = out_specs + [whole(TOKEN)]
    last = count + len(tokens) + len(outs)

    def body(sc, *refs):
        kernel(sc, *refs[:count], *refs[count + len(tokens) : last], *refs[last + 1 :])
        refs[last][...] = jnp.zeros(TOKEN, jnp.int32)

    spec = pltpu.PrefetchScalarGridSpec(
        num_scalar_prefetch=1,
        grid=grid,
        in_specs=in_specs + [ANYWHERE] * len(tokens),
        out_specs=out_specs,
        scratch_shapes=scratch,
    )
    return pl.pallas_call(
        body,
        grid_spec=spec,
        out_shape=out_shapes,
        compiler_params=params(mib),
        cost_estimate=cost_of(name),
        name=name,
    )(scalars, *arrays, *tokens)


def corner(value):
    block = (1,) * (value.ndim - 2) + (min(16, value.shape[-2]), 128)
    return pl.BlockSpec(block, lambda *_: (0,) * value.ndim)


def gate(values, tokens):
    count = len(values)

    def body(*refs):
        refs[-1][...] = jnp.zeros(TOKEN, jnp.int32)

    return pl.pallas_call(
        body,
        grid=(1,),
        in_specs=[ANYWHERE] * count + [corner(t) for t in tokens],
        out_specs=[ANYWHERE] * count + [pl.BlockSpec(memory_space=pltpu.VMEM)],
        out_shape=[jax.ShapeDtypeStruct(v.shape, v.dtype) for v in values]
        + [jax.ShapeDtypeStruct(TOKEN, jnp.int32)],
        input_output_aliases={i: i for i in range(count)},
        cost_estimate=cost_of("gate"),
        name="gate",
    )(*values, *tokens)


def norm_stats(values):
    average = jnp.mean(values, -1, keepdims=True)
    centred = values - average
    scale = lax.rsqrt(jnp.mean(centred * centred, -1, keepdims=True) + EPS)
    return centred * scale, scale


def norm_back(unit, scale, gain, grad):
    scaled = grad * gain
    mean_one = jnp.mean(scaled, -1, keepdims=True)
    mean_two = jnp.mean(scaled * unit, -1, keepdims=True)
    return scale * (scaled - mean_one - unit * mean_two)


def project_kernel(count, sc, *refs):
    rows, gains, weights = refs[:count], refs[count], refs[count + 1 : count + 4]
    outs = refs[count + 4 :]
    gain, bias = gains[0:1].astype(F32), gains[1:2].astype(F32)
    part = weights[0].shape[1]
    for i in range(count):
        unit, _ = norm_stats(rows[i][...].astype(F32))
        low = (unit * gain + bias).astype(BF16)
        outs[2 * i][...] = low
        for j, weight in enumerate(weights):
            outs[2 * i + 1][:, j * part : (j + 1) * part] = nn(low, weight[...]).astype(BF16)


def lane_masks():
    lane = lax.broadcasted_iota(jnp.int32, (1, 128), 1)
    return [lane < 64, lane >= 64]


def of_head(values, mask):
    return jnp.where(mask, values, jnp.zeros_like(values))


def by_head(first, second, masks):
    return jnp.where(masks[0], first, second)


BLOCK = 256


def own_kernel(blocks, sc, *refs):
    ins, outs = refs[: 3 * blocks], refs[3 * blocks :]
    q_out, k_out, v_out, t_out, l_out = outs[:5]
    held = outs[5]
    tok = ins[0].shape[1]
    scale = 64 ** (-0.5)
    for mask in range(blocks):
        place = sc[2 + mask]
        for i in range(3):
            values = ins[3 * mask + i][0]
            if i == 0:
                values = (values.astype(F32) * scale).astype(BF16)
            held[i, place] = values
    rows = blocks * tok
    queries = held[0].reshape(rows, 128)
    keys = held[1].reshape(rows, 128)
    values = held[2].reshape(rows, 128)
    q_out[0], k_out[0], v_out[0] = queries, keys, values
    masks = lane_masks()
    size = min(BLOCK, rows)
    lower = lax.broadcasted_iota(jnp.int32, (size, size), 0) >= lax.broadcasted_iota(
        jnp.int32, (size, size), 1
    )
    product = queries.astype(F32) * keys.astype(F32)
    head_keys = [of_head(keys, m) for m in masks]
    head_values = [of_head(values, m) for m in masks]
    selfs = [jnp.sum(of_head(product, m), -1, keepdims=True) for m in masks]
    for i in range(rows // size):
        here = slice(i * size, (i + 1) * size)
        total, sums = jnp.zeros((size, 128), F32), []
        for h in range(2):
            count = jnp.zeros((size, 1), F32)
            for j in range(i + 1):
                there = slice(j * size, (j + 1) * size)
                scores = nt(queries[here], head_keys[h][there]) - selfs[h][here]
                if i == j:
                    scores = jnp.where(lower, scores, FAR)
                weights = jnp.exp(scores)
                count = count + jnp.sum(weights, -1, keepdims=True)
                total = total + nn(weights.astype(BF16), head_values[h][there])
            sums.append(count)
        t_out[0, here] = total
        l_out[0, here] = by_head(sums[0], sums[1], masks)


def load_cached(pieces, mem):
    tok = pieces[0].shape[2]
    for mask, piece in enumerate(pieces):
        mem[:, mask * tok : (mask + 1) * tok] = piece[:, 0]


def cached_kernel(blocks, sc, *refs):
    q_in, k_in, t_in, l_in = refs[:4]
    pieces = refs[4 : 4 + blocks]
    att_out, l_out = refs[4 + blocks : 6 + blocks]
    sends = refs[6 + blocks : 6 + 2 * blocks]
    mem, low = refs[6 + 2 * blocks :]
    load_cached(pieces, mem)
    tok = pieces[0].shape[2]
    queries, keys = q_in[0], k_in[0]
    rows = queries.shape[0]
    masks = lane_masks()
    product = queries.astype(F32) * keys.astype(F32)
    selfs = [jnp.sum(of_head(product, m), -1, keepdims=True) for m in masks]
    head_keys = [of_head(mem[0], m) for m in masks]
    head_values = [of_head(mem[1], m) for m in masks]
    size = min(BLOCK, rows)
    for i in range(rows // size):
        here = slice(i * size, (i + 1) * size)
        total, sums = t_in[0, here], []
        for h in range(2):
            weights = jnp.exp(nt(queries[here], head_keys[h]) - selfs[h][here])
            sums.append(jnp.sum(weights, -1, keepdims=True))
            total = total + nn(weights.astype(BF16), head_values[h])
        count = l_in[0, here] + by_head(sums[0], sums[1], masks)
        attended = total / count
        att_out[0, here] = attended
        l_out[0, here] = count
        low[i * size // tok : (i + 1) * size // tok] = attended.astype(BF16).reshape(
            size // tok, tok, 128
        )
    for mask in range(blocks):
        sends[mask][0] = low[sc[2 + mask]]


def attention_back_kernel(blocks, sc, *refs):
    q_in, k_in, v_in, att_in, l_in = refs[:5]
    pieces = refs[5 : 5 + blocks]
    grads = refs[5 + blocks : 5 + 2 * blocks]
    sends = refs[5 + 2 * blocks : 5 + 3 * blocks]
    mem, came, low = refs[5 + 3 * blocks :]
    load_cached(pieces, mem)
    tok = pieces[0].shape[2]
    for mask in range(blocks):
        came[sc[2 + mask]] = grads[mask][0]
    queries, keys, values = q_in[0], k_in[0], v_in[0]
    rows = queries.shape[0]
    scale = 64 ** (-0.5)
    masks = lane_masks()
    grad = came[...].reshape(rows, 128).astype(F32)
    count = l_in[0]
    scaled_f = grad / count
    scaled = scaled_f.astype(BF16)
    weighed = grad * att_in[0] / count
    product = queries.astype(F32) * keys.astype(F32)
    selfs = [jnp.sum(of_head(product, m), -1, keepdims=True) for m in masks]
    fixes = [jnp.sum(of_head(weighed, m), -1, keepdims=True) for m in masks]
    own_k = [of_head(keys, m) for m in masks]
    own_v = [of_head(values, m) for m in masks]
    mem_k = [of_head(mem[0], m) for m in masks]
    mem_v = [of_head(mem[1], m) for m in masks]
    q_t = [of_head(queries, m).astype(F32).T.astype(BF16) for m in masks]
    s_t = [of_head(scaled, m).astype(F32).T.astype(BF16) for m in masks]
    size = min(BLOCK, rows)
    lower = lax.broadcasted_iota(jnp.int32, (size, size), 0) >= lax.broadcasted_iota(
        jnp.int32, (size, size), 1
    )
    steps = rows // size
    keys_t = [jnp.zeros((128, size), F32) for _ in range(steps)]
    values_t = [jnp.zeros((128, size), F32) for _ in range(steps)]
    diags = []
    for i in range(steps):
        here = slice(i * size, (i + 1) * size)
        total, sums = jnp.zeros((size, 128), F32), []
        for h in range(2):
            diag = jnp.zeros((size, 1), F32)
            for j in range(i + 1):
                there = slice(j * size, (j + 1) * size)
                scores = nt(queries[here], own_k[h][there]) - selfs[h][here]
                if i == j:
                    scores = jnp.where(lower, scores, FAR)
                weights = jnp.exp(scores)
                change = weights * (nt(scaled[here], own_v[h][there]) - fixes[h][here])
                diag = diag + jnp.sum(change, -1, keepdims=True)
                small = change.astype(BF16)
                total = total + nn(small, own_k[h][there])
                keys_t[j] = keys_t[j] + nn(q_t[h][:, here], small)
                values_t[j] = values_t[j] + nn(s_t[h][:, here], weights.astype(BF16))
            weights = jnp.exp(nt(queries[here], mem_k[h]) - selfs[h][here])
            change = weights * (nt(scaled[here], mem_v[h]) - fixes[h][here])
            diag = diag + jnp.sum(change, -1, keepdims=True)
            total = total + nn(change.astype(BF16), mem_k[h])
            sums.append(diag)
        diag = by_head(sums[0], sums[1], masks)
        diags.append(diag)
        grad_q = scale * (total - diag * keys[here].astype(F32))
        low[0, i * size // tok : (i + 1) * size // tok] = grad_q.astype(BF16).reshape(
            size // tok, tok, 128
        )
    for j in range(steps):
        there = slice(j * size, (j + 1) * size)
        grad_k = keys_t[j].T - diags[j] * queries[there].astype(F32)
        blocks_here = slice(j * size // tok, (j + 1) * size // tok)
        low[1, blocks_here] = grad_k.astype(BF16).reshape(size // tok, tok, 128)
        low[2, blocks_here] = values_t[j].T.astype(BF16).reshape(size // tok, tok, 128)
    for mask in range(blocks):
        for i in range(3):
            sends[mask][i, 0] = low[i, sc[2 + mask]]


def feed_kernel(blocks, sc, *refs):
    att_in = refs[:blocks]
    rest = refs[blocks:]
    tokens, cot, w_out, gains, w_in, w_down = rest[:6]
    rest = rest[6:]
    gain, bias = gains[2:3].astype(F32), gains[3:4].astype(F32)
    mixed, grad_res, inner_keep, to_core, normed_out, att_out, branch_keep, sums = rest[:8]
    acts = rest[8 : 8 + blocks]
    grad_att = rest[8 + blocks : 8 + 2 * blocks]
    residual, normed, total, back = rest[8 + 2 * blocks :]
    step, steps = pl.program_id(0), pl.num_programs(0)
    part, width, tile = att_in[0].shape[1], tokens.shape[1], w_in.shape[1]
    my_block, core = sc[0], sc[1]
    base = blocks * tile

    def out_rows(mask):
        return pl.ds(pl.multiple_of((my_block ^ mask) * part, part), part)

    @pl.when(step == 0)
    def _():
        branch = tokens[...].astype(F32)
        for mask in range(blocks):
            branch = branch + nn(att_in[mask][...], w_out[out_rows(mask), :])
            att_out[:, out_rows(mask)] = att_in[mask][...]
        to_core[:, base + width : base + 2 * width] = att_out[...]
        residual[...] = branch
        unit, _ = norm_stats(branch)
        low = (unit * gain + bias).astype(BF16)
        normed[...] = low
        normed_out[...] = low
        to_core[:, base : base + width] = low

    inner = nn(normed[...], w_in[...])
    square = inner * inner
    bend = jnp.tanh(GELU_A * inner * (1.0 + GELU_B * square))
    half = 0.5 * (1.0 + bend)
    act = (inner * half).astype(BF16)
    slope = half + (0.5 * GELU_A) * inner * (1.0 - bend * bend) * (1.0 + 3.0 * GELU_B * square)
    grad = (slope * nt(cot[...], w_down[...])).astype(BF16)
    into = nn(act, w_down[...])
    away = nt(grad, w_in[...])

    @pl.when(step == 0)
    def _():
        total[...] = into
        back[...] = away

    @pl.when(step > 0)
    def _():
        total[...] += into
        back[...] += away

    for j in range(2 * blocks):

        @pl.when(step == j)
        def _():
            acts[j // 2][:, (j % 2) * tile : (j % 2 + 1) * tile] = act

    columns = pl.ds(pl.multiple_of((my_block ^ (step // 2)) * tile, tile), tile)

    @pl.when(step % 2 == core)
    def _():
        inner_keep[:, columns] = grad

    @pl.when(step % 2 != core)
    def _():
        to_core[:, columns] = grad

    @pl.when(step == steps - 1)
    def _():
        here = residual[...]
        mixed[...] = (here + total[...]).astype(BF16)
        unit, scale = norm_stats(here)
        away = back[...]
        sums[0:1] = jnp.sum(away * unit, 0, keepdims=True)
        sums[1:2] = jnp.sum(away, 0, keepdims=True)
        found = cot[...].astype(F32) + norm_back(unit, scale, gain, away)
        grad_res[...] = found
        low = found.astype(BF16)
        left, right = low[:, : width // 2], low[:, width // 2 :]
        branch_keep[...] = jnp.where(core == 0, left, right)
        to_core[:, base + 2 * width :] = jnp.where(core == 0, right, left)
        for mask in range(blocks):
            grad_att[mask][...] = nt(low, w_out[out_rows(mask), :]).astype(BF16)


def in_kernel(blocks, sc, *refs):
    (normed, normed_two, inner, inner_two, att, att_two, branch, branch_two) = refs[:8]
    outs, held = refs[8:12], refs[12]
    part = normed.shape[1]
    tile = inner.shape[1] // blocks
    for q in range(blocks):
        columns = slice(q * tile, (q + 1) * tile)
        found = tn(normed[...], inner[:, columns]) + tn(normed_two[...], inner_two[:, columns])
        held[:part, columns] = found.astype(BF16)
    out = (tn(att[...], branch[...]) + tn(att_two[...], branch_two[...])).astype(BF16)
    width = out.shape[1]
    cuts = held.shape[1] // width
    high = part // cuts
    for i in range(cuts):
        held[part : part + high, i * width : (i + 1) * width] = out[i * high : (i + 1) * high]
    step = pl.program_id(0)
    half = held.shape[0] // 2
    for i, bit in enumerate((1, blocks // 2)):

        @pl.when((step & bit) != 0)
        def _():
            outs[2 * i][0] = held[i * half : (i + 1) * half]

        @pl.when((step & bit) == 0)
        def _():
            outs[2 * i + 1][0] = held[i * half : (i + 1) * half]


def down_kernel(blocks, sc, *refs):
    acts, cots, (sent, kept) = refs[:blocks], refs[blocks : 2 * blocks], refs[2 * blocks :]
    total = tn(acts[0][...], cots[0][...])
    for mask in range(1, blocks):
        total = total + tn(acts[mask][...], cots[mask][...])
    low = total.astype(BF16)

    @pl.when(pl.program_id(0) == 0)
    def _():
        sent[...] = low

    @pl.when(pl.program_id(0) == 1)
    def _():
        kept[...] = low


def qkv_kernel(blocks, halved, sc, *refs):
    normed, grads = refs[:blocks], refs[blocks : 2 * blocks]
    weights = refs[2 * blocks : 2 * blocks + 3]
    gains, sums_two = refs[2 * blocks + 3 : 2 * blocks + 5]
    outs = refs[2 * blocks + 5 :]
    part = grads[0].shape[2]
    share = part // 2 if halved else part
    ahead = jnp.zeros((part, 1), F32)
    plain = jnp.zeros((part, 1), F32)
    for j in range(3):
        total = tn(normed[0][...], grads[0][j])
        count = jnp.sum(grads[0][j].astype(F32), 0, keepdims=True)
        for mask in range(1, blocks):
            total = total + tn(normed[mask][...], grads[mask][j])
            count = count + jnp.sum(grads[mask][j].astype(F32), 0, keepdims=True)
        weight = weights[j][...].astype(F32)
        ahead = ahead + jnp.sum(weight * total, -1, keepdims=True)
        plain = plain + jnp.sum(weight * count, -1, keepdims=True)
        low = total.astype(BF16)
        columns = slice(j * part, (j + 1) * part)
        if halved:
            first, second = low[:share], low[share:]
            outs[0][0, :share, columns] = jnp.where(sc[1] == 0, second, first)
            outs[1][0, :share, columns] = jnp.where(sc[1] == 0, first, second)
        else:
            outs[0][0, :share, columns] = low
    flat = [jnp.broadcast_to(v, (part, 128)).T[0:1] for v in (ahead, plain)]
    shift = (flat[0] - gains[1:2].astype(F32) * flat[1]) / gains[0:1].astype(F32)
    row = lax.broadcasted_iota(jnp.int32, (16, part), 0)
    vectors = jnp.zeros((16, part), F32)
    for i, vector in enumerate((shift, flat[1], sums_two[0:1], sums_two[1:2])):
        vectors = jnp.where(row == i, vector, vectors)
    vectors = vectors.astype(BF16)
    for out in outs:
        out[0, share:] = jnp.zeros((16, 3 * part), BF16)
    outs[-1][0, share:, :part] = vectors


def down_finish_kernel(sc, *refs):
    parts, grad_down = refs[:4], refs[4]
    core, low = sc[1], sc[sc.shape[0] - 1]
    for i in range(4):
        wanted = 2 * (core ^ (i // 2)) + (low ^ (i % 2))

        @pl.when(pl.program_id(0) == wanted)
        def _():
            grad_down[...] = parts[i][...].astype(F32)


def in_finish_kernel(blocks, sc, *refs):
    parts, (grad_in, grad_out, held) = refs[:4], refs[4:]
    step = pl.program_id(0)
    core, low = sc[1], sc[sc.shape[0] - 1]
    half, columns = parts[0].shape
    part, tile = grad_in.shape
    width = grad_out.shape[1]
    cuts = columns // width
    high = part // cuts

    @pl.when(step == 0)
    def _():
        for i in range(4):
            rows = pl.ds(pl.multiple_of((low ^ (i % 2)) * half, 16), half)
            held[i // 2, rows] = parts[i][...]

    which = jnp.where(step % 2 == core, 0, 1)
    at = pl.ds(pl.multiple_of((step // 2) * tile, tile), tile)
    grad_in[...] = held[which, :part, at].astype(F32)

    @pl.when(step < 2)
    def _():
        for i in range(cuts):
            grad_out[i * high : (i + 1) * high] = held[
                which, part : part + high, i * width : (i + 1) * width
            ].astype(F32)


def qkv_finish_kernel(blocks, halved, sc, *refs):
    parts, grad_qkv, sums = refs[:4], refs[4], refs[5:]
    half, high, wide = parts[0].shape
    share, width = grad_qkv.shape[0], grad_qkv.shape[1] // 3
    part = wide // 3
    core, low = sc[1], sc[sc.shape[0] - 1]
    for i in range(4 if halved else 2):

        @pl.when(pl.program_id(0) == ((core ^ (i // 2)) if halved else 0))
        def _():
            for j in range(half):
                mask = (low ^ (i % 2)) * half + j
                for k in range(3):
                    first = k * width + (sc[0] ^ mask) * part
                    columns = pl.ds(pl.multiple_of(first, part), part)
                    piece = parts[i][j, :share, k * part : (k + 1) * part]
                    grad_qkv[:, columns] = piece.astype(F32)

    @pl.when(pl.program_id(0) == 0)
    def _():
        total = jnp.zeros((high - share, part), F32)
        for i in range(4 if halved else 2):
            for j in range(half):
                total = total + parts[i][j, share:, :part].astype(F32)
        for i, out in enumerate(sums):
            out[...] = total[i]


def tokens_kernel(blocks, sc, tokens, grad_res, gains, *refs):
    pieces = refs[:blocks]
    weights = refs[blocks : blocks + 3]
    grad_tokens, total = refs[blocks + 3 :]
    step, steps = pl.program_id(0), pl.num_programs(0)
    for mask in range(blocks):

        @pl.when(step == mask)
        def _():
            found = nt(pieces[mask][0], weights[0][...])
            found = found + nt(pieces[mask][1], weights[1][...])
            found = found + nt(pieces[mask][2], weights[2][...])
            if mask == 0:
                total[...] = found
            else:
                total[...] += found

    @pl.when(step == steps - 1)
    def _():
        unit, scale = norm_stats(tokens[...].astype(F32))
        grad_tokens[...] = grad_res[...] + norm_back(
            unit, scale, gains[0:1].astype(F32), total[...]
        )


def index_kernel(blocks, place, continues, scalars, banks):
    my_block, my_group = lax.axis_index("blk"), lax.axis_index("grp")
    chip, core = my_group // 2, my_group % 2
    scalars[0], scalars[1] = my_block, core
    for mask in range(blocks):
        scalars[2 + mask] = place[my_block ^ mask]
    scalars[2 + blocks] = chip % 2
    banks[0], banks[1] = chip, core
    for i in range(continues.shape[0]):
        banks[2 + i] = continues[i]


def indices(place, continues):
    smem = pl.BlockSpec(memory_space=pltpu.SMEM)
    blocks, banks = place.shape[0], continues.shape[0]
    return pl.pallas_call(
        functools.partial(index_kernel, blocks),
        in_specs=[smem, smem],
        out_specs=[smem, smem],
        out_shape=[
            jax.ShapeDtypeStruct((3 + blocks,), jnp.int32),
            jax.ShapeDtypeStruct((2 + banks,), jnp.int32),
        ],
        name="indices",
    )(place, continues)


def cross_kernel(sc, one, two, top, low):
    half = one.shape[1] // 2
    top[...], low[...] = one[:, :half], two[:, half:]


def join_kernel(sc, top, low, out):
    half = top.shape[1]
    out[:, :half], out[:, half:] = top[...], low[...]


def nothing_kernel(sc):
    pass


def copy_kernel(sc, values, out):
    out[...] = values[...]


def sum_kernel(sc, *refs):
    total = refs[0][...].astype(F32)
    for ref in refs[1:-1]:
        total = total + ref[...].astype(F32)
    refs[-1][...] = total.astype(BF16)


def stack_kernel(sc, *refs):
    for i, ref in enumerate(refs[:-1]):
        refs[-1][i] = ref[...]


def sums_kernel(count, sc, *refs):
    outs = refs[len(refs) - len(refs) // (count + 1) :]
    for i, out in enumerate(outs):
        total = refs[i * count][...].astype(F32)
        for ref in refs[i * count + 1 : (i + 1) * count]:
            total = total + ref[...].astype(F32)
        out[...] = total.astype(BF16)


def exchange_sum_kernel(sc, kept, came, away, held):
    for i in range(held.shape[0]):
        held[i] = (kept[2 * i].astype(F32) + came[2 * i].astype(F32)).astype(BF16)
        away[i] = (kept[2 * i + 1].astype(F32) + came[2 * i + 1].astype(F32)).astype(BF16)


def place_halves(sc, first, second, mine, other):
    low = sc[sc.shape[0] - 1] == 1
    mine[...] = jnp.where(low, second, first)
    other[...] = jnp.where(low, first, second)


def split_sum_kernel(count, sc, *refs):
    totals = []
    for i in range(2):
        total = refs[i * count][...].astype(F32)
        for ref in refs[i * count + 1 : (i + 1) * count]:
            total = total + ref[...].astype(F32)
        totals.append(total.astype(BF16))
    place_halves(sc, *totals, *refs[2 * count :])


def split_stack_kernel(sc, *refs):
    pieces, (mine, other) = refs[:-2], refs[-2:]
    half = len(pieces) // 2
    low = sc[sc.shape[0] - 1] == 1
    for i in range(half):
        first, second = pieces[i][...], pieces[half + i][...]
        mine[i] = jnp.where(low, second, first)
        other[i] = jnp.where(low, first, second)


def cut(chips, tok, width, piece):
    high = max(16, tok // chips)
    across = high * chips // tok
    wide = width // across
    return (
        pl.ds(pl.multiple_of((piece // across) * high, high), high),
        pl.ds(pl.multiple_of((piece % across) * wide, wide), wide),
    )


def piece_shape(chips, tok, width):
    high = max(16, tok // chips)
    return high, tok * width // (chips * high)


def split_kernel(chips, sc, keys, values, came, *outs):
    _, tok, width = keys.shape
    for mask in range(chips):
        rows, columns = cut(chips, tok, width, sc[0] ^ mask)
        own = jnp.where(sc[1] == 0, keys[:, rows, columns], values[:, rows, columns])
        outs[mask][0] = own
        outs[mask][1] = came[:, rows, columns]


def route_kernel(chips, sc, *refs):
    ins, outs, held = refs[:chips], refs[chips : 2 * chips], refs[2 * chips]
    count = ins[0].shape[1]
    per_chip = 2 * count
    for mask in range(chips):
        held[mask] = ins[mask][...]
    for mask in range(chips):
        for i in range(per_chip):
            bank = sc[2 + (sc[0] ^ mask) * per_chip + i]
            outs[mask][i] = held[
                (bank // per_chip) ^ sc[0], ((bank // count) % 2) ^ sc[1], bank % count
            ]


def head_columns_kernel(blocks, keys, values, *outs):
    part = keys.shape[2] // blocks
    outs[-1][...] = jnp.zeros(TOKEN, jnp.int32)
    for mask in range(blocks):
        columns = pl.ds(pl.multiple_of((lax.axis_index("blk") ^ mask) * part, part), part)
        outs[mask][0] = keys[:, :, columns]
        outs[mask][1] = values[:, :, columns]


def choose_kernel(chips, sc, *refs):
    ins, outs, held = refs[: 2 * chips], refs[2 * chips : 3 * chips], refs[3 * chips]
    count = ins[0].shape[1]
    for i in range(2 * chips):
        held[i // chips, i % chips] = ins[i][...]
    for mask in range(chips):
        for i in range(count):
            bank = sc[2 + (sc[0] ^ mask) * 2 * count + sc[1] * count + i]
            core, chip = (bank // count) % 2, bank // (2 * count)
            for j in range(2):
                outs[mask][j, i] = held[core ^ sc[1], chip ^ sc[0], j, bank % count]


def gather_kernel(chips, sc, *refs):
    ins, (kept, sent) = refs[:chips], refs[chips:]
    count, tok, width = kept.shape
    high, wide = ins[0].shape[1:]
    across = width // wide
    for mask in range(chips):
        _, columns = cut(chips, tok, width, sc[0] ^ mask)
        rows = slice((mask // across) * high, (mask // across + 1) * high)
        for i in range(count):
            kept[i, rows, columns] = ins[mask][sc[1] * count + i]
            sent[i, rows, columns] = ins[mask][(1 - sc[1]) * count + i]


def columns_kernel(blocks, sc, kept, came, *outs):
    part = kept.shape[2] // blocks
    for mask in range(blocks):
        columns = pl.ds(pl.multiple_of((sc[0] ^ mask) * part, part), part)
        mine, other = kept[:, :, columns], came[:, :, columns]
        outs[mask][0] = jnp.where(sc[1] == 0, mine, other)
        outs[mask][1] = jnp.where(sc[1] == 0, other, mine)


def fetch_shares(order, mem_keys, mem_values, places, blocks, zero, first, turn, second):
    count, tok, width = mem_keys.shape
    share = ((2, count, tok, width // blocks), BF16)
    *parts, token = pl.pallas_call(
        functools.partial(head_columns_kernel, blocks),
        in_specs=[pl.BlockSpec(memory_space=pltpu.VMEM)] * 2,
        out_specs=[pl.BlockSpec(memory_space=pltpu.VMEM)] * (blocks + 1),
        out_shape=[jax.ShapeDtypeStruct(*share)] * blocks
        + [jax.ShapeDtypeStruct(TOKEN, jnp.int32)],
        compiler_params=params(10),
        cost_estimate=cost_of("bank_columns"),
        name="bank_columns",
    )(mem_keys, mem_values)
    order.last = (token,)
    zero()
    moved = [swap(parts[m], "blk", m) for m in range(1, blocks)]
    own = swap(parts[0], "grp", 1)
    order.last = order.last + tuple(moved) + (own,)
    first()
    parts = [parts[0]] + [swap(p, "grp", 2 * (m + 1)) for m, p in enumerate(moved)]
    turn()
    others = [own] + [swap(p, "grp", 1) for p in parts[1:]]
    parts = order.call(
        functools.partial(choose_kernel, blocks),
        "choose_banks",
        (1,),
        parts + others,
        [share] * blocks,
        [pltpu.VMEM((2, blocks) + share[0], BF16)],
        14,
        places,
    )
    second()
    return [parts[0]] + [swap(parts[m], "grp", 2 * m) for m in range(1, blocks)]


def fetch_banks(order, mem_keys, mem_values, places, groups, my_group, blocks, first, second):
    count, tok, width = mem_keys.shape
    core, chips = my_group % 2, groups // 2
    came = swap(jnp.where(core == 0, mem_values, mem_keys), "grp", 1)
    piece = piece_shape(chips, tok, width)

    def line(parts):
        return [parts[0]] + [swap(parts[m], "grp", 2 * m) for m in range(1, chips)]

    parts = order.call(
        functools.partial(split_kernel, chips),
        "split_banks",
        (1,),
        [mem_keys, mem_values, came],
        [((2, count) + piece, BF16)] * chips,
        [],
        10,
        places,
    )
    first()
    parts = order.call(
        functools.partial(route_kernel, chips),
        "route_banks",
        (1,),
        line(parts),
        [((2 * count,) + piece, BF16)] * chips,
        [pltpu.VMEM((chips, 2, count) + piece, BF16)],
        10,
        places,
    )
    second()
    kept, sent = order.call(
        functools.partial(gather_kernel, chips),
        "gather_banks",
        (1,),
        line(parts),
        [((count, tok, width), BF16)] * 2,
        [],
        10,
        places,
    )
    parts = order.call(
        functools.partial(columns_kernel, blocks),
        "bank_columns",
        (1,),
        [kept, swap(sent, "grp", 1)],
        [((2, count, tok, width // blocks), BF16)] * blocks,
        [],
        10,
    )
    return [parts[0]] + [swap(parts[m], "blk", m) for m in range(1, blocks)]


class Order:
    def __init__(self, scalars, last=()):
        self.scalars, self.last = scalars, last

    def call(self, kernel, name, grid, ins, outs, scratch, mib, scalars=None):
        found = call(
            kernel,
            name,
            grid,
            ins,
            outs,
            scratch,
            self.scalars if scalars is None else scalars,
            mib,
            tuple(self.last),
        )
        self.last = (found[-1],)
        return found[:-1]

    def small(self, kernel, name, items, outs):
        ins = []
        for item in items:
            if isinstance(item, tuple) and len(item) == 2:
                array, at = item
                block = (None,) + array.shape[1:]
                zeros = (0,) * (array.ndim - 1)
                ins.append((array, block, lambda i, sc, at=at, zeros=zeros: (at,) + zeros))
            else:
                ins.append(item)
        return self.call(kernel, name, (1,), ins, [(o, BF16) for o in outs], [], 8)

    def copy(self, value):
        return self.small(copy_kernel, "copy", [value], [value.shape])[0]

    def gate(self, values):
        *found, token = gate(values, self.last)
        self.last = (token,)
        return found


def on_device(
    tokens,
    gain_one,
    bias_one,
    w_qkv,
    w_out,
    gain_two,
    bias_two,
    w_in,
    w_down,
    mem_keys,
    mem_values,
    continues,
    block_place,
    cotangent,
):
    seq_count, tok, width = tokens.shape
    hidden_width = w_in.shape[1]
    blocks, groups = lax.axis_size("blk"), lax.axis_size("grp")
    my_block, my_group = lax.axis_index("blk"), lax.axis_index("grp")
    core = my_group % 2
    part = width // blocks
    pairs = part // 128
    halved = pairs > 1
    rows = seq_count * tok
    seg_rows = blocks * tok
    tile = hidden_width // (2 * blocks)
    scalars, banks = indices(block_place, continues)
    gains = jnp.stack([gain_one, bias_one, gain_two, bias_two])
    flat = tokens.reshape(rows, width)
    cot = cotangent.reshape(rows, width)

    def head_weights(j, at=None):
        def index(i, sc):
            return (0, j * blocks + (sc[0] ^ i if at is None else sc[0]))

        return (w_qkv, (width, part), index)

    def heads_block(j):
        return (1, tok, 128), lambda s, p, sc: (s, 0, j * pairs + p)

    seg_block = (1, seg_rows, 128), lambda s, p, sc: (s, 0, p)
    seg_shape = (seq_count, seg_rows, part)
    tok_block = (1, tok, 128), lambda s, p, sc: (s, 0, p)
    mem_block = (2, 1, tok, 128), lambda s, p, sc: (0, s, 0, p)
    early = {}


    order = Order(scalars)
    rows_block = (None, rows, width)
    normed, qkv, pieces = [], [], []

    def project(some):
        found = order.call(
            functools.partial(project_kernel, len(some)),
            "project",
            (1,),
            [(p, rows_block, lambda i, sc: (0, 0, 0)) for p in some]
            + [gains]
            + [head_weights(j, 0) for j in range(3)],
            [((rows, width), BF16), ((rows, 3 * part), BF16)] * len(some),
            [],
            20,
        )
        pieces.extend(some)
        normed.extend(found[::2])
        qkv.extend(f.reshape(seq_count, tok, 3 * part) for f in found[1::2])

    def own_keys():
        early["own"] = order.call(
            functools.partial(own_kernel, blocks),
            "own_keys",
            (seq_count, pairs),
            [(qkv[m],) + heads_block(j) for m in range(blocks) for j in range(3)],
            [(seg_shape, BF16) + seg_block] * 3 + [(seg_shape, F32) + seg_block] * 2,
            [pltpu.VMEM((3, blocks, tok, 128), BF16)],
            16,
        )

    row_shape = (rows, width)
    both_shape = (2, rows, width)
    half_shape = (2, rows // 2, width)

    def zero():
        early["both"] = order.call(
            stack_kernel, "rows_stack", (1,), [flat, cot], [(both_shape, BF16)], [], 8
        )[0]

    def first():
        (both,) = order.gate([early["both"]])
        masks = (1, 2) if blocks == 4 else range(1, blocks)
        early["both"], early["rows"] = both, [swap(both, "blk", m) for m in masks]

    def turn():
        if blocks == 4:
            top, low = order.call(
                cross_kernel, "cross", (1,), early["rows"], [(half_shape, BF16)] * 2, [], 8
            )
            early["last"] = [swap(top, "blk", 2), swap(low, "blk", 1)]

    def second():
        project([early["both"]] + early["rows"])
        if blocks == 4:
            (piece,) = order.call(
                join_kernel, "join", (1,), early["last"], [(both_shape, BF16)], [], 8
            )
            project([piece])
        own_keys()

    if blocks == groups // 2:
        mem = fetch_shares(order, mem_keys, mem_values, banks, blocks, zero, first, turn, second)
    else:
        mem = fetch_banks(
            order,
            mem_keys,
            mem_values,
            banks,
            groups,
            my_group,
            blocks,
            lambda: (zero(), first(), turn()),
            second,
        )
    queries, keys, values, partial, counts = early["own"]
    found = order.call(
        functools.partial(cached_kernel, blocks),
        "cached_keys",
        (seq_count, pairs),
        [(a,) + seg_block for a in (queries, keys, partial, counts)]
        + [(a,) + mem_block for a in mem],
        [(seg_shape, F32) + seg_block] * 2
        + [((seq_count, tok, part), BF16) + tok_block] * blocks,
        [pltpu.VMEM((2, seg_rows, 128), BF16), pltpu.VMEM((blocks, tok, 128), BF16)],
        16,
    )
    attended_f, counts = found[:2]
    attended = [found[2]] + [swap(found[2 + m], "blk", m) for m in range(1, blocks)]
    attended = [a.reshape(rows, part) for a in attended]

    def ff_tile(j, sc):
        return 2 * (sc[0] ^ (j // 2)) + j % 2

    base = blocks * tile
    found = order.call(
        functools.partial(feed_kernel, blocks),
        "feed",
        (2 * blocks,),
        attended
        + [flat, cot, w_out, gains]
        + [
            (w_in, (width, tile), lambda j, sc: (0, ff_tile(j, sc))),
            (w_down, (tile, width), lambda j, sc: (ff_tile(j, sc), 0)),
        ],
        [
            ((rows, width), BF16),
            ((rows, width), F32),
            ((rows, base), BF16),
            ((rows, base + 2 * width + width // 2), BF16),
            ((rows, width), BF16),
            ((rows, width), BF16),
            ((rows, width // 2), BF16),
            ((2, width), F32),
        ]
        + [((rows, 2 * tile), BF16)] * blocks
        + [((rows, part), BF16)] * blocks,
        [
            pltpu.VMEM((rows, width), F32),
            pltpu.VMEM((rows, width), BF16),
            pltpu.VMEM((rows, width), F32),
            pltpu.VMEM((rows, width), F32),
        ],
        28,
    )
    mixed, grad_res, inner_keep, to_core, normed_two, att_all, branch, sums_two = found[:8]
    acts, grad_att = found[8 : 8 + blocks], found[8 + blocks :]
    grad_att = [grad_att[0]] + [swap(grad_att[m], "blk", m) for m in range(1, blocks)]
    grad_att = [g.reshape(seq_count, tok, part) for g in grad_att]
    core_came = swap(to_core, "grp", 1)
    order.last = order.last + tuple(grad_att[1:]) + (core_came,)
    made = {}

    def acts_path():
        made["acts"] = [acts[0]] + [
            swap(a, "blk", m + 1) for m, a in enumerate(order.gate(acts[1:]))
        ]
        return True
        yield

    top = blocks // 2

    def of_mask(shape, mask, wanted):
        def index(m, sc):
            if mask == 1:
                return (m >> 1, 0, 0)
            return (jnp.maximum(m - top, 0) if wanted else jnp.minimum(m, top - 1), 0, 0)

        return ((top,) + shape, BF16, (1,) + shape, index)

    def columns(start):
        return lambda m, sc: (0, start // part + (sc[0] ^ m))

    in_rows = part + part * width // (2 * base)
    in_shape = (in_rows // 2, base)
    bits = [1 << i for i in range(blocks.bit_length() - 1)]
    results = {}

    def go(names):
        for name in names:
            if name == ".":
                order.call(nothing_kernel, "pause", (1,), [], [], [], 4)
            elif name not in results:
                try:
                    next(paths[name])
                except StopIteration as stop:
                    results[name] = stop.value

    def total(*items):
        first = items[0]
        if not isinstance(first, tuple):
            shape = first.shape
        elif len(first) == 2:
            shape = first[0].shape[1:]
        else:
            shape = first[1]
        return order.small(sum_kernel, "sum", items, [shape])[0]

    def sum_chips(mine, other, late=True):
        came = swap(other, "grp", 2)
        yield
        held = total(mine, came)
        for bit in range(2, groups.bit_length() - 1):
            came = swap(held, "grp", 1 << bit)
            yield
            held = total(held, came)
        other = swap(held, "grp", 2)
        core_held = swap(held, "grp", 1)
        if late:
            yield
            other = order.copy(other)
        return held, other, core_held, swap(other, "grp", 1)

    def back_path():
        found = order.call(
        functools.partial(attention_back_kernel, blocks),
        "attention_back",
        (seq_count, pairs),
        [(a,) + seg_block for a in (queries, keys, values, attended_f, counts)]
        + [(a,) + mem_block for a in mem]
        + [(a,) + tok_block for a in grad_att],
        [
            (
                (3, seq_count, tok, part),
                BF16,
                (3, 1, tok, 128),
                lambda s, p, sc: (0, s, 0, p),
            )
        ]
        * blocks,
        [
            pltpu.VMEM((2, seg_rows, 128), BF16),
            pltpu.VMEM((blocks, tok, 128), BF16),
            pltpu.VMEM((3, blocks, tok, 128), BF16),
        ],
        24,
    )
        made["grads"] = [g.reshape(3, rows, part) for g in found]
        return True
        yield

    def in_start():
        found = order.call(
        functools.partial(in_kernel, blocks),
        "grad_in",
        (blocks,),
        [
            (normed_two, (rows, part), columns(0)),
            (core_came, (rows, part), columns(base)),
            inner_keep,
            (core_came, (rows, base), lambda m, sc: (0, 0)),
            (att_all, (rows, part), columns(0)),
            (core_came, (rows, part), columns(base + width)),
            branch,
            (core_came, (rows, width // 2), lambda m, sc: (0, 2 * (base + 2 * width) // width)),
        ],
        [of_mask(in_shape, mask, sent) for mask in (1, top) for sent in (True, False)],
        [pltpu.VMEM((in_rows, base), BF16)],
        28,
    )
        made["kept"] = found[1], found[3]
        made["came"] = swap(found[0], "blk", 1), swap(found[2], "blk", top)
        return True
        yield

    def in_path():
        firsts, rests = (1, top), (bits[1:], bits[:-1][::-1])
        masks = [[m for m in range(blocks) if not m & bit] for bit in firsts]
        in_kept, came = made["kept"], made["came"]
        terms = [
            {m: [(in_kept[h], i), (came[h], i)] for i, m in enumerate(masks[h])} for h in range(2)
        ]
        for bit in range(len(bits) - 1):
            away = [[m for m in masks[h] if m & rests[h][bit]] for h in range(2)]
            masks = [[m for m in masks[h] if not m & rests[h][bit]] for h in range(2)]
            items = [v for h in range(2) for m in away[h] for v in terms[h][m]]
            count = len(away[0])
            sent = order.small(
                functools.partial(sums_kernel, len(items) // (2 * count)),
                "sums",
                items,
                [in_shape] * (2 * count),
            )
            for h in range(2):
                for i, m in enumerate(masks[h]):
                    came = swap(sent[h * count + i], "blk", rests[h][bit])
                    terms[h][m] = terms[h][m] + [came]
            yield
        items = [v for h in range(2) for v in terms[h][0]]
        mine, other = order.small(
            functools.partial(split_sum_kernel, len(items) // 2), "split", items, [in_shape] * 2
        )
        return (yield from sum_chips(mine, other))

    def down_start():
        found = order.call(
        functools.partial(down_kernel, blocks),
        "grad_down",
        (2,),
        [
            (a, (rows, tile), lambda i, sc: (0, jnp.where(i == 0, 1 - sc[1], sc[1])))
            for a in made["acts"]
        ]
        + [(p, rows_block, lambda i, sc: (1, 0, 0)) for p in pieces],
        [((tile, width), BF16)] * 2,
        [],
        28,
    )
        made["down"] = found[1], swap(found[0], "grp", 1)
        return True
        yield

    def down_path():
        down_kept, down_came = made["down"]
        block = (tile // 2, width)
        items = [
            (v, block, lambda i, sc, h=h: (h, 0)) for h in range(2) for v in (down_kept, down_came)
        ]
        mine, other = order.small(
            functools.partial(split_sum_kernel, 2), "split", items, [block] * 2
        )
        return (yield from sum_chips(mine, other, False))

    share = part // 2 if halved else part
    share_block = (1, share + 16, 3 * part), lambda m, sc: (m, 0, 0)

    def own_weights(j):
        return (w_qkv, (part, part), lambda m, sc: (sc[0] ^ m, j * blocks + sc[0]))

    def qkv_start():
        found = order.call(
        functools.partial(qkv_kernel, blocks, halved),
        "grad_qkv",
        (blocks,),
        [(n, (rows, part), columns(0)) for n in normed]
        + made["grads"]
        + [own_weights(j) for j in range(3)]
        + [(gains, (4, part), columns(0))]
        + [(sums_two, (2, part), columns(0))],
        [((blocks, share + 16, 3 * part), BF16) + share_block] * (2 if halved else 1),
        [],
        28,
    )
        made["qkv"] = found[-1], swap(found[0], "grp", 1)
        return True
        yield

    def qkv_path():
        qkv_kept, came = made["qkv"]
        shape = qkv_kept.shape[1:]
        half = (blocks // 2,) + shape
        away, kept = order.small(
            exchange_sum_kernel, "sums", [qkv_kept, came], [half] * 2
        )
        came = swap(away, "blk", 1)
        yield
        held = {2 * i: [(kept, i), (came, i)] for i in range(blocks // 2)}
        for bit in bits[1:]:
            masks = [m for m in sorted(held) if m & bit]
            items = [v for m in masks for v in held[m]]
            (away,) = order.small(stack_kernel, "stack", items, [(len(items),) + shape])
            came = swap(away, "blk", bit)
            yield
            held = {m: v for m, v in held.items() if not m & bit}
            count = len(held[0])
            for i, m in enumerate(sorted(held)):
                held[m] = held[m] + [(came, i * count + k) for k in range(count)]
        mine, other = order.small(split_stack_kernel, "split", held[0], [half] * 2)
        return (yield from sum_chips(mine, other))

    def tokens_path():
        shape = (3, rows, part)
        held = {m: [g] for m, g in enumerate(made["grads"])}
        for bit in bits:
            items = [v for m in sorted(held) if m & bit for v in held[m]]
            (away,) = order.small(stack_kernel, "stack", items, [(len(items),) + shape])
            came = swap(away, "blk", bit)
            yield
            held = {m: v for m, v in held.items() if not m & bit}
            count = len(held[0])
            for i, m in enumerate(sorted(held)):
                held[m] = held[m] + [(came, i * count + k) for k in range(count)]
        grads = held[0][:1] + [
            (g, (None,) + shape, lambda i, sc, at=at: (at, 0, 0, 0)) for g, at in held[0][1:]
        ]
        return order.call(
            functools.partial(tokens_kernel, blocks),
            "tokens_back",
            (blocks,),
            [flat, grad_res, gains] + grads + [head_weights(j) for j in range(3)],
            [((rows, width), F32)],
            [pltpu.VMEM((rows, width), F32)],
            24,
        )

    def down_finish():
        return order.call(
            down_finish_kernel,
            "down_finish",
            (4,),
            list(results["d"]),
            [((2 * tile, width), F32, (tile // 2, width), lambda i, sc: (i, 0))],
            [],
            16,
        )
        yield

    def in_finish():
        return order.call(
            functools.partial(in_finish_kernel, blocks),
            "in_finish",
            (2 * blocks,),
            list(results["i"]),
            [
                ((part, hidden_width), F32, (part, tile), lambda j, sc: (0, j)),
                ((part, width), F32, (part, width // 2), lambda j, sc: (0, jnp.minimum(j, 1))),
            ],
            [pltpu.VMEM((2, in_rows, base), BF16)],
            16,
        )
        yield

    def qkv_finish():
        return order.call(
            functools.partial(qkv_finish_kernel, blocks, halved),
            "qkv_finish",
            (2 if halved else 1,),
            list(results["q"]),
            [((part, 3 * width), F32, (share, 3 * width), lambda k, sc: (k, 0))]
            + [((part,), F32)] * 4,
            [],
            16,
        )
        yield

    paths = {
        "A": acts_path(),
        "B": back_path(),
        "N": in_start(),
        "W": down_start(),
        "Y": qkv_start(),
        "d": down_path(),
        "i": in_path(),
        "q": qkv_path(),
        "t": tokens_path(),
        "F": down_finish(),
        "H": in_finish(),
        "G": qkv_finish(),
    }
    go(PLAN if groups == 8 and blocks == 4 else "ABNWY")
    while len(results) < len(paths):
        for name in paths:
            needs = {"F": "d", "H": "i", "G": "q"}.get(name)
            if needs is None or needs in results:
                go(name)
    (grad_down,) = results["F"]
    grad_qkv, *sums = results["G"]
    grad_in, grad_out = results["H"]
    (grad_tokens,) = results["t"]
    return (
        mixed.reshape(tokens.shape),
        grad_tokens.reshape(tokens.shape),
        sums[0],
        sums[1],
        grad_qkv,
        grad_out,
        sums[2],
        sums[3],
        grad_in,
        grad_down,
    )


def solution(mesh):
    rows = P("grp", "blk", None)
    in_specs = (rows,) + (P(),) * 8 + (rows, rows, P(), P(), rows)
    out_specs = (rows, rows) + (P("blk"),) * 2 + (P("blk", None),) * 2
    out_specs = out_specs + (P("blk"),) * 2 + (P("blk", None),) * 2
    return jax.shard_map(
        on_device, mesh=mesh, in_specs=in_specs, out_specs=out_specs, check_vma=False
    )
```
